32 devices in a mesh: seq: 32 (over z, y, x, core).
Axes of the slice: x: 2, y: 2, z: 4, core: 2. Of those that a mesh axis runs over, the one named last changes fastest.
Arguments:
- tokens: bfloat16 [16384, 1024], P('seq'), may hold values from -6 to 6
- init_state: bfloat16 [512, 1024], replicated, may hold values from -6 to 6
- w_query: bfloat16 [1024, 1024], replicated, may hold values from -1 to 1
- w_key: bfloat16 [1024, 1024], replicated, may hold values from -1 to 1
- w_value: bfloat16 [1024, 1024], replicated, may hold values from -0.1875 to 0.1875
- w_out: bfloat16 [1024, 1024], replicated, may hold values from -0.1875 to 0.1875
- w_query_state: bfloat16 [1024, 1024], replicated, may hold values from -1 to 1
- w_cand_gate: bfloat16 [1024, 2048], replicated, may hold values from -0.1875 to 0.1875
- w_state_kv: bfloat16 [1024, 2048], replicated, may hold values from -0.1875 to 0.1875
- gate_bias: float32 [1024], replicated, may hold values from -2 to 5
- mixing: float32 [2, 3], replicated, may hold values from 0.2 to 0.6
- retrieval: int32 [32, 8], P('seq'), may hold values from 0 to 31, all different within a row
Outputs:
- mixed: bfloat16 [16384, 1024], P('seq')
- new_state: bfloat16 [16384, 1024], P('seq')
The draws below stay inside these ranges and needn't reach their ends.
Inputs may be any that keep to these rules, and one draw needn't show every extreme that they name: `retrieval`: entries of one segment differ. Entry e names block e % 8 of the segment e // 8 + 1 places earlier; entries reaching before the first segment are ignored.
All inputs are finite; a program needn't handle non-finite values.
Results may differ from the reference program's by a relative error of at most 0.008.
Values may be sent and summed in bfloat16 or wider, within the bound.
No kernel may reach another device: no remote copies, remote signals or barrier semaphores. Data moves between devices by JAX's collectives and lax.ppermute only.
A program may use at most 128 MiB of HBM per device.

```python
import math
import jax
import jax.numpy as jnp
from jax import lax

D = 1024
HEADS = 8
STATES = 512
SEG = 512
BLK = 64
MBLK = 8
WIN = 4
RET = 8
ITERS = 2
TOKENS = 16384
N_SEQ = 32


def drawn_weight(key, salt):
    inner = jax.random.fold_in(key, salt)
    return jnp.clip(jax.random.normal(inner, (D, D), jnp.float32), -6.0, 6.0) / math.sqrt(D)


def draw_w_query(key, part):
    return drawn_weight(key, 101).astype(jnp.bfloat16)


def draw_w_key(key, part):
    return drawn_weight(key, 102).astype(jnp.bfloat16)


def draw_w_query_state(key, part):
    return drawn_weight(key, 103).astype(jnp.bfloat16)


def draw_tokens(key, part):
    inner = jax.random.fold_in(key, 201)
    normal_rows = jnp.clip(jax.random.normal(inner, (TOKENS, D), jnp.float32), -6.0, 6.0)
    return normal_rows.astype(jnp.bfloat16)


def draw_init_state(key, part):
    inner = jax.random.fold_in(key, 301)
    normal_rows = jnp.clip(jax.random.normal(inner, (STATES, D), jnp.float32), -6.0, 6.0)
    return normal_rows.astype(jnp.bfloat16)


def distinct(rng, rows, amount, top, lift):
    order = jax.random.permutation(jax.random.fold_in(rng, 1), amount)
    boost = order
    for power in range(3):
        boost = boost * boost // amount
    boost = boost * lift // amount
    tickets = jax.random.randint(jax.random.fold_in(rng, 2), (rows, amount), 0, 4096) + boost
    fixed_rows = jax.random.permutation(jax.random.fold_in(rng, 3), rows)[jnp.arange(amount) % rows]
    tickets = jnp.where(jnp.arange(rows)[:, None] == fixed_rows[None, :], 1 << 14, tickets)
    merit = tickets * amount + jnp.arange(amount)
    return lax.top_k(merit.astype(jnp.int32), top)[1].astype(jnp.int32)


def scatter_about(key, dims, deviation, most, kind=jnp.bfloat16):
    result = deviation * jax.random.normal(key, dims, jnp.float32)
    return jnp.clip(result, min=-most, max=most).astype(kind)


def setup_inputs(seed: int = 0) -> dict:
    key_list = jax.random.split(jax.random.key(seed), 13)
    tokens = draw_tokens(jax.random.fold_in(key_list[12], 71), 0)
    init_state = draw_init_state(jax.random.fold_in(key_list[12], 71), 0)
    w_query = draw_w_query(jax.random.fold_in(key_list[12], 71), 0)
    w_key = draw_w_key(jax.random.fold_in(key_list[12], 71), 0)
    w_value = scatter_about(key_list[4], (D, D), D ** -0.5, 0.1875)
    w_out = scatter_about(key_list[5], (D, D), D ** -0.5, 0.1875)
    w_query_state = draw_w_query_state(jax.random.fold_in(key_list[12], 71), 0)
    w_cand_gate = scatter_about(key_list[7], (D, 2 * D), D ** -0.5, 0.1875)
    w_state_kv = scatter_about(key_list[8], (D, 2 * D), D ** -0.5, 0.1875)
    gate_bias = jnp.clip(jax.random.uniform(key_list[9], (D,), jnp.float32, -2.0, 5.0), -2.0, 5.0)
    mixing = jnp.clip(jax.random.uniform(key_list[10], (ITERS, 3), jnp.float32, 0.2, 0.6), 0.2, 0.6)
    retrieval = distinct(key_list[11], N_SEQ, WIN * MBLK, RET, 4096)
    return {"tokens": tokens, "init_state": init_state, "w_query": w_query, "w_key": w_key, "w_value": w_value, "w_out": w_out, "w_query_state": w_query_state, "w_cand_gate": w_cand_gate, "w_state_kv": w_state_kv, "gate_bias": gate_bias, "mixing": mixing, "retrieval": retrieval}


def attend(queries, key_rows, value_rows, allowed):
    count = queries.shape[0]
    width = queries.shape[1]
    head_width = width // HEADS
    query_head_rows = queries.astype(jnp.float32).reshape(count, HEADS, head_width)
    key_head_rows = key_rows.astype(jnp.float32).reshape(-1, HEADS, head_width)
    value_head_rows = value_rows.astype(jnp.float32).reshape(-1, HEADS, head_width)
    attention_logits = jnp.einsum('sep,bep->esb', query_head_rows, key_head_rows) / math.sqrt(head_width)
    if allowed is not None:
        attention_logits = jnp.where(allowed[None], attention_logits, -jnp.inf)
    peak = lax.optimization_barrier(jnp.max(attention_logits, axis=-1, keepdims=True))
    expd = jnp.exp(attention_logits - peak)
    attention_weight = (expd / lax.optimization_barrier(jnp.sum(expd, axis=-1, keepdims=True))).astype(jnp.bfloat16)
    attention_output = jnp.einsum('kqp,pkj->qkj', attention_weight.astype(jnp.float32), value_head_rows)
    return attention_output.astype(jnp.bfloat16).reshape(count, width)

def update_state(state, key_seg, value_seg, w_query_state, w_cand_gate, gate_bias):
    width = state.shape[1]
    state_query = jnp.dot(state, w_query_state, preferred_element_type=jnp.float32).astype(jnp.bfloat16)
    attended = attend(state_query, key_seg, value_seg, None)
    preact = jnp.dot(attended, w_cand_gate, preferred_element_type=jnp.float32)
    candidate = jnp.tanh(preact[:, :width])
    forget = jax.nn.sigmoid(preact[:, width:] + gate_bias)
    return (forget * state.astype(jnp.float32) + (1.0 - forget) * candidate).astype(jnp.bfloat16)

def reference(tokens, init_state, w_query, w_key, w_value, w_out, w_query_state, w_cand_gate, w_state_kv, gate_bias, mixing, retrieval):
    query_all = jnp.dot(tokens, w_query, preferred_element_type=jnp.float32).astype(jnp.bfloat16).reshape(N_SEQ, SEG, D)
    key_all = jnp.dot(tokens, w_key, preferred_element_type=jnp.float32).astype(jnp.bfloat16).reshape(N_SEQ, SEG, D)
    value_all = jnp.dot(tokens, w_value, preferred_element_type=jnp.float32).astype(jnp.bfloat16).reshape(N_SEQ, SEG, D)
    token_seg = tokens.reshape(N_SEQ, SEG, D)

    def step_all(states):
        return lax.map(lambda group: update_state(group[0], group[1], group[2], w_query_state, w_cand_gate, gate_bias), (states, key_all, value_all))
    current = jnp.broadcast_to(init_state[None], (N_SEQ, STATES, D))
    prev_shift = current
    for sweep in range(ITERS):
        updated = step_all(current)
        shifted = jnp.concatenate([init_state[None], updated[:-1]], axis=0)
        current = (mixing[sweep, 0] * shifted.astype(jnp.float32) + mixing[sweep, 1] * current.astype(jnp.float32) + mixing[sweep, 2] * prev_shift.astype(jnp.float32)).astype(jnp.bfloat16)
        prev_shift = shifted
    new_state = step_all(current)
    key_blocks = key_all.reshape(N_SEQ * MBLK, BLK, D)
    value_blocks = value_all.reshape(N_SEQ * MBLK, BLK, D)
    causal = jnp.tril(jnp.ones((SEG, SEG), dtype=bool))

    def token_part(group):
        segment_no, queries, key_seg, value_seg, state, rows, block_ids = group
        state_kv = jnp.dot(state, w_state_kv, preferred_element_type=jnp.float32).astype(jnp.bfloat16)
        source = segment_no - (block_ids // MBLK + 1)
        valid = source >= 0
        flat_index = (jnp.maximum(source, 0) * MBLK + block_ids % MBLK).astype(jnp.int32)
        mem_keys = jnp.take(key_blocks, flat_index, axis=0).reshape(RET * BLK, D)
        mem_values = jnp.take(value_blocks, flat_index, axis=0).reshape(RET * BLK, D)
        slot_allowed = jnp.broadcast_to(jnp.repeat(valid, BLK)[None], (SEG, RET * BLK))
        allowed = jnp.concatenate([causal, jnp.ones((SEG, STATES), dtype=bool), slot_allowed], axis=1)
        key_rows = jnp.concatenate([key_seg, state_kv[:, :D], mem_keys], axis=0)
        value_rows = jnp.concatenate([value_seg, state_kv[:, D:], mem_values], axis=0)
        attended = attend(queries, key_rows, value_rows, allowed)
        return (rows.astype(jnp.float32) + jnp.dot(attended, w_out, preferred_element_type=jnp.float32)).astype(jnp.bfloat16)
    segment_ids = jnp.arange(N_SEQ).astype(jnp.int32)
    mixed = lax.map(token_part, (segment_ids, query_all, key_all, value_all, current, token_seg, retrieval))
    return (mixed.reshape(N_SEQ * SEG, D), new_state.reshape(N_SEQ * STATES, D))
```

```python
import functools
import math

import jax
import jax.numpy as jnp
from jax import lax
from jax.experimental import pallas as pl
from jax.experimental.pallas import tpu as pltpu
from jax.sharding import PartitionSpec as P

HEADS = 8
BLK = 64
MBLK = 8
WIN = 4
NEG = -1e30
VMEM_LIMIT = 40 * 1024 * 1024

ANY = pl.BlockSpec(memory_space=pl.ANY)
SMEM = pl.BlockSpec(memory_space=pltpu.SMEM)
BF16 = jnp.bfloat16
F32 = jnp.float32


def dot(a, b):
    return jnp.dot(a, b, preferred_element_type=F32)


def dot_t(a, b):
    return lax.dot_general(a, b, (((1,), (1,)), ((), ())), preferred_element_type=F32)


def project(x_ref, w_ref, store, tile=256):
    for col in range(0, w_ref.shape[1], tile):
        store(col, dot(x_ref[...], w_ref[:, col : col + tile]))


def store_plain(out_ref):
    def store(col, value):
        out_ref[:, col : col + value.shape[1]] = value.astype(BF16)

    return store


def store_values(vx_ref, head):
    rows = vx_ref.shape[0]

    def store(col, value):
        for part in range(0, value.shape[1], head):
            at = 2 * (col + part)
            vx_ref[:, at : at + head] = value[:, part : part + head].astype(BF16)
            vx_ref[:, at + head : at + 2 * head] = jnp.ones((rows, head), BF16)

    return store


def in_turn(units, scores, finish):
    ahead = scores(*units[0])
    for number, unit in enumerate(units):
        now = ahead
        if number + 1 < len(units):
            ahead = scores(*units[number + 1])
        finish(*unit, now)


def update_rows(h_ref, wqs_ref, k_ref, vx_ref, wcg_ref, bias_ref, qs_ref, o_ref, out_ref, before):
    rows, width = h_ref.shape
    head = width // HEADS
    scale = math.log2(math.e) / math.sqrt(head)
    tile = min(256, rows)
    project(h_ref, wqs_ref, store_plain(qs_ref))
    before("kv")

    def scores(h, r):
        return dot_t(qs_ref[r : r + tile, h * head : (h + 1) * head], k_ref[:, h * head : (h + 1) * head])

    def finish(h, r, s):
        t = s * scale
        p = jnp.exp2(t - jnp.max(t, axis=1, keepdims=True)).astype(BF16)
        ol = dot(p, vx_ref[:, 2 * h * head : 2 * (h + 1) * head])
        o_ref[r : r + tile, h * head : (h + 1) * head] = (ol[:, :head] / ol[:, head:]).astype(BF16)

    in_turn([(h, r) for h in range(HEADS) for r in range(0, rows, tile)], scores, finish)
    before("wcg")
    for col in range(0, width, 256):
        zc = dot(o_ref[...], wcg_ref[:, col : col + 256])
        zg = dot(o_ref[...], wcg_ref[:, width + col : width + col + 256])
        cand = jnp.tanh(zc)
        forget = 0.5 * jnp.tanh(0.5 * (zg + bias_ref[:, col : col + 256])) + 0.5
        h = h_ref[:, col : col + 256].astype(F32)
        out_ref[:, col : col + 256] = (forget * h + (1.0 - forget) * cand).astype(BF16)


def attend_more(q_ref, k_ref, vx_ref, o_ref, ml_ref, row0, tile, limit, first, mask):
    head = q_ref.shape[1] // HEADS
    scale = math.log2(math.e) / math.sqrt(head)

    def scores(h, r):
        return dot_t(
            q_ref[r : r + tile, h * head : (h + 1) * head],
            k_ref[: limit(r), h * head : (h + 1) * head],
        )

    def finish(h, r, s):
        t = mask(s * scale, r)
        top = jnp.max(t, axis=1, keepdims=True)
        if not first:
            old = ml_ref[r : r + tile, h : h + 1]
            top = jnp.maximum(top, old)
        p = jnp.exp2(t - top).astype(BF16)
        ol = dot(p, vx_ref[: limit(r), 2 * h * head : 2 * (h + 1) * head])
        o, l = ol[:, :head], ol[:, head : head + 1]
        if not first:
            keep = jnp.exp2(old - top)
            o = o + keep * o_ref[r : r + tile, h * head : (h + 1) * head]
            l = l + keep * ml_ref[r : r + tile, HEADS + h : HEADS + h + 1]
        o_ref[r : r + tile, h * head : (h + 1) * head] = o
        ml_ref[r : r + tile, h : h + 1] = top
        ml_ref[r : r + tile, HEADS + h : HEADS + h + 1] = l

    in_turn([(h, r) for h in range(HEADS) for r in row0], scores, finish)


def fetch(pairs, sems):
    copies = [pltpu.make_async_copy(src, dst, sems.at[i]) for i, (src, dst) in enumerate(pairs)]
    for copy in copies:
        copy.start()
    return copies


def first_kernel(
    tok, init, wk, wv, wqs, wcg, bias, k_out, vx_out, s_out,
    tok_v, init_v, wk_v, wv_v, wqs_v, wcg_v, bias_v, k_v, vx_v, qs_v, o_v, s_v, sems, osems,
):
    head = tok.shape[1] // HEADS
    ins = fetch(
        [(tok, tok_v), (wk, wk_v), (wv, wv_v), (init, init_v), (wqs, wqs_v), (wcg, wcg_v), (bias, bias_v)], sems
    )
    outs = [pltpu.make_async_copy(*pair, osems.at[i]) for i, pair in enumerate([(k_v, k_out), (vx_v, vx_out), (s_v, s_out)])]
    ins[0].wait()
    ins[1].wait()
    project(tok_v, wk_v, store_plain(k_v))
    outs[0].start()
    ins[2].wait()
    project(tok_v, wv_v, store_values(vx_v, head))
    outs[1].start()
    ins[3].wait()
    ins[4].wait()

    def before(name):
        if name == "wcg":
            ins[5].wait()
            ins[6].wait()

    update_rows(init_v, wqs_v, k_v, vx_v, wcg_v, bias_v, qs_v, o_v, s_v, before)
    outs[2].start()
    for copy in outs:
        copy.wait()


def local_kernel(
    tok, wq, k, vx, q_out, o_out, ml_out,
    tok_v, wq_v, k_v, vx_v, q_v, o_v, ml_v, sems, osems,
):
    rows = tok.shape[0]
    tile = min(128, rows)
    ins = fetch([(tok, tok_v), (wq, wq_v), (k, k_v), (vx, vx_v)], sems)
    outs = [pltpu.make_async_copy(*pair, osems.at[i]) for i, pair in enumerate([(q_v, q_out), (o_v, o_out), (ml_v, ml_out)])]
    ins[0].wait()
    ins[1].wait()
    project(tok_v, wq_v, store_plain(q_v))
    outs[0].start()
    ins[2].wait()
    ins[3].wait()

    def causal(t, r):
        keys = t.shape[1]
        row = r + lax.broadcasted_iota(jnp.int32, (tile, tile), 0)
        col = keys - tile + lax.broadcasted_iota(jnp.int32, (tile, tile), 1)
        last = jnp.where(col <= row, t[:, keys - tile :], NEG)
        if keys == tile:
            return last
        return jnp.concatenate([t[:, : keys - tile], last], axis=1)

    attend_more(q_v, k_v, vx_v, o_v, ml_v, range(0, rows, tile), tile, lambda r: r + tile, True, causal)
    outs[1].start()
    outs[2].start()
    for copy in outs:
        copy.wait()


def mixed_guess(shift_v, cur_v, prev_v, mixing, sweep, guess_v):
    a, b, c = mixing[sweep, 0], mixing[sweep, 1], mixing[sweep, 2]
    rows = guess_v.shape[0]
    step = min(64, rows)
    for r in range(0, rows, step):
        part = slice(r, r + step)
        guess = a * shift_v[part, :].astype(F32) + b * cur_v[part, :].astype(F32)
        guess_v[part, :] = (guess + c * prev_v[part, :].astype(F32)).astype(BF16)


def fetch_chosen(first, init, other, buf, sem):
    @pl.when(first)
    def _():
        pltpu.make_async_copy(init, buf, sem).start()

    @pl.when(jnp.logical_not(first))
    def _():
        pltpu.make_async_copy(other, buf, sem).start()

    return pltpu.make_async_copy(other, buf, sem)


def second_kernel(
    place, mixing, got, init, k, vx, wqs, wcg, bias, guess_out, s_out,
    shift_v, init_v, k_v, vx_v, wqs_v, wcg_v, bias_v, guess_v, qs_v, o_v, s_v, sems, csem, osems,
):
    shift = fetch_chosen(place[0] == 0, init, got, shift_v, csem.at[0])
    ins = fetch([(init, init_v), (wqs, wqs_v), (k, k_v), (vx, vx_v), (wcg, wcg_v), (bias, bias_v)], sems)
    outs = [pltpu.make_async_copy(*pair, osems.at[i]) for i, pair in enumerate([(guess_v, guess_out), (s_v, s_out)])]
    shift.wait()
    ins[0].wait()
    mixed_guess(shift_v, init_v, init_v, mixing, 0, guess_v)
    outs[0].start()
    ins[1].wait()

    def before(name):
        for i in (2, 3) if name == "kv" else (4, 5):
            ins[i].wait()

    update_rows(guess_v, wqs_v, k_v, vx_v, wcg_v, bias_v, qs_v, o_v, s_v, before)
    outs[1].start()
    for copy in outs:
        copy.wait()


def third_kernel(
    place, mixing, got, before_got, init, cur, k, vx, wqs, wcg, bias, wskv, q, o, ml, s_out, o_out, ml_out,
    shift_v, prev_v, cur_v, k_v, vx_v, wqs_v, wcg_v, bias_v, guess_v, qs_v, os_v, s_v,
    wskv_v, q_v, oacc_v, ml_v, sems, csem, osems,
):
    width = cur.shape[1]
    head = width // HEADS
    rows = q.shape[0]
    shift = fetch_chosen(place[0] == 0, init, got, shift_v, csem.at[0])
    prev = fetch_chosen(place[0] == 0, init, before_got, prev_v, csem.at[1])
    ins = fetch(
        [(cur, cur_v), (wqs, wqs_v), (k, k_v), (vx, vx_v), (wcg, wcg_v), (bias, bias_v),
         (wskv, wskv_v), (q, q_v), (o, oacc_v), (ml, ml_v)], sems
    )
    outs = [pltpu.make_async_copy(*pair, osems.at[i]) for i, pair in enumerate([(s_v, s_out), (oacc_v, o_out), (ml_v, ml_out)])]
    shift.wait()
    prev.wait()
    ins[0].wait()
    mixed_guess(shift_v, cur_v, prev_v, mixing, 1, guess_v)
    ins[1].wait()

    def before(name):
        for i in (2, 3) if name == "kv" else (4, 5):
            ins[i].wait()

    update_rows(guess_v, wqs_v, k_v, vx_v, wcg_v, bias_v, qs_v, os_v, s_v, before)
    outs[0].start()
    ins[6].wait()
    project(guess_v, wskv_v.at[:, :width], store_plain(k_v))
    project(guess_v, wskv_v.at[:, width:], store_values(vx_v, head))
    for i in (7, 8, 9):
        ins[i].wait()
    tile = min(256, rows)
    keys = cur.shape[0]
    attend_more(q_v, k_v, vx_v, oacc_v, ml_v, range(0, rows, tile), tile, lambda r: keys, False, lambda t, r: t)
    outs[1].start()
    outs[2].start()
    for copy in outs:
        copy.wait()


def last_kernel(
    place, retrieval, back1, back2, back3, back4, tok, wk, wv, wout, q, o, ml, mixed_out,
    mem_v, tok_v, wk_v, wv_v, wout_v, q_v, oacc_v, ml_v, k_v, vx_v, on_v, mixed_v, sems, bsems, osem,
):
    width = tok.shape[1]
    head = width // HEADS
    rows = tok.shape[0]
    count = mem_v.shape[0] // BLK
    ins = fetch(
        [(wk, wk_v), (wv, wv_v), (q, q_v), (o, oacc_v), (ml, ml_v), (wout, wout_v), (tok, tok_v)], sems
    )
    lane_block = lax.broadcasted_iota(jnp.int32, (1, count * BLK), 1) // BLK
    bias = jnp.zeros((1, count * BLK), F32)
    waits = []
    for e in range(count):
        entry = retrieval[0, e]
        distance = entry // MBLK
        start = pl.multiple_of((entry % MBLK) * BLK, BLK)
        target = mem_v.at[e * BLK : (e + 1) * BLK, :]
        for number, source in enumerate((back1, back2, back3, back4)):

            @pl.when(distance == number)
            def _(source=source, start=start, target=target, e=e):
                pltpu.make_async_copy(source.at[pl.ds(start, BLK), :], target, bsems.at[e]).start()

        waits.append(pltpu.make_async_copy(back1.at[0:BLK, :], target, bsems.at[e]))
        bias = jnp.where((lane_block == e) & (distance + 1 > place[0]), NEG, bias)
    for copy in waits:
        copy.wait()
    ins[0].wait()
    project(mem_v, wk_v, store_plain(k_v))
    ins[1].wait()
    project(mem_v, wv_v, store_values(vx_v, head))
    for i in (2, 3, 4):
        ins[i].wait()
    tile = min(256, rows)
    keys = count * BLK
    attend_more(q_v, k_v, vx_v, oacc_v, ml_v, range(0, rows, tile), tile, lambda r: keys, False, lambda t, r: t + bias)
    for h in range(HEADS):
        part = slice(h * head, (h + 1) * head)
        on_v[:, part] = (oacc_v[:, part] / ml_v[:, HEADS + h : HEADS + h + 1]).astype(BF16)
    ins[5].wait()
    ins[6].wait()

    def store(col, value):
        part = slice(col, col + value.shape[1])
        mixed_v[:, part] = (tok_v[:, part].astype(F32) + value).astype(BF16)

    project(on_v, wout_v, store)
    copy = pltpu.make_async_copy(mixed_v, mixed_out, osem.at[0])
    copy.start()
    copy.wait()


def call(kernel, args, specs, outs, scratch, name, flops):
    return pl.pallas_call(
        kernel,
        out_shape=outs,
        in_specs=specs,
        out_specs=[ANY] * len(outs),
        scratch_shapes=scratch,
        compiler_params=pltpu.CompilerParams(vmem_limit_bytes=VMEM_LIMIT),
        cost_estimate=pl.CostEstimate(flops=flops, bytes_accessed=4 << 20, transcendentals=0),
        name=name,
    )(*args)


def bf(*shape):
    return jax.ShapeDtypeStruct(shape, BF16)


def f32(*shape):
    return jax.ShapeDtypeStruct(shape, F32)


def vm(*shape, dtype=BF16):
    return pltpu.VMEM(shape, dtype)


def dma(count):
    return pltpu.SemaphoreType.DMA((count,))


def per_device(
    tokens, init_state, w_query, w_key, w_value, w_out, w_query_state, w_cand_gate, w_state_kv,
    gate_bias, mixing, retrieval,
):
    rows, width = tokens.shape
    states = init_state.shape[0]
    count = lax.axis_size("seq")
    me = lax.axis_index("seq")
    place = me.astype(jnp.int32).reshape(1)
    bias = gate_bias.reshape(1, width)
    even = me % 2 == 0
    low = me % WIN < WIN // 2
    work = 2 * rows * width * width

    def step(value, by):
        return lax.ppermute(value, "seq", [(i, i + by) for i in range(count - by)])

    def swap(value, bit):
        return lax.ppermute(value, "seq", [(i, i ^ bit) for i in range(count)])

    back4 = step(tokens, WIN)
    key, vx, out1 = call(
        first_kernel,
        (tokens, init_state, w_key, w_value, w_query_state, w_cand_gate, bias),
        [ANY] * 7,
        [bf(rows, width), bf(rows, 2 * width), bf(states, width)],
        [vm(rows, width), vm(states, width), vm(width, width), vm(width, width), vm(width, width),
         vm(width, 2 * width), vm(1, width, dtype=F32), vm(rows, width), vm(rows, 2 * width),
         vm(states, width), vm(states, width), vm(states, width), dma(7), dma(3)],
        "keys_values_update",
        6 * work,
    )
    got1 = step(out1, 1)
    q, o, ml = call(
        local_kernel,
        (tokens, w_query, key, vx),
        [ANY] * 4,
        [bf(rows, width), f32(rows, width), f32(rows, 128)],
        [vm(rows, width), vm(width, width), vm(rows, width), vm(rows, 2 * width), vm(rows, width),
         vm(rows, width, dtype=F32), vm(rows, 128, dtype=F32), dma(4), dma(3)],
        "query_local",
        2 * work,
    )
    back2 = swap(jnp.where(low, tokens, back4), WIN // 2)
    guess1, out2 = call(
        second_kernel,
        (place, mixing, got1, init_state, key, vx, w_query_state, w_cand_gate, bias),
        [SMEM] * 2 + [ANY] * 7,
        [bf(states, width), bf(states, width)],
        [vm(states, width), vm(states, width), vm(rows, width), vm(rows, 2 * width), vm(width, width),
         vm(width, 2 * width), vm(1, width, dtype=F32), vm(states, width), vm(states, width),
         vm(states, width), vm(states, width), dma(6), dma(1), dma(2)],
        "update",
        4 * work,
    )
    got2 = step(out2, 1)
    back1 = swap(jnp.where(even, tokens, back2), 1)
    back3 = swap(jnp.where(even, back2, back4), 1)
    new_state, o, ml = call(
        third_kernel,
        (place, mixing, got2, got1, init_state, guess1, key, vx, w_query_state, w_cand_gate, bias,
         w_state_kv, q, o, ml),
        [SMEM] * 2 + [ANY] * 13,
        [bf(states, width), f32(rows, width), f32(rows, 128)],
        [vm(states, width), vm(states, width), vm(states, width), vm(rows, width), vm(rows, 2 * width),
         vm(width, width), vm(width, 2 * width), vm(1, width, dtype=F32), vm(states, width),
         vm(states, width), vm(states, width), vm(states, width), vm(width, 2 * width), vm(rows, width),
         vm(rows, width, dtype=F32), vm(rows, 128, dtype=F32), dma(10), dma(2), dma(3)],
        "update_state_keys",
        8 * work,
    )
    mem = retrieval.shape[1] * BLK
    (mixed,) = call(
        last_kernel,
        (place, retrieval, back1, back2, back3, back4, tokens, w_key, w_value, w_out, q, o, ml),
        [SMEM] * 2 + [ANY] * 11,
        [bf(rows, width)],
        [vm(mem, width), vm(rows, width), vm(width, width), vm(width, width), vm(width, width),
         vm(rows, width), vm(rows, width, dtype=F32), vm(rows, 128, dtype=F32), vm(mem, width),
         vm(mem, 2 * width), vm(rows, width), vm(rows, width), dma(7), dma(retrieval.shape[1]), dma(1)],
        "memory_out",
        4 * work,
    )
    return mixed, new_state


def solution(mesh):
    return jax.shard_map(
        per_device,
        mesh=mesh,
        in_specs=(P("seq", None), P(), P(), P(), P(), P(), P(), P(), P(), P(), P(), P("seq", None)),
        out_specs=(P("seq", None), P("seq", None)),
        check_vma=False,
    )
```

```python
import math

import jax
import jax.numpy as jnp
from jax import lax
from jax.experimental import pallas as pl
from jax.experimental.pallas import tpu as pltpu
from jax.sharding import PartitionSpec as P

HEADS = 8
BLK = 64
MBLK = 8
WIN = 4
PARTS = 2
ONES = 16
NEG = -1e30
VMEM_LIMIT = 63 * 1024 * 1024

BF16 = jnp.bfloat16
F32 = jnp.float32


def dot(a, b):
    return jnp.dot(a, b, preferred_element_type=F32)


def dot_t(a, b):
    return lax.dot_general(a, b, (((1,), (1,)), ((), ())), preferred_element_type=F32)


class Kernel:
    def __init__(self, name, flops):
        self.name, self.flops = name, flops
        self.smem, self.staged, self.raw, self.outs, self.scratch = {}, {}, {}, {}, {}
        self.aliases = {}
        self.spare = 0

    def call(self, body, after=()):
        smem, staged, raw = list(self.smem), list(self.staged), list(self.raw)
        outs, scratch = list(self.outs), list(self.scratch)
        operands = [self.smem[n] for n in smem] + [self.staged[n] for n in staged] + [self.raw[n] for n in raw]
        ranges = [x[1] if isinstance(x, tuple) else None for x in operands]
        arrays = [x[0] if isinstance(x, tuple) else x for x in operands]
        first_after = len(arrays)
        arrays += list(after)
        hbm = pl.BlockSpec(memory_space=pltpu.HBM)
        specs = [pl.BlockSpec(memory_space=pltpu.SMEM)] * len(smem) + [hbm] * (len(arrays) - len(smem))
        shapes = []
        for i in range(len(smem), len(smem) + len(staged)):
            shape = arrays[i].shape
            if ranges[i]:
                shape = (ranges[i][1] - ranges[i][0], *shape[1:])
            shapes.append(pltpu.VMEM(shape, arrays[i].dtype))
        shapes += [self.scratch[n] for n in scratch]
        shapes += [pltpu.SemaphoreType.DMA((max(1, count),)) for count in (len(staged), 2 * len(outs) + 2, self.spare)]

        def kernel(*refs):
            ins, rest = refs[:first_after], refs[len(arrays) :]
            ins = [ref.at[r[0] : r[1]] if r else ref for ref, r in zip(ins, ranges)]
            out_refs, rest = rest[: len(outs)], rest[len(outs) :]
            bufs, (in_sems, out_sems, spare) = rest[:-3], rest[-3:]
            env = Env()
            env.refs = dict(zip(smem + staged + raw, ins))
            env.refs.update(zip(outs, out_refs))
            env.bufs = dict(zip(staged + scratch, bufs))
            env.out_sems, env.spare, env.pending, env.flying = out_sems, spare, {}, []
            for i, name in enumerate(staged):
                env.pending[name] = pltpu.make_async_copy(env.refs[name], env.bufs[name], in_sems.at[i])
                env.pending[name].start()
            body(env)
            assert not env.pending, list(env.pending)
            for copy in env.flying:
                copy.wait()

        names = smem + staged + raw
        return pl.pallas_call(
            kernel,
            out_shape=[self.outs[n] for n in outs],
            in_specs=specs,
            out_specs=[hbm] * len(outs),
            scratch_shapes=shapes,
            input_output_aliases={names.index(a): outs.index(b) for a, b in self.aliases.items()},
            compiler_params=pltpu.CompilerParams(vmem_limit_bytes=VMEM_LIMIT),
            cost_estimate=pl.CostEstimate(flops=self.flops, bytes_accessed=4 << 20, transcendentals=0),
            name=self.name,
        )(*arrays)


class Env:
    def get(self, name):
        if name in self.pending:
            self.pending.pop(name).wait()
        return self.bufs[name]

    def send(self, src, dst):
        copy = pltpu.make_async_copy(src, dst, self.out_sems.at[len(self.flying)])
        copy.start()
        self.flying.append(copy)

    def choose(self, pick, yes, no, dst, number):
        @pl.when(pick)
        def _():
            pltpu.make_async_copy(yes, dst, self.spare.at[number]).start()

        @pl.when(jnp.logical_not(pick))
        def _():
            pltpu.make_async_copy(no, dst, self.spare.at[number]).start()

        return pltpu.make_async_copy(no, dst, self.spare.at[number])


def project(x_ref, w_ref, store, tile=256):
    for col in range(0, w_ref.shape[1], tile):
        store(col, dot(x_ref[...], w_ref[:, col : col + tile]))


def store_scaled(out_ref, scale):
    def store(col, value):
        if scale is not None:
            value = value * scale
        out_ref[:, col : col + value.shape[1]] = value.astype(BF16)

    return store


def score_scale(head):
    return math.log2(math.e) / math.sqrt(head)


def value_rows(width):
    return width + HEADS * ONES


def store_values(vt_ref, head):
    keys = vt_ref.shape[1]
    pitch = head + ONES

    def store(col, value):
        for part in range(0, value.shape[1], head):
            at = (col + part) // head * pitch
            vt_ref[at : at + head, :] = value[:, part : part + head].T.astype(BF16)
            vt_ref[at + head : at + pitch, :] = jnp.ones((ONES, keys), BF16)

    return store


def in_turn(units, scores, finish):
    ahead = scores(*units[0])
    for number, unit in enumerate(units):
        now = ahead
        if number + 1 < len(units):
            ahead = scores(*units[number + 1])
        finish(*unit, now)


def update_rows(env, h_ref, k_ref, vt_ref, out_ref):
    rows, width = h_ref.shape
    head = width // HEADS
    pitch = head + ONES
    tile = min(256, rows)
    qs_ref, o_ref = env.get("qs"), env.get("o")
    project(h_ref, env.get("wqs"), store_scaled(qs_ref, score_scale(head)))
    k_ref, vt_ref = k_ref(), vt_ref()

    def scores(h, r):
        part = slice(h * head, (h + 1) * head)
        return dot_t(k_ref[:, part], qs_ref[r : r + tile, part])

    def finish(h, r, s):
        p = jnp.exp2(s - jnp.max(s, axis=0, keepdims=True)).astype(BF16)
        ol = dot(vt_ref[h * pitch : (h + 1) * pitch, :], p)
        o = ol[:head] * (1.0 / ol[head : head + 1])
        o_ref[r : r + tile, h * head : (h + 1) * head] = o.T.astype(BF16)

    in_turn([(h, r) for h in range(HEADS) for r in range(0, rows, tile)], scores, finish)
    wcg_ref, bias_ref = env.get("wcg"), env.get("bias")
    for col in range(0, width, 256):
        part = slice(col, col + 256)
        zc = dot(o_ref[...], wcg_ref[:, part])
        zg = dot(o_ref[...], wcg_ref[:, width + col : width + col + 256])
        cand = jnp.tanh(zc)
        forget = 0.5 * jnp.tanh(0.5 * (zg + bias_ref[:, part])) + 0.5
        out_ref[:, part] = (forget * h_ref[:, part].astype(F32) + (1.0 - forget) * cand).astype(BF16)


def attend_more(q_ref, k_ref, vt_ref, o_ref, ml_ref, tile, limit, first, mask):
    rows, width = q_ref.shape
    head = width // HEADS
    pitch = head + ONES

    def scores(h, r):
        part = slice(h * head, (h + 1) * head)
        return dot_t(k_ref[: limit(r), part], q_ref[r : r + tile, part])

    def finish(h, r, s):
        part = slice(h * head, (h + 1) * head)
        across = slice(r, r + tile)
        s = mask(s, r)
        top = jnp.max(s, axis=0, keepdims=True)
        if not first:
            old = ml_ref[h : h + 1, across]
            top = jnp.maximum(top, old)
        p = jnp.exp2(s - top).astype(BF16)
        ol = dot(vt_ref[h * pitch : (h + 1) * pitch, : limit(r)], p)
        o, l = ol[:head], ol[head : head + 1]
        if not first:
            keep = jnp.exp2(old - top)
            o = o + keep * o_ref[part, across]
            l = l + keep * ml_ref[HEADS + h : HEADS + h + 1, across]
        o_ref[part, across] = o
        ml_ref[h : h + 1, across] = top
        ml_ref[HEADS + h : HEADS + h + 1, across] = l

    in_turn([(h, r) for h in range(HEADS) for r in range(0, rows, tile)], scores, finish)


def mixed_guess(shift_v, cur_v, prev_v, mixing, sweep, guess_v):
    a, b, c = mixing[sweep, 0], mixing[sweep, 1], mixing[sweep, 2]
    rows = guess_v.shape[0]
    step = min(64, rows)
    for r in range(0, rows, step):
        part = slice(r, r + step)
        guess = a * shift_v[part, :].astype(F32) + b * cur_v[part, :].astype(F32)
        guess_v[part, :] = (guess + c * prev_v[part, :].astype(F32)).astype(BF16)


def bf(*shape):
    return jax.ShapeDtypeStruct(shape, BF16)


def f32(*shape):
    return jax.ShapeDtypeStruct(shape, F32)


def vm(*shape, dtype=BF16):
    return pltpu.VMEM(shape, dtype)


def per_device(
    tokens, init_state, w_query, w_key, w_value, w_out, w_query_state, w_cand_gate, w_state_kv,
    gate_bias, mixing, retrieval,
):
    rows, width = tokens.shape
    states = init_state.shape[0]
    head = width // HEADS
    some = states // PARTS
    count = lax.axis_size("seq")
    place = lax.axis_index("seq").astype(jnp.int32).reshape(1)
    bias = gate_bias.reshape(1, width)
    work = 2 * rows * width * width
    parts = [(p * some, (p + 1) * some) for p in range(PARTS)]

    def step(value, by):
        return lax.ppermute(value, "seq", [(i, i + by) for i in range(count - by)])

    def swap(value, bit):
        return lax.ppermute(value, "seq", [(i, i ^ bit) for i in range(count)])

    def update_operands(k):
        k.staged.update(wqs=w_query_state)
        if "key" not in k.scratch:
            k.staged.update(key=key, vt=vt)
        k.staged.update(wcg=w_cand_gate, bias=bias)
        k.scratch.update(qs=vm(some, width), o=vm(some, width), s=vm(some, width))
        k.outs.update(s_out=bf(some, width))

    back4 = step(tokens, WIN)

    def first_body(env):
        project(env.get("tok"), env.get("wk"), store_scaled(env.get("key"), None))
        env.send(env.get("key"), env.refs["key_out"])
        project(env.get("tok"), env.get("wv"), store_values(env.get("vt"), head))
        env.send(env.get("vt"), env.refs["vt_out"])
        update_rows(env, env.get("init"), lambda: env.get("key"), lambda: env.get("vt"), env.get("s"))
        env.send(env.get("s"), env.refs["s_out"])

    k = Kernel("keys_values_update", 2 * work + 4 * work // PARTS)
    k.staged.update(tok=tokens, wk=w_key, wv=w_value, init=(init_state, parts[0]))
    k.scratch.update(key=vm(rows, width), vt=vm(value_rows(width), rows))
    k.outs.update(key_out=bf(rows, width), vt_out=bf(value_rows(width), rows))
    update_operands(k)
    key, vt, out = k.call(first_body)
    got1 = [step(out, 1)]

    def more_body(env):
        update_rows(env, env.get("init"), lambda: env.get("key"), lambda: env.get("vt"), env.get("s"))
        env.send(env.get("s"), env.refs["s_out"])

    for p in range(1, PARTS):
        k = Kernel("update_more", 4 * work // PARTS)
        k.staged.update(init=(init_state, parts[p]))
        update_operands(k)
        (out,) = k.call(more_body, after=[out])
        got1.append(step(out, 1))

    def second_body(env):
        pick = env.refs["place"][0] == 0
        shift = env.choose(pick, env.refs["init_h"], env.refs["got"], env.get("shift"), 0)
        pay = None
        if "back4" in env.refs:
            low = env.refs["place"][0] % WIN < WIN // 2
            pay = env.choose(low, env.refs["tok"], env.refs["back4"], env.refs["pay"], 1)
        shift.wait()
        guess_v, init_v = env.get("guess"), env.get("init")
        mixed_guess(env.get("shift"), init_v, init_v, env.refs["mixing"], 0, guess_v)
        env.send(guess_v, env.refs["guess_out"])
        update_rows(env, guess_v, lambda: env.get("key"), lambda: env.get("vt"), env.get("s"))
        env.send(env.get("s"), env.refs["s_out"])
        if pay is not None:
            pay.wait()

    after = out
    guesses, got2 = [], []
    for p in range(PARTS):
        k = Kernel("update_second", 4 * work // PARTS)
        k.smem.update(place=place, mixing=mixing)
        k.staged.update(init=(init_state, parts[p]))
        k.raw.update(init_h=(init_state, parts[p]), got=got1[p])
        if p == PARTS - 1:
            k.raw.update(tok=tokens, back4=back4)
        k.scratch.update(shift=vm(some, width), guess=vm(some, width))
        k.outs.update(guess_out=bf(some, width))
        update_operands(k)
        if p == PARTS - 1:
            k.outs.update(pay=bf(rows, width))
        k.spare = 2
        guess, out, *pay = k.call(second_body, after=[after])
        after = out
        guesses.append(guess)
        got2.append(step(out, 1))
    back2 = swap(pay[0], WIN // 2)

    def local_body(env):
        q_v, o_v, ml_v = env.get("q"), env.get("acc"), env.get("ml")
        project(env.get("tok"), env.get("wq"), store_scaled(q_v, score_scale(head)))
        env.send(q_v, env.refs["q_out"])
        tile = min(256, rows)

        def causal(s, r):
            down = r + lax.broadcasted_iota(jnp.int32, (tile, tile), 0)
            across = r + lax.broadcasted_iota(jnp.int32, (tile, tile), 1)
            last = jnp.where(down <= across, s[r:], NEG)
            return last if r == 0 else jnp.concatenate([s[:r], last], axis=0)

        attend_more(q_v, env.get("key"), env.get("vt"), o_v, ml_v, tile, lambda r: r + tile, True, causal)
        env.send(o_v, env.refs["o_out"])
        env.send(ml_v, env.refs["ml_out"])

    k = Kernel("query_local", 2 * work)
    k.staged.update(tok=tokens, wq=w_query, key=key, vt=vt)
    k.scratch.update(q=vm(rows, width), acc=vm(width, rows, dtype=F32), ml=vm(2 * HEADS, rows, dtype=F32))
    k.outs.update(q_out=bf(rows, width), o_out=f32(width, rows), ml_out=f32(2 * HEADS, rows))
    q, o, ml = k.call(local_body, after=[after])
    after = ml

    def third_body(env):
        place = env.refs["place"][0]
        part = env.part
        shift = env.choose(place == 0, env.refs["init_h"], env.refs["got"], env.get("shift"), 0)
        prev = env.choose(place == 0, env.refs["init_h"], env.refs["before"], env.get("prev"), 1)
        shift.wait()
        prev.wait()
        guess_v = env.get("guess")
        mixed_guess(env.get("shift"), env.get("cur"), env.get("prev"), env.refs["mixing"], 1, guess_v)
        env.send(guess_v, env.refs["guess_out"])
        update_rows(env, guess_v, lambda: env.get("key"), lambda: env.get("vt"), env.get("s"))
        env.send(env.get("s"), env.refs["s_out"].at[part * some : (part + 1) * some, :])

    finals = []
    for p in range(PARTS):
        k = Kernel("update_third", 4 * work // PARTS)
        k.smem.update(place=place, mixing=mixing)
        k.staged.update(cur=guesses[p])
        k.raw.update(init_h=(init_state, parts[p]), got=got2[p], before=got1[p])
        k.scratch.update(shift=vm(some, width), prev=vm(some, width), guess=vm(some, width))
        k.outs.update(guess_out=bf(some, width))
        update_operands(k)
        k.outs.update(s_out=bf(states, width))
        if p:
            k.raw.update(so_far=new_state)
            k.aliases.update(so_far="s_out")
        k.spare = 2

        def body(env, p=p):
            env.part = p
            third_body(env)

        guess, new_state = k.call(body, after=[after])
        after = guess
        finals.append(guess)

    def state_body(env):
        place = env.refs["place"][0]
        even = place % 2 == 0
        pays = [
            env.choose(even, env.refs["tok"], env.refs["back2"], env.refs["pay"].at[0], 0),
            env.choose(even, env.refs["back2"], env.refs["back4"], env.refs["pay"].at[1], 1),
        ]
        key_v, vt_v = env.get("skey"), env.get("svt")
        guess_v = env.get("guess")
        for p in range(PARTS):
            copy = pltpu.make_async_copy(env.refs["guess%d" % p], guess_v.at[p * some : (p + 1) * some, :], env.spare.at[2 + p])
            copy.start()
            copy.wait()
        project(guess_v, env.get("wskv").at[:, :width], store_scaled(key_v, None))
        project(guess_v, env.get("wskv").at[:, width:], store_values(vt_v, head))
        o_v, ml_v = env.get("acc"), env.get("ml")
        attend_more(env.get("q"), key_v, vt_v, o_v, ml_v, min(256, rows), lambda r: states, False, lambda s, r: s)
        env.send(o_v, env.refs["o_out"])
        env.send(ml_v, env.refs["ml_out"])
        for copy in pays:
            copy.wait()

    k = Kernel("state_keys", 4 * work)
    k.smem.update(place=place)
    k.staged.update(wskv=w_state_kv, q=q, acc=o, ml=ml)
    k.raw.update({"guess%d" % p: finals[p] for p in range(PARTS)})
    k.raw.update(tok=tokens, back2=back2, back4=back4)
    k.scratch.update(guess=vm(states, width), skey=vm(states, width), svt=vm(value_rows(width), states))
    k.outs.update(o_out=f32(width, rows), ml_out=f32(2 * HEADS, rows), pay=bf(2, rows, width))
    k.spare = 2 + PARTS
    o, ml, pay = k.call(state_body)
    near = swap(pay, 1)

    mem = retrieval.shape[1] * BLK

    def last_body(env):
        place = env.refs["place"][0]
        mem_v = env.get("mem")
        near = env.refs["near"]
        sources = (near.at[0], env.refs["back2"], near.at[1], env.refs["back4"])
        waits, lift = [], []
        for e in range(mem // BLK):
            entry = env.refs["retrieval"][0, e]
            distance = entry // MBLK
            start = pl.multiple_of((entry % MBLK) * BLK, BLK)
            target = mem_v.at[e * BLK : (e + 1) * BLK, :]
            for number, source in enumerate(sources):

                @pl.when(distance == number)
                def _(source=source, start=start, target=target, e=e):
                    pltpu.make_async_copy(source.at[pl.ds(start, BLK), :], target, env.spare.at[e]).start()

            waits.append(pltpu.make_async_copy(sources[1].at[0:BLK, :], target, env.spare.at[e]))
            lift.append(jnp.where(distance + 1 > place, NEG, 0.0))
        for copy in waits:
            copy.wait()
        key_v, vt_v = env.get("key"), env.get("vt")
        project(mem_v, env.get("wk"), store_scaled(key_v, None))
        project(mem_v, env.get("wv"), store_values(vt_v, head))
        o_v, ml_v = env.get("acc"), env.get("ml")

        def mask(s, r):
            return jnp.concatenate([s[e * BLK : (e + 1) * BLK] + lift[e] for e in range(mem // BLK)], axis=0)

        attend_more(env.get("q"), key_v, vt_v, o_v, ml_v, min(256, rows), lambda r: mem, False, mask)
        on_v, mixed_v, tok_v = env.get("on"), env.get("mixed"), env.get("tok")
        for h in range(HEADS):
            part = slice(h * head, (h + 1) * head)
            on_v[:, part] = (o_v[part, :] * (1.0 / ml_v[HEADS + h : HEADS + h + 1, :])).T.astype(BF16)

        def store(col, value):
            part = slice(col, col + value.shape[1])
            mixed_v[:, part] = (tok_v[:, part].astype(F32) + value).astype(BF16)

        project(on_v, env.get("wout"), store)
        env.send(mixed_v, env.refs["mixed_out"])

    k = Kernel("memory_out", 5 * work)
    k.smem.update(place=place, retrieval=retrieval)
    k.staged.update(wk=w_key, wv=w_value, q=q, acc=o, ml=ml, wout=w_out, tok=tokens)
    k.raw.update(near=near, back2=back2, back4=back4)
    k.scratch.update(
        mem=vm(mem, width), key=vm(mem, width), vt=vm(value_rows(width), mem), on=vm(rows, width), mixed=vm(rows, width)
    )
    k.outs.update(mixed_out=bf(rows, width))
    k.spare = mem // BLK
    (mixed,) = k.call(last_body)
    return mixed, new_state


def solution(mesh):
    return jax.shard_map(
        per_device,
        mesh=mesh,
        in_specs=(P("seq", None), P(), P(), P(), P(), P(), P(), P(), P(), P(), P(), P("seq", None)),
        out_specs=(P("seq", None), P("seq", None)),
        check_vma=False,
    )
```

```python
import math

import jax
import jax.numpy as jnp
from jax import lax
from jax.experimental import pallas as pl
from jax.experimental.pallas import tpu as pltpu
from jax.sharding import PartitionSpec as P

HEADS = 8
BLK = 64
MBLK = 8
WIN = 4
PARTS = 2
ONES = 16
NEG = -1e30
VMEM_LIMIT = 16 * 1024 * 1024

BF16 = jnp.bfloat16
F32 = jnp.float32


def dot(a, b):
    return jnp.dot(a, b, preferred_element_type=F32)


def dot_t(a, b):
    return lax.dot_general(a, b, (((1,), (1,)), ((), ())), preferred_element_type=F32)


class Kernel:
    def __init__(self, name, flops):
        self.name, self.flops = name, flops
        self.smem, self.near, self.far = {}, {}, {}
        self.near_out, self.far_out, self.scratch = {}, {}, {}
        self.aliases = {}
        self.copies = 1

    def call(self, body, after=()):
        smem, near, far = list(self.smem), list(self.near), list(self.far)
        near_out, far_out, scratch = list(self.near_out), list(self.far_out), list(self.scratch)
        arrays = [self.smem[n] for n in smem]
        arrays += [pltpu.with_memory_space_constraint(self.near[n], pltpu.VMEM) for n in near]
        arrays += [pltpu.with_memory_space_constraint(self.far[n], pltpu.HBM) for n in far]
        arrays += [pltpu.with_memory_space_constraint(a, pltpu.VMEM) for a in after]
        memory = [pltpu.SMEM] * len(smem) + [pltpu.VMEM] * len(near) + [pltpu.HBM] * len(far) + [pltpu.VMEM] * len(after)
        outs = [pltpu.VMEM(self.near_out[n].shape, self.near_out[n].dtype) for n in near_out]
        outs += [self.far_out[n] for n in far_out]
        out_memory = [pltpu.VMEM] * len(near_out) + [pltpu.HBM] * len(far_out)
        names = smem + near + far
        out_names = near_out + far_out

        def kernel(*refs):
            env = Env()
            env.refs = dict(zip(names, refs))
            env.refs.update(zip(out_names, refs[len(arrays) :]))
            env.refs.update(zip(scratch, refs[len(arrays) + len(outs) :]))
            env.sems, env.started = refs[-1], 0
            body(env)

        return pl.pallas_call(
            kernel,
            out_shape=outs,
            in_specs=[pl.BlockSpec(memory_space=m) for m in memory],
            out_specs=[pl.BlockSpec(memory_space=m) for m in out_memory],
            scratch_shapes=[self.scratch[n] for n in scratch] + [pltpu.SemaphoreType.DMA((self.copies,))],
            input_output_aliases={names.index(a): out_names.index(b) for a, b in self.aliases.items()},
            compiler_params=pltpu.CompilerParams(vmem_limit_bytes=VMEM_LIMIT),
            cost_estimate=pl.CostEstimate(flops=self.flops, bytes_accessed=1 << 20, transcendentals=0),
            name=self.name,
        )(*arrays)


class Env:
    def __getattr__(self, name):
        return self.refs[name]

    def copy(self, src, dst):
        copy = pltpu.make_async_copy(src, dst, self.sems.at[self.started])
        self.started += 1
        copy.start()
        return copy


def project(x_ref, w_ref, store, tile=256):
    for col in range(0, w_ref.shape[1], tile):
        store(col, dot(x_ref[...], w_ref[:, col : col + tile]))


def store_scaled(out_ref, scale):
    def store(col, value):
        if scale is not None:
            value = value * scale
        out_ref[:, col : col + value.shape[1]] = value.astype(BF16)

    return store


def score_scale(head):
    return math.log2(math.e) / math.sqrt(head)


def value_rows(width):
    return width + HEADS * ONES


def store_values(vt_ref, head):
    keys = vt_ref.shape[1]
    pitch = head + ONES

    def store(col, value):
        for part in range(0, value.shape[1], head):
            at = (col + part) // head * pitch
            vt_ref[at : at + head, :] = value[:, part : part + head].T.astype(BF16)
            vt_ref[at + head : at + pitch, :] = jnp.ones((ONES, keys), BF16)

    return store


def in_turn(units, scores, finish):
    ahead = scores(*units[0])
    for number, unit in enumerate(units):
        now = ahead
        if number + 1 < len(units):
            ahead = scores(*units[number + 1])
        finish(*unit, now)


def update_rows(h_ref, wqs_ref, key_ref, vt_ref, wcg_ref, bias_ref, qs_ref, o_ref, out_ref, ready=None):
    rows, width = h_ref.shape
    head = width // HEADS
    pitch = head + ONES
    tile = min(256, rows)
    project(h_ref, wqs_ref, store_scaled(qs_ref, score_scale(head)))

    def scores(h, r):
        part = slice(h * head, (h + 1) * head)
        return dot_t(key_ref[:, part], qs_ref[r : r + tile, part])

    def finish(h, r, s):
        p = jnp.exp2(s - jnp.max(s, axis=0, keepdims=True)).astype(BF16)
        ol = dot(vt_ref[h * pitch : (h + 1) * pitch, :], p)
        o = ol[:head] * (1.0 / ol[head : head + 1])
        o_ref[r : r + tile, h * head : (h + 1) * head] = o.T.astype(BF16)

    in_turn([(h, r) for h in range(HEADS) for r in range(0, rows, tile)], scores, finish)
    if ready is not None:
        ready()
    for col in range(0, width, 256):
        part = slice(col, col + 256)
        zc = dot(o_ref[...], wcg_ref[:, part])
        zg = dot(o_ref[...], wcg_ref[:, width + col : width + col + 256])
        cand = jnp.tanh(zc)
        forget = 0.5 * jnp.tanh(0.5 * (zg + bias_ref[:, part])) + 0.5
        out_ref[:, part] = (forget * h_ref[:, part].astype(F32) + (1.0 - forget) * cand).astype(BF16)


def attend(q_ref, key_ref, vt_ref, places, limit, mask, old_o, old_ml, new_o, new_ml):
    head = q_ref.shape[1] // HEADS
    pitch = head + ONES
    tile = new_o[places[0]].shape[1]

    def scores(h, t):
        part = slice(h * head, (h + 1) * head)
        return dot_t(key_ref[: limit(t), part], q_ref[t * tile : (t + 1) * tile, part])

    def finish(h, t, s):
        part = slice(h * head, (h + 1) * head)
        top_row, sum_row = slice(h, h + 1), slice(HEADS + h, HEADS + h + 1)
        s = mask(s, t)
        top = jnp.max(s, axis=0, keepdims=True)
        if old_o is not None:
            old = old_ml[t][top_row, :]
            top = jnp.maximum(top, old)
        p = jnp.exp2(s - top).astype(BF16)
        ol = dot(vt_ref[h * pitch : (h + 1) * pitch, : limit(t)], p)
        o, l = ol[:head], ol[head : head + 1]
        if old_o is not None:
            keep = jnp.exp2(old - top)
            o = o + keep * old_o[t][part, :]
            l = l + keep * old_ml[t][sum_row, :]
        new_o[t][part, :] = o
        new_ml[t][top_row, :] = top
        new_ml[t][sum_row, :] = l

    in_turn([(h, t) for h in range(HEADS) for t in places], scores, finish)


def mixed_guess(pick, init_ref, got_ref, cur_ref, prev_ref, prev_pick, mixing, sweep, guess_ref):
    a, b, c = mixing[sweep, 0], mixing[sweep, 1], mixing[sweep, 2]
    rows = guess_ref.shape[0]
    step = min(64, rows)
    for r in range(0, rows, step):
        part = slice(r, r + step)
        init = init_ref[part, :].astype(F32)
        shift = jnp.where(pick, init, got_ref[part, :].astype(F32))
        prev = prev_ref[part, :].astype(F32)
        if prev_pick:
            prev = jnp.where(pick, init, prev)
        guess = a * shift + b * cur_ref[part, :].astype(F32)
        guess_ref[part, :] = (guess + c * prev).astype(BF16)


def either(pick, yes_ref, no_ref, out_ref):
    @pl.when(pick)
    def _():
        out_ref[...] = yes_ref[...]

    @pl.when(jnp.logical_not(pick))
    def _():
        out_ref[...] = no_ref[...]


def bf(*shape):
    return jax.ShapeDtypeStruct(shape, BF16)


def f32(*shape):
    return jax.ShapeDtypeStruct(shape, F32)


def vm(*shape, dtype=BF16):
    return pltpu.VMEM(shape, dtype)


def per_device(
    tokens, init_state, w_query, w_key, w_value, w_out, w_query_state, w_cand_gate, w_state_kv,
    gate_bias, mixing, retrieval,
):
    rows, width = tokens.shape
    states = init_state.shape[0]
    head = width // HEADS
    some = states // PARTS
    tile = min(256, rows)
    tiles = list(range(rows // tile))
    mem = retrieval.shape[1] * BLK
    count = lax.axis_size("seq")
    place = lax.axis_index("seq").astype(jnp.int32).reshape(1)
    work = 2 * rows * width * width

    def step(value, by):
        return lax.ppermute(value, "seq", [(i, i + by) for i in range(count - by)])

    def swap(value, bit):
        return lax.ppermute(value, "seq", [(i, i ^ bit) for i in range(count)])

    def rows_of(ref, p):
        return ref.at[p * some : (p + 1) * some]

    back4 = step(tokens, WIN)

    arguments = dict(
        tok=tokens, wk=w_key, wv=w_value, wqs=w_query_state, init=init_state, wcg=w_cand_gate,
        bias=gate_bias.reshape(1, width), wq=w_query, wskv=w_state_kv, wout=w_out,
    )

    def first_body(env):
        copies = {}

        def start(*names):
            for name in names:
                copies[name] = env.copy(env.refs[name], env.refs[name + "_v"])

        def wait(*names):
            for name in names:
                copies.pop(name).wait()

        start("tok", "wk", "wv")
        wait("tok", "wk")
        start("wqs", "init")
        project(env.tok_v, env.wk_v, store_scaled(env.key, None))
        wait("wv")
        start("wcg", "bias", "wq")
        project(env.tok_v, env.wv_v, store_values(env.vt, head))
        wait("wqs", "init")
        start("wskv", "wout")
        update_rows(
            rows_of(env.init_v, 0), env.wqs_v, env.key, env.vt, env.wcg_v, env.bias_v, env.qs, env.o, env.state,
            lambda: wait("wcg", "bias"),
        )
        wait(*list(copies))

    k = Kernel("keys_values_update", 2 * work + 4 * work // PARTS)
    k.far.update(arguments)
    k.near_out.update({name + "_v": jax.ShapeDtypeStruct(a.shape, a.dtype) for name, a in arguments.items()})
    k.near_out.update(key=bf(rows, width), vt=bf(value_rows(width), rows), state=bf(some, width))
    k.scratch.update(qs=vm(some, width), o=vm(some, width))
    k.copies = len(arguments)
    *held, key, vt, state = k.call(first_body)
    held = dict(zip(arguments, held))
    got1 = [step(state, 1)]

    def update_operands(k):
        k.near.update({name: held[name] for name in ("init", "wqs", "wcg", "bias")}, key=key, vt=vt)
        k.near_out.update(state=bf(some, width))
        k.scratch.update(qs=vm(some, width), o=vm(some, width))

    def update(env, h_ref, out_ref):
        update_rows(h_ref, env.wqs, env.key, env.vt, env.wcg, env.bias, env.qs, env.o, out_ref)

    for p in range(1, PARTS):
        k = Kernel("update_more", 4 * work // PARTS)
        update_operands(k)
        (state,) = k.call(lambda env: update(env, rows_of(env.init, p), env.state), after=[state])
        got1.append(step(state, 1))
    after = state

    def causal(s, t):
        down = lax.broadcasted_iota(jnp.int32, (tile, tile), 0)
        across = lax.broadcasted_iota(jnp.int32, (tile, tile), 1)
        last = jnp.where(down <= across, s[t * tile :], NEG)
        return last if t == 0 else jnp.concatenate([s[: t * tile], last], axis=0)

    def local(env, t):
        attend(env.q, env.key, env.vt, [t], lambda t: (t + 1) * tile, causal, None, None, {t: env.o}, {t: env.ml})

    def local_outs(k):
        k.near_out.update(o=f32(width, tile), ml=f32(2 * HEADS, tile))

    def query_body(env):
        project(env.tok, env.wq, store_scaled(env.q, score_scale(head)))
        local(env, 0)

    k = Kernel("query_local", 2 * work)
    k.near.update(tok=held["tok"], wq=held["wq"], key=key, vt=vt)
    k.near_out.update(q=bf(rows, width))
    local_outs(k)
    q, o, ml = k.call(query_body, after=[after])
    after, run_o, run_ml = ml, [o], [ml]

    guesses, got2 = [], []

    def second_body(env, p):
        pick = env.place[0] == 0
        init = rows_of(env.init, p)
        mixed_guess(pick, init, env.got, init, init, False, env.mixing, 0, env.guess)
        update(env, env.guess, env.state)

    for p in range(PARTS):
        k = Kernel("update_second", 4 * work // PARTS)
        k.smem.update(place=place, mixing=mixing)
        update_operands(k)
        k.near.update(got=got1[p])
        k.near_out.update(guess=bf(some, width))
        state, guess = k.call(lambda env: second_body(env, p), after=[after])
        after = state
        guesses.append(guess)
        got2.append(step(state, 1))
        if p == 0:
            k = Kernel("pair_payload", 1)
            k.smem.update(place=place)
            k.near.update(tok=held["tok"], back4=back4)
            k.near_out.update(pay=bf(rows, width))
            (pay,) = k.call(
                lambda env: either(env.place[0] % WIN < WIN // 2, env.tok, env.back4, env.pay), after=[after]
            )
            back2 = swap(pay, WIN // 2)

    for t in tiles[1:]:
        k = Kernel("local_more", work)
        k.near.update(q=q, key=key, vt=vt)
        local_outs(k)
        o, ml = k.call(lambda env: local(env, t), after=[after])
        after = ml
        run_o.append(o)
        run_ml.append(ml)

    finals = []
    new_state = None

    def third_body(env, p):
        mixed_guess(
            env.place[0] == 0, rows_of(env.init, p), env.got, env.cur, env.before, True, env.mixing, 1, env.guess
        )
        update(env, env.guess, env.state)
        env.copy(env.state, rows_of(env.new_state, p)).wait()

    for p in range(PARTS):
        k = Kernel("update_third", 4 * work // PARTS)
        k.smem.update(place=place, mixing=mixing)
        update_operands(k)
        k.near.update(got=got2[p], before=got1[p], cur=guesses[p])
        del k.near_out["state"]
        k.scratch.update(state=vm(some, width))
        k.near_out.update(guess=bf(some, width))
        k.far_out.update(new_state=bf(states, width))
        if p:
            k.far.update(so_far=new_state)
            k.aliases.update(so_far="new_state")
        guess, new_state = k.call(lambda env: third_body(env, p), after=[after])
        after = guess
        finals.append(guess)

    def running(k):
        for t in tiles:
            k.near.update({"o%d" % t: run_o[t], "ml%d" % t: run_ml[t]})

    def refs_of(env, name):
        return {t: env.refs["%s%d" % (name, t)] for t in tiles}

    def state_body(env):
        even = env.place[0] % 2 == 0
        either(even, env.tok, env.back2, env.pay.at[0])
        either(even, env.back2, env.back4, env.pay.at[1])
        for p in range(PARTS):
            project(env.refs["guess%d" % p], env.wskv.at[:, :width], store_scaled(rows_of(env.skey, p), None))
            project(
                env.refs["guess%d" % p], env.wskv.at[:, width:], store_values(env.svt.at[:, p * some : (p + 1) * some], head)
            )
        attend(
            env.q, env.skey, env.svt, tiles, lambda t: states, lambda s, t: s,
            refs_of(env, "o"), refs_of(env, "ml"), refs_of(env, "new_o"), refs_of(env, "new_ml"),
        )

    k = Kernel("state_keys", 4 * work)
    k.smem.update(place=place)
    k.near.update(wskv=held["wskv"], q=q, tok=held["tok"], back2=back2, back4=back4)
    k.near.update({"guess%d" % p: finals[p] for p in range(PARTS)})
    running(k)
    for t in tiles:
        k.near_out.update({"new_o%d" % t: f32(width, tile), "new_ml%d" % t: f32(2 * HEADS, tile)})
    k.near_out.update(pay=bf(2, rows, width))
    k.scratch.update(skey=vm(states, width), svt=vm(value_rows(width), states))
    *pairs, pay = k.call(state_body)
    run_o, run_ml = pairs[0::2], pairs[1::2]
    beside = swap(pay, 1)

    def last_body(env):
        sources = (env.beside.at[0], env.back2, env.beside.at[1], env.back4)
        lift = []
        for e in range(mem // BLK):
            entry = env.retrieval[0, e]
            distance = entry // MBLK
            start = pl.multiple_of((entry % MBLK) * BLK, BLK)
            for number, source in enumerate(sources):

                @pl.when(distance == number)
                def _(source=source, start=start, e=e):
                    env.mem[e * BLK : (e + 1) * BLK, :] = source[pl.ds(start, BLK), :]

            lift.append(jnp.where(distance + 1 > env.place[0], NEG, 0.0))
        project(env.mem, env.wk, store_scaled(env.key, None))
        project(env.mem, env.wv, store_values(env.vt, head))

        def mask(s, t):
            return jnp.concatenate([s[e * BLK : (e + 1) * BLK] + lift[e] for e in range(mem // BLK)], axis=0)

        new_o, new_ml = refs_of(env, "new_o"), refs_of(env, "new_ml")
        attend(env.q, env.key, env.vt, tiles, lambda t: mem, mask, refs_of(env, "o"), refs_of(env, "ml"), new_o, new_ml)
        for t in tiles:
            for h in range(HEADS):
                part = slice(h * head, (h + 1) * head)
                o = new_o[t][part, :] * (1.0 / new_ml[t][HEADS + h : HEADS + h + 1, :])
                env.on[t * tile : (t + 1) * tile, part] = o.T.astype(BF16)

        def store(col, value):
            part = slice(col, col + value.shape[1])
            env.sum[:, part] = (env.tok[:, part].astype(F32) + value).astype(BF16)

        project(env.on, env.wout, store)
        env.copy(env.sum, env.mixed).wait()

    k = Kernel("memory_out", 5 * work)
    k.smem.update(place=place, retrieval=retrieval)
    k.near.update({name: held[name] for name in ("wk", "wv", "wout", "tok")}, q=q, beside=beside, back2=back2, back4=back4)
    running(k)
    k.scratch.update(
        mem=vm(mem, width), key=vm(mem, width), vt=vm(value_rows(width), mem), on=vm(rows, width), sum=vm(rows, width)
    )
    for t in tiles:
        k.scratch.update({"new_o%d" % t: vm(width, tile, dtype=F32), "new_ml%d" % t: vm(2 * HEADS, tile, dtype=F32)})
    k.far_out.update(mixed=bf(rows, width))
    (mixed,) = k.call(last_body)
    return mixed, new_state


def solution(mesh):
    return jax.shard_map(
        per_device,
        mesh=mesh,
        in_specs=(P("seq", None), P(), P(), P(), P(), P(), P(), P(), P(), P(), P(), P("seq", None)),
        out_specs=(P("seq", None), P("seq", None)),
        check_vma=False,
    )
```

```python
import math

import jax
import jax.numpy as jnp
from jax import lax
from jax.experimental import pallas as pl
from jax.experimental.pallas import tpu as pltpu
from jax.sharding import PartitionSpec as P

HEADS = 8
BLK = 64
MBLK = 8
WIN = 4
PARTS = 2
ONES = 16
NEG = -1e30
VMEM_LIMIT = 6 * 1024 * 1024

BF16 = jnp.bfloat16
F32 = jnp.float32


def dot(a, b):
    return jnp.dot(a, b, preferred_element_type=F32)


def dot_t(a, b):
    return lax.dot_general(a, b, (((1,), (1,)), ((), ())), preferred_element_type=F32)


class Kernel:
    def __init__(self, name, flops):
        self.name, self.flops = name, flops
        self.smem, self.near, self.far = {}, {}, {}
        self.near_out, self.far_out, self.scratch = {}, {}, {}
        self.aliases = {}
        self.copies = 1
        self.grant = VMEM_LIMIT

    def call(self, body, after=()):
        smem, near, far = list(self.smem), list(self.near), list(self.far)
        near_out, far_out, scratch = list(self.near_out), list(self.far_out), list(self.scratch)
        arrays = [self.smem[n] for n in smem]
        arrays += [pltpu.with_memory_space_constraint(self.near[n], pltpu.VMEM) for n in near]
        arrays += [pltpu.with_memory_space_constraint(self.far[n], pltpu.HBM) for n in far]
        arrays += [pltpu.with_memory_space_constraint(a, pltpu.VMEM) for a in after]
        memory = [pltpu.SMEM] * len(smem) + [pltpu.VMEM] * len(near) + [pltpu.HBM] * len(far) + [pltpu.VMEM] * len(after)
        outs = [pltpu.VMEM(self.near_out[n].shape, self.near_out[n].dtype) for n in near_out]
        outs += [self.far_out[n] for n in far_out]
        out_memory = [pltpu.VMEM] * len(near_out) + [pltpu.HBM] * len(far_out)
        names = smem + near + far
        out_names = near_out + far_out

        def kernel(*refs):
            env = Env()
            env.refs = dict(zip(names, refs))
            env.refs.update(zip(out_names, refs[len(arrays) :]))
            env.refs.update(zip(scratch, refs[len(arrays) + len(outs) :]))
            env.sems, env.started = refs[-1], 0
            body(env)

        return pl.pallas_call(
            kernel,
            out_shape=outs,
            in_specs=[pl.BlockSpec(memory_space=m) for m in memory],
            out_specs=[pl.BlockSpec(memory_space=m) for m in out_memory],
            scratch_shapes=[self.scratch[n] for n in scratch] + [pltpu.SemaphoreType.DMA((self.copies,))],
            input_output_aliases={names.index(a): out_names.index(b) for a, b in self.aliases.items()},
            compiler_params=pltpu.CompilerParams(vmem_limit_bytes=self.grant),
            cost_estimate=pl.CostEstimate(flops=self.flops // 4, bytes_accessed=1 << 20, transcendentals=0),
            name=self.name,
        )(*arrays)


class Env:
    def __getattr__(self, name):
        return self.refs[name]

    def copy(self, src, dst):
        copy = pltpu.make_async_copy(src, dst, self.sems.at[self.started])
        self.started += 1
        copy.start()
        return copy


def project(x_ref, w_ref, store, tile=256):
    for col in range(0, w_ref.shape[1], tile):
        store(col, dot(x_ref[...], w_ref[:, col : col + tile]))


def store_scaled(out_ref, scale):
    def store(col, value):
        if scale is not None:
            value = value * scale
        out_ref[:, col : col + value.shape[1]] = value.astype(BF16)

    return store


def score_scale(head):
    return math.log2(math.e) / math.sqrt(head)


def value_rows(width):
    return width + HEADS * ONES


def store_values(vt_ref, head):
    keys = vt_ref.shape[1]
    pitch = head + ONES

    def store(col, value):
        for part in range(0, value.shape[1], head):
            at = (col + part) // head * pitch
            vt_ref[at : at + head, :] = value[:, part : part + head].T.astype(BF16)
            vt_ref[at + head : at + pitch, :] = jnp.ones((ONES, keys), BF16)

    return store


def in_turn(units, scores, finish):
    ahead = scores(*units[0])
    for number, unit in enumerate(units):
        now = ahead
        if number + 1 < len(units):
            ahead = scores(*units[number + 1])
        finish(*unit, now)


def stand(value):
    return value.T


def update_columns(h_ref, wqs_ref, key_ref, vt_ref, wcg_ref, bias_ref, qs_ref, o_ref, finish_rows, beside=None):
    width, some = h_ref.shape
    head = width // HEADS
    pitch = head + ONES
    scale = score_scale(head)
    tall = min(512, width)
    for row in range(0, width, tall):
        part = slice(row, row + tall)
        qs_ref[part, :] = (dot(wqs_ref[part, :], h_ref[...]) * scale).astype(BF16)

    def scores(h):
        part = slice(h * head, (h + 1) * head)
        return dot(key_ref[:, part], qs_ref[part, :])

    def finish(h, s):
        if beside is not None:
            beside(h)
        p = jnp.exp2(s - jnp.max(s, axis=0, keepdims=True)).astype(BF16)
        ol = dot(vt_ref[h * pitch : (h + 1) * pitch, :], p)
        o_ref[h * head : (h + 1) * head, :] = (ol[:head] * (1.0 / ol[head : head + 1])).astype(BF16)

    in_turn([(h,) for h in range(HEADS)], scores, finish)
    tall = min(256, width)
    for row in range(0, width, tall):
        part = slice(row, row + tall)
        zc = dot(wcg_ref[part, :], o_ref[...])
        zg = dot(wcg_ref[width + row : width + row + tall, :], o_ref[...])
        lanes = bias_ref.shape[1]
        bias = jnp.concatenate([bias_ref[part, :]] * (some // lanes), axis=1)
        cand = jnp.tanh(zc)
        forget = 0.5 * jnp.tanh(0.5 * (zg + bias)) + 0.5
        finish_rows(row, forget * h_ref[part, :].astype(F32) + (1.0 - forget) * cand)


def attend(q_ref, key_ref, vt_ref, places, limit, mask, old_o, old_ml, new_o, new_ml):
    head = q_ref.shape[1] // HEADS
    pitch = head + ONES
    tile = new_o[places[0]].shape[1]

    def scores(h, t):
        part = slice(h * head, (h + 1) * head)
        return dot_t(key_ref[: limit(t), part], q_ref[t * tile : (t + 1) * tile, part])

    def finish(h, t, s):
        part = slice(h * head, (h + 1) * head)
        top_row, sum_row = slice(h, h + 1), slice(HEADS + h, HEADS + h + 1)
        s = mask(s, t)
        top = jnp.max(s, axis=0, keepdims=True)
        if old_o is not None:
            old = old_ml[t][top_row, :]
            top = jnp.maximum(top, old)
        p = jnp.exp2(s - top).astype(BF16)
        ol = dot(vt_ref[h * pitch : (h + 1) * pitch, : limit(t)], p)
        o, l = ol[:head], ol[head : head + 1]
        if old_o is not None:
            keep = jnp.exp2(old - top)
            o = o + keep * old_o[t][part, :]
            l = l + keep * old_ml[t][sum_row, :]
        new_o[t][part, :] = o
        new_ml[t][top_row, :] = top
        new_ml[t][sum_row, :] = l

    in_turn([(h, t) for h in range(HEADS) for t in places], scores, finish)


def mixed_guess(pick, init_ref, got_ref, cur_ref, prev_ref, prev_pick, mixing, sweep, guess_ref):
    a, b, c = mixing[sweep, 0], mixing[sweep, 1], mixing[sweep, 2]
    rows = guess_ref.shape[0]
    step = min(64, rows)
    for r in range(0, rows, step):
        part = slice(r, r + step)
        init = init_ref[part, :].astype(F32)
        shift = jnp.where(pick, init, got_ref[part, :].astype(F32))
        prev = prev_ref[part, :].astype(F32)
        if prev_pick:
            prev = jnp.where(pick, init, prev)
        guess = a * shift + b * cur_ref[part, :].astype(F32)
        guess_ref[part, :] = (guess + c * prev).astype(BF16)


def either(pick, yes_ref, no_ref, out_ref):
    @pl.when(pick)
    def _():
        out_ref[...] = yes_ref[...]

    @pl.when(jnp.logical_not(pick))
    def _():
        out_ref[...] = no_ref[...]


def bf(*shape):
    return jax.ShapeDtypeStruct(shape, BF16)


def f32(*shape):
    return jax.ShapeDtypeStruct(shape, F32)


def vm(*shape, dtype=BF16):
    return pltpu.VMEM(shape, dtype)


def per_device(
    tokens, init_state, w_query, w_key, w_value, w_out, w_query_state, w_cand_gate, w_state_kv,
    gate_bias, mixing, retrieval,
):
    rows, width = tokens.shape
    states = init_state.shape[0]
    head = width // HEADS
    some = states // PARTS
    tile = min(256, rows)
    tiles = list(range(rows // tile))
    mem = retrieval.shape[1] * BLK
    count = lax.axis_size("seq")
    place = lax.axis_index("seq").astype(jnp.int32).reshape(1)
    work = 2 * rows * width * width

    def step(value, by):
        return lax.ppermute(value, "seq", [(i, i + by) for i in range(count - by)])

    def swap(value, bit):
        return lax.ppermute(value, "seq", [(i, i ^ bit) for i in range(count)])

    def columns_of(ref, p):
        return ref.at[:, p * some : (p + 1) * some]

    def state_rows(env):
        def store(row, value):
            env.state[row : row + value.shape[0], :] = value.astype(BF16)

        return store

    back4 = step(tokens, WIN)

    arguments = dict(
        tok=tokens, wk=w_key, wv=w_value, wqs=w_query_state, init=init_state, wcg=w_cand_gate,
        bias=gate_bias.reshape(1, width), wq=w_query,
    )
    lanes = 128

    def first_body(env):
        copies = {}
        places = dict(tok=env.tok_v, wq=env.wq_v)

        def start(*names):
            for name in names:
                copies[name] = env.copy(env.refs[name], places.get(name, env.refs.get(name + "_s")))

        def wait(*names):
            for name in names:
                copies.pop(name).wait()

        start("tok", "wk")
        start("wv", "wqs", "init")
        wait("tok", "wk")
        start("wcg", "bias", "wq")
        project(env.tok_v, env.wk_s, store_scaled(env.key, None))
        wait("wv", "wqs", "init")
        store = store_values(env.vt, head)

        def store_and_turn(col, value):
            store(col, value)
            part = slice(col, col + value.shape[1])
            env.wqs_t[part, :] = stand(env.wqs_s[:, part])
            env.init_t[part, :] = stand(env.init_s[:, part])

        project(env.tok_v, env.wv_s, store_and_turn)
        wait("wcg", "bias")
        for col in range(0, width, lanes):
            part = slice(col, col + lanes)
            env.bias_t[part, :] = jnp.broadcast_to(env.bias_s[:, part], (lanes, lanes)).T

        def turn_gates(h):
            size = 2 * width // HEADS
            part = slice(h * size, (h + 1) * size)
            env.wcg_t[part, :] = stand(env.wcg_s[:, part])

        update_columns(
            columns_of(env.init_t, 0), env.wqs_t, env.key, env.vt, env.wcg_t, env.bias_t, env.qs, env.o,
            state_rows(env), turn_gates,
        )
        wait(*list(copies))

    k = Kernel("keys_values_update", 2 * work + 4 * work // PARTS)
    k.far.update(arguments)
    k.near_out.update(
        tok_v=bf(rows, width), wq_v=bf(width, width), wqs_t=bf(width, width), init_t=bf(width, states),
        wcg_t=bf(2 * width, width), bias_t=f32(width, lanes), key=bf(rows, width), vt=bf(value_rows(width), rows),
        state=bf(width, some),
    )
    k.scratch.update(
        {n + "_s": vm(*arguments[n].shape, dtype=arguments[n].dtype) for n in ("wk", "wv", "wqs", "init", "wcg", "bias")},
        qs=vm(width, some), o=vm(width, some),
    )
    k.copies = len(arguments)
    k.grant = 16 * 1024 * 1024
    tok_v, wq_v, wqs_t, init_t, wcg_t, bias_t, key, vt, state = k.call(first_body)
    got1 = [step(state, 1)]

    def update_operands(k):
        k.near.update(init=init_t, wqs=wqs_t, wcg=wcg_t, bias=bias_t, key=key, vt=vt)
        k.near_out.update(state=bf(width, some))
        k.scratch.update(qs=vm(width, some), o=vm(width, some))

    def update(env, h_ref, finish_rows):
        update_columns(h_ref, env.wqs, env.key, env.vt, env.wcg, env.bias, env.qs, env.o, finish_rows)

    for p in range(1, PARTS):
        k = Kernel("update_more", 4 * work // PARTS)
        update_operands(k)
        (state,) = k.call(lambda env: update(env, columns_of(env.init, p), state_rows(env)), after=[state])
        got1.append(step(state, 1))
    after = state

    def causal(s, t):
        down = lax.broadcasted_iota(jnp.int32, (tile, tile), 0)
        across = lax.broadcasted_iota(jnp.int32, (tile, tile), 1)
        last = jnp.where(down <= across, s[t * tile :], NEG)
        return last if t == 0 else jnp.concatenate([s[: t * tile], last], axis=0)

    def local(env, t):
        attend(env.q, env.key, env.vt, [t], lambda t: (t + 1) * tile, causal, None, None, {t: env.o}, {t: env.ml})

    def local_outs(k):
        k.near_out.update(o=f32(width, tile), ml=f32(2 * HEADS, tile))

    def query_body(env):
        project(env.tok, env.wq, store_scaled(env.q, score_scale(head)))
        local(env, 0)

    k = Kernel("query_local", 2 * work)
    k.near.update(tok=tok_v, wq=wq_v, key=key, vt=vt)
    k.near_out.update(q=bf(rows, width))
    local_outs(k)
    q, o, ml = k.call(query_body, after=[after])
    after, run_o, run_ml = ml, [o], [ml]

    guesses, got2 = [], []

    def second_body(env, p):
        init = columns_of(env.init, p)
        mixed_guess(env.place[0] == 0, init, env.got, init, init, False, env.mixing, 0, env.guess)
        update(env, env.guess, state_rows(env))

    for p in range(PARTS):
        k = Kernel("update_second", 4 * work // PARTS)
        k.smem.update(place=place, mixing=mixing)
        update_operands(k)
        k.near.update(got=got1[p])
        k.near_out.update(guess=bf(width, some))
        state, guess = k.call(lambda env: second_body(env, p), after=[after])
        after = state
        guesses.append(guess)
        got2.append(step(state, 1))

    def more_body(env, t):
        wskv = env.copy(env.wskv, env.wskv_v) if t == tiles[-1] else None
        local(env, t)
        if wskv is not None:
            either(env.place[0] % WIN < WIN // 2, env.tok, env.back4, env.pair)
            either(env.place[0] % 2 == 0, env.tok, env.back4, env.core)
            wskv.wait()

    for t in tiles[1:]:
        k = Kernel("local_more", work // 8)
        k.smem.update(place=place)
        k.near.update(q=q, key=key, vt=vt)
        local_outs(k)
        if t == tiles[-1]:
            k.near.update(tok=tok_v, back4=back4)
            k.far.update(wskv=w_state_kv)
            k.near_out.update(pair=bf(rows, width), core=bf(rows, width), wskv_v=bf(width, 2 * width))
        o, ml, *more = k.call(lambda env: more_body(env, t), after=[after])
        after = ml
        run_o.append(o)
        run_ml.append(ml)
    pair, core, wskv_v = more
    back2 = swap(pair, WIN // 2)
    beside = swap(core, 1)

    finals, state_parts = [], []

    def third_body(env, p):
        mixed_guess(
            env.place[0] == 0, columns_of(env.init, p), env.got, env.cur, env.before, True, env.mixing, 1, env.guess
        )

        def store(row, value):
            env.state[:, row : row + value.shape[0]] = value.T.astype(BF16)

        update(env, env.guess, store)

    for p in range(PARTS):
        k = Kernel("update_third", 128 * work // PARTS)
        k.smem.update(place=place, mixing=mixing)
        update_operands(k)
        k.near.update(got=got2[p], before=got1[p], cur=guesses[p])
        k.near_out.update(state=bf(some, width), guess=bf(width, some))
        state, guess = k.call(lambda env: third_body(env, p), after=[after])
        after = guess
        finals.append(guess)
        state_parts.append(state)

    def running(k):
        for t in tiles:
            k.near.update({"o%d" % t: run_o[t], "ml%d" % t: run_ml[t]})

    def refs_of(env, name):
        return {t: env.refs["%s%d" % (name, t)] for t in tiles}

    def state_body(env):
        copies = [
            env.copy(env.refs["state%d" % p], env.new_state.at[p * some : (p + 1) * some]) for p in range(PARTS)
        ]
        copies += [env.copy(env.refs[n], env.refs[n + "_v"]) for n in ("wk", "wv", "wout")]
        for p in range(PARTS):
            for col in range(0, width, tile):
                part = slice(col, col + tile)
                env.guess[p * some : (p + 1) * some, part] = stand(env.refs["guess%d" % p][part, :])
        project(env.guess, env.wskv.at[:, :width], store_scaled(env.skey, None))
        project(env.guess, env.wskv.at[:, width:], store_values(env.svt, head))
        attend(
            env.q, env.skey, env.svt, tiles, lambda t: states, lambda s, t: s,
            refs_of(env, "o"), refs_of(env, "ml"), refs_of(env, "new_o"), refs_of(env, "new_ml"),
        )
        for copy in copies:
            copy.wait()

    k = Kernel("state_keys", 128 * work)
    k.near.update(wskv=wskv_v, q=q)
    k.near.update({"guess%d" % p: finals[p] for p in range(PARTS)})
    k.near.update({"state%d" % p: state_parts[p] for p in range(PARTS)})
    k.far.update(wk=w_key, wv=w_value, wout=w_out)
    running(k)
    for t in tiles:
        k.near_out.update({"new_o%d" % t: f32(width, tile), "new_ml%d" % t: f32(2 * HEADS, tile)})
    k.near_out.update({n: bf(width, width) for n in ("wk_v", "wv_v", "wout_v")})
    k.far_out.update(new_state=bf(states, width))
    k.scratch.update(skey=vm(states, width), svt=vm(value_rows(width), states), guess=vm(states, width))
    k.copies = PARTS + 3
    k.grant = 8 * 1024 * 1024
    *pairs, wk_v, wv_v, wout_v, new_state = k.call(state_body)
    run_o, run_ml = pairs[0::2], pairs[1::2]

    k = Kernel("pass_on", 1)
    k.near.update(back2=back2)
    k.near_out.update(out=bf(rows, width))
    k.aliases.update(back2="out")
    (back2,) = k.call(lambda env: None, after=[run_ml[0]])
    last = swap(back2, 1)

    def last_body(env):
        even = env.place[0] % 2 == 0
        lift = []
        for e in range(mem // BLK):
            entry = env.retrieval[0, e]
            distance = entry // MBLK + 1
            start = pl.multiple_of((entry % MBLK) * BLK, BLK)
            from_last = ((distance == 1) & even) | ((distance == 3) & jnp.logical_not(even))
            from_beside = ((distance == 3) & even) | ((distance == 1) & jnp.logical_not(even))
            for pick, source in (
                (from_last, env.last), (from_beside, env.beside), (distance == 2, env.back2), (distance == 4, env.back4)
            ):

                @pl.when(pick)
                def _(source=source, start=start, e=e):
                    env.mem[e * BLK : (e + 1) * BLK, :] = source[pl.ds(start, BLK), :]

            lift.append(jnp.where(distance > env.place[0], NEG, 0.0))
        project(env.mem, env.wk, store_scaled(env.key, None))
        project(env.mem, env.wv, store_values(env.vt, head))

        def mask(s, t):
            return jnp.concatenate([s[e * BLK : (e + 1) * BLK] + lift[e] for e in range(mem // BLK)], axis=0)

        new_o, new_ml = refs_of(env, "new_o"), refs_of(env, "new_ml")
        attend(env.q, env.key, env.vt, tiles, lambda t: mem, mask, refs_of(env, "o"), refs_of(env, "ml"), new_o, new_ml)
        for t in tiles:
            for h in range(HEADS):
                part = slice(h * head, (h + 1) * head)
                o = new_o[t][part, :] * (1.0 / new_ml[t][HEADS + h : HEADS + h + 1, :])
                env.on[t * tile : (t + 1) * tile, part] = o.T.astype(BF16)
        copies = []

        def store(col, value):
            part = slice(col, col + value.shape[1])
            env.sum[:, part] = (env.tok[:, part].astype(F32) + value).astype(BF16)
            copies.append(env.copy(env.sum.at[:, part], env.mixed.at[:, part]))

        project(env.on, env.wout, store)
        for copy in copies:
            copy.wait()

    k = Kernel("memory_out", 5 * work)
    k.smem.update(place=place, retrieval=retrieval)
    k.near.update(wk=wk_v, wv=wv_v, wout=wout_v, tok=tok_v, q=q, last=last, beside=beside, back2=back2, back4=back4)
    running(k)
    k.scratch.update(
        mem=vm(mem, width), key=vm(mem, width), vt=vm(value_rows(width), mem), on=vm(rows, width), sum=vm(rows, width)
    )
    for t in tiles:
        k.scratch.update({"new_o%d" % t: vm(width, tile, dtype=F32), "new_ml%d" % t: vm(2 * HEADS, tile, dtype=F32)})
    k.far_out.update(mixed=bf(rows, width))
    k.copies = width // 256
    k.grant = 10 * 1024 * 1024
    (mixed,) = k.call(last_body)
    return mixed, new_state


def solution(mesh):
    return jax.shard_map(
        per_device,
        mesh=mesh,
        in_specs=(P("seq", None), P(), P(), P(), P(), P(), P(), P(), P(), P(), P(), P("seq", None)),
        out_specs=(P("seq", None), P("seq", None)),
        check_vma=False,
    )
```

```python
import math

import jax
import jax.numpy as jnp
from jax import lax
from jax.experimental import pallas as pl
from jax.experimental.pallas import tpu as pltpu
from jax.sharding import PartitionSpec as P

HEADS = 8
BLK = 64
MBLK = 8
WIN = 4
PARTS = 2
ONES = 16
NEG = -1e30
VMEM_LIMIT = 6 * 1024 * 1024

BF16 = jnp.bfloat16
F32 = jnp.float32


def dot(a, b):
    return jnp.dot(a, b, preferred_element_type=F32)


def dot_t(a, b):
    return lax.dot_general(a, b, (((1,), (1,)), ((), ())), preferred_element_type=F32)


class Kernel:
    def __init__(self, name, flops):
        self.name, self.flops = name, flops
        self.smem, self.near, self.far = {}, {}, {}
        self.near_out, self.far_out, self.scratch = {}, {}, {}
        self.aliases = {}
        self.copies = 1
        self.grant = VMEM_LIMIT

    def call(self, body, after=()):
        smem, near, far = list(self.smem), list(self.near), list(self.far)
        near_out, far_out, scratch = list(self.near_out), list(self.far_out), list(self.scratch)
        arrays = [self.smem[n] for n in smem]
        arrays += [pltpu.with_memory_space_constraint(self.near[n], pltpu.VMEM) for n in near]
        arrays += [pltpu.with_memory_space_constraint(self.far[n], pltpu.HBM) for n in far]
        arrays += [pltpu.with_memory_space_constraint(a, pltpu.VMEM) for a in after]
        memory = [pltpu.SMEM] * len(smem) + [pltpu.VMEM] * len(near) + [pltpu.HBM] * len(far) + [pltpu.VMEM] * len(after)
        outs = [pltpu.VMEM(self.near_out[n].shape, self.near_out[n].dtype) for n in near_out]
        outs += [pltpu.HBM(self.far_out[n].shape, self.far_out[n].dtype) for n in far_out]
        out_memory = [pltpu.VMEM] * len(near_out) + [pltpu.HBM] * len(far_out)
        names = smem + near + far
        out_names = near_out + far_out

        def kernel(*refs):
            env = Env()
            env.refs = dict(zip(names, refs))
            env.refs.update(zip(out_names, refs[len(arrays) :]))
            env.refs.update(zip(scratch, refs[len(arrays) + len(outs) :]))
            env.sems, env.started = refs[-1], 0
            body(env)

        return pl.pallas_call(
            kernel,
            out_shape=outs,
            in_specs=[pl.BlockSpec(memory_space=m) for m in memory],
            out_specs=[pl.BlockSpec(memory_space=m) for m in out_memory],
            scratch_shapes=[self.scratch[n] for n in scratch] + [pltpu.SemaphoreType.DMA((self.copies,))],
            input_output_aliases={names.index(a): out_names.index(b) for a, b in self.aliases.items()},
            compiler_params=pltpu.CompilerParams(vmem_limit_bytes=self.grant),
            cost_estimate=pl.CostEstimate(flops=self.flops, bytes_accessed=1 << 10, transcendentals=0),
            name=self.name,
        )(*arrays)


class Env:
    def __getattr__(self, name):
        return self.refs[name]

    def copy(self, src, dst):
        copy = pltpu.make_async_copy(src, dst, self.sems.at[self.started])
        self.started += 1
        copy.start()
        return copy


def project(x_ref, w_ref, store, tile=256):
    for col in range(0, w_ref.shape[1], tile):
        store(col, dot(x_ref[...], w_ref[:, col : col + tile]))


def store_scaled(out_ref, scale):
    def store(col, value):
        if scale is not None:
            value = value * scale
        out_ref[:, col : col + value.shape[1]] = value.astype(BF16)

    return store


def score_scale(head):
    return math.log2(math.e) / math.sqrt(head)


def value_rows(width):
    return width + HEADS * ONES


def store_values(vt_ref, head):
    keys = vt_ref.shape[1]
    pitch = head + ONES

    def store(col, value):
        for part in range(0, value.shape[1], head):
            at = (col + part) // head * pitch
            vt_ref[at : at + head, :] = value[:, part : part + head].T.astype(BF16)
            vt_ref[at + head : at + pitch, :] = jnp.ones((ONES, keys), BF16)

    return store


def in_turn(units, scores, finish):
    ahead = scores(*units[0])
    for number, unit in enumerate(units):
        now = ahead
        if number + 1 < len(units):
            ahead = scores(*units[number + 1])
        finish(*unit, now)


def stand(value):
    return value.T


def update_columns(h_ref, wqs_ref, key_ref, vt_ref, wcg_ref, bias_ref, qs_ref, o_ref, z_ref, finish_rows, beside=None, ready=None):
    width, some = h_ref.shape
    head = width // HEADS
    pitch = head + ONES
    scale = score_scale(head)
    qs_ref[...] = (dot(wqs_ref[...], h_ref[...]) * scale).astype(BF16)

    def scores(h):
        part = slice(h * head, (h + 1) * head)
        return dot(key_ref[:, part], qs_ref[part, :])

    def finish(h, s):
        if beside is not None:
            beside(h)
        p = jnp.exp2(s - jnp.max(s, axis=0, keepdims=True)).astype(BF16)
        ol = dot(vt_ref[h * pitch : (h + 1) * pitch, :], p)
        o_ref[h * head : (h + 1) * head, :] = (ol[:head] * (1.0 / ol[head : head + 1])).astype(BF16)

    in_turn([(h,) for h in range(HEADS)], scores, finish)
    if ready is not None:
        ready()
    z_ref[...] = dot(wcg_ref[...], o_ref[...])
    tall = min(128, width)
    for row in range(0, width, tall):
        part = slice(row, row + tall)
        zc = z_ref[part, :]
        zg = z_ref[width + row : width + row + tall, :]
        lanes = bias_ref.shape[1]
        bias = jnp.concatenate([bias_ref[part, :]] * (some // lanes), axis=1)
        cand = jnp.tanh(zc)
        forget = 0.5 * jnp.tanh(0.5 * (zg + bias)) + 0.5
        finish_rows(row, forget * h_ref[part, :].astype(F32) + (1.0 - forget) * cand)


def attend(q_ref, key_ref, vt_ref, places, limit, mask, old_o, old_ml, new_o, new_ml):
    head = q_ref.shape[1] // HEADS
    pitch = head + ONES
    tile = new_o[places[0]].shape[1]

    def scores(h, t):
        part = slice(h * head, (h + 1) * head)
        return dot_t(key_ref[: limit(t), part], q_ref[t * tile : (t + 1) * tile, part])

    def finish(h, t, s):
        part = slice(h * head, (h + 1) * head)
        top_row, sum_row = slice(h, h + 1), slice(HEADS + h, HEADS + h + 1)
        s = mask(s, t)
        top = jnp.max(s, axis=0, keepdims=True)
        if old_o is not None:
            old = old_ml[t][top_row, :]
            top = jnp.maximum(top, old)
        p = jnp.exp2(s - top).astype(BF16)
        ol = dot(vt_ref[h * pitch : (h + 1) * pitch, : limit(t)], p)
        o, l = ol[:head], ol[head : head + 1]
        if old_o is not None:
            keep = jnp.exp2(old - top)
            o = o + keep * old_o[t][part, :]
            l = l + keep * old_ml[t][sum_row, :]
        new_o[t][part, :] = o
        new_ml[t][top_row, :] = top
        new_ml[t][sum_row, :] = l

    in_turn([(h, t) for h in range(HEADS) for t in places], scores, finish)


def mixed_guess(pick, init_ref, got_ref, cur_ref, prev_ref, prev_pick, mixing, sweep, guess_ref):
    a, b, c = mixing[sweep, 0], mixing[sweep, 1], mixing[sweep, 2]
    rows = guess_ref.shape[0]
    step = min(64, rows)
    for r in range(0, rows, step):
        part = slice(r, r + step)
        init = init_ref[part, :].astype(F32)
        shift = jnp.where(pick, init, got_ref[part, :].astype(F32))
        prev = prev_ref[part, :].astype(F32)
        if prev_pick:
            prev = jnp.where(pick, init, prev)
        guess = a * shift + b * cur_ref[part, :].astype(F32)
        guess_ref[part, :] = (guess + c * prev).astype(BF16)


def either(pick, yes_ref, no_ref, out_ref):
    @pl.when(pick)
    def _():
        out_ref[...] = yes_ref[...]

    @pl.when(jnp.logical_not(pick))
    def _():
        out_ref[...] = no_ref[...]


def bf(*shape):
    return jax.ShapeDtypeStruct(shape, BF16)


def f32(*shape):
    return jax.ShapeDtypeStruct(shape, F32)


def vm(*shape, dtype=BF16):
    return pltpu.VMEM(shape, dtype)


def per_device(
    tokens, init_state, w_query, w_key, w_value, w_out, w_query_state, w_cand_gate, w_state_kv,
    gate_bias, mixing, retrieval,
):
    rows, width = tokens.shape
    states = init_state.shape[0]
    head = width // HEADS
    some = states // PARTS
    tile = min(256, rows)
    tiles = list(range(rows // tile))
    mem = retrieval.shape[1] * BLK
    count = lax.axis_size("seq")
    place = lax.axis_index("seq").astype(jnp.int32).reshape(1)
    work = 2 * rows * width * width

    def step(value, by):
        return lax.ppermute(value, "seq", [(i, i + by) for i in range(count - by)])

    def swap(value, bit):
        return lax.ppermute(value, "seq", [(i, i ^ bit) for i in range(count)])

    def columns_of(ref, p):
        return ref.at[:, p * some : (p + 1) * some]

    def state_rows(env):
        def store(row, value):
            env.state[row : row + value.shape[0], :] = value.astype(BF16)

        return store

    back4 = step(tokens, WIN)

    arguments = dict(
        tok=tokens, wk=w_key, wv=w_value, wqs=w_query_state, init=init_state, wcg=w_cand_gate,
        bias=gate_bias.reshape(1, width),
    )
    lanes = 128

    def first_body(env):
        copies = {}

        def start(*names):
            for name in names:
                copies[name] = env.copy(env.refs[name], env.refs[name + "_s"])

        def wait(*names):
            for name in names:
                copies.pop(name).wait()

        start("tok", "wk")
        start("wv", "wqs", "init")
        wait("tok", "wk")
        start("wcg", "bias")
        project(env.tok_s, env.wk_s, store_scaled(env.key, None))
        wait("wv", "wqs", "init")
        store = store_values(env.vt, head)

        def store_and_turn(col, value):
            store(col, value)
            part = slice(col, col + value.shape[1])
            env.wqs_t[part, :] = stand(env.wqs_s[:, part])
            env.init_t[part, :] = stand(env.init_s[:, part])

        project(env.tok_s, env.wv_s, store_and_turn)
        wait("wcg", "bias")
        for col in range(0, width, lanes):
            part = slice(col, col + lanes)
            env.bias_t[part, :] = jnp.broadcast_to(env.bias_s[:, part], (lanes, lanes)).T

        def turn_gates(h):
            size = 2 * width // HEADS
            part = slice(h * size, (h + 1) * size)
            env.wcg_h[part, :] = stand(env.wcg_s[:, part])
            outs.append(env.copy(env.wcg_h.at[part, :], env.wcg_t.at[part, :]))

        outs = []

        update_columns(
            columns_of(env.init_t, 0), env.wqs_t, env.key, env.vt, env.wcg_h, env.bias_t, env.qs, env.o,
            env.z, state_rows(env), turn_gates,
        )
        wait(*list(copies))
        for copy in outs:
            copy.wait()

    k = Kernel("keys_values_update", 2 * work + 4 * work // PARTS)
    k.far.update(arguments)
    k.near_out.update(
        wqs_t=bf(width, width), init_t=bf(width, states), bias_t=f32(width, lanes), key=bf(rows, width), vt=bf(value_rows(width), rows),
        state=bf(width, some),
    )
    k.scratch.update(
        {n + "_s": vm(*arguments[n].shape, dtype=arguments[n].dtype) for n in arguments},
        qs=vm(width, some), o=vm(width, some), z=vm(2 * width, some, dtype=F32), wcg_h=vm(2 * width, width),
    )
    k.far_out.update(wcg_t=bf(2 * width, width))
    k.copies = len(arguments) + HEADS
    k.grant = 24 * 1024 * 1024
    wqs_t, init_t, bias_t, key, vt, state, wcg_t = k.call(first_body)
    got1 = [step(state, 1)]

    def update_operands(k):
        k.near.update(init=init_t, wqs=wqs_t, bias=bias_t, key=key, vt=vt)
        k.far.update(wcg=wcg_t)
        k.near_out.update(state=bf(width, some))
        k.scratch.update(
            qs=vm(width, some), o=vm(width, some), z=vm(2 * width, some, dtype=F32), gates=vm(2 * width, width)
        )
        k.copies = 2
        k.grant = 12 * 1024 * 1024

    def update(env, h_ref, finish_rows, gates):
        update_columns(
            h_ref, env.wqs, env.key, env.vt, env.gates, env.bias, env.qs, env.o, env.z, finish_rows, None, gates.wait
        )

    for p in range(1, PARTS):
        k = Kernel("update_more", work // 32)
        update_operands(k)

        def more_states(env, p=p):
            update(env, columns_of(env.init, p), state_rows(env), env.copy(env.wcg, env.gates))

        (state,) = k.call(more_states, after=[state])
        got1.append(step(state, 1))
    after = state

    def causal(s, t):
        down = lax.broadcasted_iota(jnp.int32, (tile, tile), 0)
        across = lax.broadcasted_iota(jnp.int32, (tile, tile), 1)
        last = jnp.where(down <= across, s[t * tile :], NEG)
        return last if t == 0 else jnp.concatenate([s[: t * tile], last], axis=0)

    def local(env, t):
        attend(env.q, env.key, env.vt, [t], lambda t: (t + 1) * tile, causal, None, None, {t: env.o}, {t: env.ml})

    def local_outs(k):
        k.near_out.update(o=f32(width, tile), ml=f32(2 * HEADS, tile))

    def query_body(env):
        for copy in [env.copy(env.tok_h, env.tok), env.copy(env.wq_h, env.wq)]:
            copy.wait()
        project(env.tok, env.wq, store_scaled(env.q, score_scale(head)))
        local(env, 0)

    k = Kernel("query_local", work // 32)
    k.near.update(key=key, vt=vt)
    k.far.update(tok_h=tokens, wq_h=w_query)
    k.scratch.update(tok=vm(rows, width), wq=vm(width, width))
    k.copies = 2
    k.near_out.update(q=bf(rows, width))
    local_outs(k)
    q, o, ml = k.call(query_body, after=[after])
    after, run_o, run_ml = ml, [o], [ml]

    guesses, got2 = [], []

    def second_body(env, p):
        gates = env.copy(env.wcg, env.gates)
        init = columns_of(env.init, p)
        mixed_guess(env.place[0] == 0, init, env.got, init, init, False, env.mixing, 0, env.guess)
        update(env, env.guess, state_rows(env), gates)

    for p in range(PARTS):
        k = Kernel("update_second", work // 32)
        k.smem.update(place=place, mixing=mixing)
        update_operands(k)
        k.near.update(got=got1[p])
        k.near_out.update(guess=bf(width, some))
        state, guess = k.call(lambda env: second_body(env, p), after=[after])
        after = state
        guesses.append(guess)
        got2.append(step(state, 1))

    def more_body(env, t):
        late = t == tiles[-1]
        tok = env.copy(env.tok_h, env.tok) if late else None
        local(env, t)
        if late:
            tok.wait()
            either(env.place[0] % WIN < WIN // 2, env.tok, env.back4, env.pair)
            either(env.place[0] % 2 == 0, env.tok, env.back4, env.core)

    for t in tiles[1:]:
        k = Kernel("local_more", work // 32)
        k.smem.update(place=place)
        k.near.update(q=q, key=key, vt=vt)
        local_outs(k)
        if t == tiles[-1]:
            k.near.update(back4=back4)
            k.far.update(tok_h=tokens)
            k.scratch.update(tok=vm(rows, width))
            k.near_out.update(pair=bf(rows, width), core=bf(rows, width))
        o, ml, *more = k.call(lambda env: more_body(env, t), after=[after])
        after = ml
        run_o.append(o)
        run_ml.append(ml)
    pair, core = more
    back2 = swap(pair, WIN // 2)
    beside = swap(core, 1)

    finals, state_parts = [], []

    def third_body(env, p):
        gates = env.copy(env.wcg, env.gates)
        wskv = env.copy(env.wskv, env.wskv_v) if p == PARTS - 1 else None
        mixed_guess(
            env.place[0] == 0, columns_of(env.init, p), env.got, env.cur, env.before, True, env.mixing, 1, env.guess
        )

        def store(row, value):
            env.state[:, row : row + value.shape[0]] = value.T.astype(BF16)

        update(env, env.guess, store, gates)
        if wskv is not None:
            wskv.wait()

    for p in range(PARTS):
        k = Kernel("update_third", 32 * work // PARTS)
        k.smem.update(place=place, mixing=mixing)
        update_operands(k)
        k.near.update(got=got2[p], before=got1[p], cur=guesses[p])
        k.near_out.update(state=bf(some, width), guess=bf(width, some))
        if p == PARTS - 1:
            k.far.update(wskv=w_state_kv)
            k.near_out.update(wskv_v=bf(width, 2 * width))
        state, guess, *wskv_v = k.call(lambda env: third_body(env, p), after=[after])
        after = guess
        finals.append(guess)
        state_parts.append(state)

    def running(k):
        for t in tiles:
            k.near.update({"o%d" % t: run_o[t], "ml%d" % t: run_ml[t]})

    def refs_of(env, name):
        return {t: env.refs["%s%d" % (name, t)] for t in tiles}

    def state_body(env):
        copies = [
            env.copy(env.refs["state%d" % p], env.new_state.at[p * some : (p + 1) * some]) for p in range(PARTS)
        ]
        copies += [env.copy(env.refs[n], env.refs[n + "_v"]) for n in ("wk", "wv")]
        for p in range(PARTS):
            for col in range(0, width, tile):
                part = slice(col, col + tile)
                env.guess[p * some : (p + 1) * some, part] = stand(env.refs["guess%d" % p][part, :])
        project(env.guess, env.wskv.at[:, :width], store_scaled(env.skey, None))
        project(env.guess, env.wskv.at[:, width:], store_values(env.svt, head))
        attend(
            env.q, env.skey, env.svt, tiles, lambda t: states, lambda s, t: s,
            refs_of(env, "o"), refs_of(env, "ml"), refs_of(env, "new_o"), refs_of(env, "new_ml"),
        )
        for copy in copies:
            copy.wait()

    k = Kernel("state_keys", 32 * work)
    k.near.update(wskv=wskv_v[0], q=q)
    k.near.update({"guess%d" % p: finals[p] for p in range(PARTS)})
    k.near.update({"state%d" % p: state_parts[p] for p in range(PARTS)})
    k.far.update(wk=w_key, wv=w_value)
    running(k)
    for t in tiles:
        k.near_out.update({"new_o%d" % t: f32(width, tile), "new_ml%d" % t: f32(2 * HEADS, tile)})
    k.near_out.update({n: bf(width, width) for n in ("wk_v", "wv_v")})
    k.far_out.update(new_state=bf(states, width))
    k.scratch.update(skey=vm(states, width), svt=vm(value_rows(width), states), guess=vm(states, width))
    k.copies = PARTS + 2
    k.grant = 8 * 1024 * 1024
    *pairs, wk_v, wv_v, new_state = k.call(state_body)
    run_o, run_ml = pairs[0::2], pairs[1::2]

    k = Kernel("pass_on", 1)
    k.near.update(back2=back2)
    k.near_out.update(out=bf(rows, width))
    k.aliases.update(back2="out")
    (back2,) = k.call(lambda env: None, after=[run_ml[0]])
    last = swap(back2, 1)

    def last_body(env):
        late = [env.copy(env.tok_h, env.tok), env.copy(env.wout_h, env.wout)]
        even = env.place[0] % 2 == 0
        lift = []
        for e in range(mem // BLK):
            entry = env.retrieval[0, e]
            distance = entry // MBLK + 1
            start = pl.multiple_of((entry % MBLK) * BLK, BLK)
            from_last = ((distance == 1) & even) | ((distance == 3) & jnp.logical_not(even))
            from_beside = ((distance == 3) & even) | ((distance == 1) & jnp.logical_not(even))
            for pick, source in (
                (from_last, env.last), (from_beside, env.beside), (distance == 2, env.back2), (distance == 4, env.back4)
            ):

                @pl.when(pick)
                def _(source=source, start=start, e=e):
                    env.mem[e * BLK : (e + 1) * BLK, :] = source[pl.ds(start, BLK), :]

            lift.append(jnp.where(distance > env.place[0], NEG, 0.0))
        project(env.mem, env.wk, store_scaled(env.key, None))
        project(env.mem, env.wv, store_values(env.vt, head))

        def mask(s, t):
            return jnp.concatenate([s[e * BLK : (e + 1) * BLK] + lift[e] for e in range(mem // BLK)], axis=0)

        new_o, new_ml = refs_of(env, "new_o"), refs_of(env, "new_ml")
        attend(env.q, env.key, env.vt, tiles, lambda t: mem, mask, refs_of(env, "o"), refs_of(env, "ml"), new_o, new_ml)
        for t in tiles:
            for h in range(HEADS):
                part = slice(h * head, (h + 1) * head)
                o = new_o[t][part, :] * (1.0 / new_ml[t][HEADS + h : HEADS + h + 1, :])
                env.on[t * tile : (t + 1) * tile, part] = o.T.astype(BF16)
        copies = []
        for copy in late:
            copy.wait()

        def store(col, value):
            part = slice(col, col + value.shape[1])
            env.sum[:, part] = (env.tok[:, part].astype(F32) + value).astype(BF16)
            copies.append(env.copy(env.sum.at[:, part], env.mixed.at[:, part]))

        project(env.on, env.wout, store)
        for copy in copies:
            copy.wait()

    k = Kernel("memory_out", 5 * work)
    k.smem.update(place=place, retrieval=retrieval)
    k.far.update(tok_h=tokens, wout_h=w_out)
    k.scratch.update(tok=vm(rows, width), wout=vm(width, width))
    k.near.update(wk=wk_v, wv=wv_v, q=q, last=last, beside=beside, back2=back2, back4=back4)
    running(k)
    k.scratch.update(
        mem=vm(mem, width), key=vm(mem, width), vt=vm(value_rows(width), mem), on=vm(rows, width), sum=vm(rows, width)
    )
    for t in tiles:
        k.scratch.update({"new_o%d" % t: vm(width, tile, dtype=F32), "new_ml%d" % t: vm(2 * HEADS, tile, dtype=F32)})
    k.far_out.update(mixed=bf(rows, width))
    k.copies = width // 256 + 2
    k.grant = 14 * 1024 * 1024
    (mixed,) = k.call(last_body)
    return mixed, new_state


def solution(mesh):
    return jax.shard_map(
        per_device,
        mesh=mesh,
        in_specs=(P("seq", None), P(), P(), P(), P(), P(), P(), P(), P(), P(), P(), P("seq", None)),
        out_specs=(P("seq", None), P("seq", None)),
        check_vma=False,
    )
```

```python
import math

import jax
import jax.numpy as jnp
from jax import lax
from jax.experimental import pallas as pl
from jax.experimental.pallas import tpu as pltpu
from jax.sharding import PartitionSpec as P

HEADS = 8
BLK = 64
MBLK = 8
WIN = 4
PARTS = 2
ONES = 16
NEG = -1e30
VMEM_LIMIT = 6 * 1024 * 1024

BF16 = jnp.bfloat16
F32 = jnp.float32


def dot(a, b):
    return jnp.dot(a, b, preferred_element_type=F32)


def dot_t(a, b):
    return lax.dot_general(a, b, (((1,), (1,)), ((), ())), preferred_element_type=F32)


class Kernel:
    def __init__(self, name, flops):
        self.name, self.flops = name, flops
        self.smem, self.near, self.far = {}, {}, {}
        self.near_out, self.far_out, self.scratch = {}, {}, {}
        self.aliases = {}
        self.copies = 1
        self.grant = VMEM_LIMIT

    def call(self, body, after=()):
        smem, near, far = list(self.smem), list(self.near), list(self.far)
        near_out, far_out, scratch = list(self.near_out), list(self.far_out), list(self.scratch)
        arrays = [self.smem[n] for n in smem]
        arrays += [pltpu.with_memory_space_constraint(self.near[n], pltpu.VMEM) for n in near]
        arrays += [pltpu.with_memory_space_constraint(self.far[n], pltpu.HBM) for n in far]
        arrays += [pltpu.with_memory_space_constraint(a, pltpu.VMEM) for a in after]
        memory = [pltpu.SMEM] * len(smem) + [pltpu.VMEM] * len(near) + [pltpu.HBM] * len(far) + [pltpu.VMEM] * len(after)
        outs = [pltpu.VMEM(self.near_out[n].shape, self.near_out[n].dtype) for n in near_out]
        outs += [pltpu.HBM(self.far_out[n].shape, self.far_out[n].dtype) for n in far_out]
        out_memory = [pltpu.VMEM] * len(near_out) + [pltpu.HBM] * len(far_out)
        names = smem + near + far
        out_names = near_out + far_out

        def kernel(*refs):
            env = Env()
            env.refs = dict(zip(names, refs))
            env.refs.update(zip(out_names, refs[len(arrays) :]))
            env.refs.update(zip(scratch, refs[len(arrays) + len(outs) :]))
            env.sems, env.started = refs[-1], 0
            body(env)

        return pl.pallas_call(
            kernel,
            out_shape=outs,
            in_specs=[pl.BlockSpec(memory_space=m) for m in memory],
            out_specs=[pl.BlockSpec(memory_space=m) for m in out_memory],
            scratch_shapes=[self.scratch[n] for n in scratch] + [pltpu.SemaphoreType.DMA((self.copies,))],
            input_output_aliases={names.index(a): out_names.index(b) for a, b in self.aliases.items()},
            compiler_params=pltpu.CompilerParams(vmem_limit_bytes=self.grant),
            cost_estimate=pl.CostEstimate(flops=self.flops, bytes_accessed=1 << 10, transcendentals=0),
            name=self.name,
        )(*arrays)


class Env:
    def __getattr__(self, name):
        return self.refs[name]

    def copy(self, src, dst):
        copy = pltpu.make_async_copy(src, dst, self.sems.at[self.started])
        self.started += 1
        copy.start()
        return copy


def span(index, size):
    return pl.ds(pl.multiple_of(index * size, size), size)


def loop(count, body, unroll=1):
    lax.fori_loop(0, count // unroll, lambda i, _: [body([i * unroll + u for u in range(unroll)]), 0][1], 0)


def project(x_ref, w_ref, store, tile=256):
    def body(numbers):
        for n in numbers:
            store(n, dot(x_ref[...], w_ref[:, span(n, tile)]))

    loop(w_ref.shape[1] // tile, body)


def store_scaled(out_ref, scale):
    def store(number, value):
        if scale is not None:
            value = value * scale
        out_ref[:, span(number, value.shape[1])] = value.astype(BF16)

    return store


def score_scale(head):
    return math.log2(math.e) / math.sqrt(head)


def value_rows(width):
    return width + HEADS * ONES


def store_values(vt_ref, head):
    keys = vt_ref.shape[1]
    pitch = head + ONES

    def store(number, value):
        each = value.shape[1] // head
        tall = jnp.concatenate(
            sum([[value[:, u * head : (u + 1) * head].T.astype(BF16), jnp.ones((ONES, keys), BF16)] for u in range(each)], []),
            axis=0,
        )
        vt_ref[span(number, each * pitch), :] = tall

    return store


def stand(value):
    return value.T


def in_turn(count, scores, finish, unroll):
    def body(heads):
        values = [scores(h) for h in heads]
        for h, value in zip(heads, values):
            finish(h, value)

    loop(count, body, unroll)


def update_columns(
    h_ref, wqs_ref, key_ref, vt_ref, wcg_ref, bias_ref, qs_ref, o_ref, finish_rows, beside=None, ready=None
):
    width, some = h_ref.shape
    head = width // HEADS
    pitch = head + ONES
    scale = score_scale(head)
    tall = min(256, width)

    def queries(numbers):
        for n in numbers:
            qs_ref[span(n, tall), :] = (dot(wqs_ref[span(n, tall), :], h_ref[...]) * scale).astype(BF16)

    loop(width // tall, queries)

    def scores(h):
        return dot(key_ref[:, span(h, head)], qs_ref[span(h, head), :])

    def finish(h, s):
        if beside is not None:
            beside(h)
        p = jnp.exp2(s - jnp.max(s, axis=0, keepdims=True)).astype(BF16)
        ol = dot(vt_ref[span(h, pitch), :], p)
        o_ref[span(h, head), :] = (ol[:head] * (1.0 / ol[head : head + 1])).astype(BF16)

    in_turn(HEADS, scores, finish, 2)
    if ready is not None:
        ready()
    lanes = bias_ref.shape[1]

    def gate(numbers):
        for n in numbers:
            zc = dot(wcg_ref[span(n, tall), :], o_ref[...])
            zg = dot(wcg_ref[span(n + width // tall, tall), :], o_ref[...])
            bias = jnp.concatenate([bias_ref[span(n, tall), :]] * (some // lanes), axis=1)
            cand = jnp.tanh(zc)
            forget = 0.5 * jnp.tanh(0.5 * (zg + bias)) + 0.5
            finish_rows(n, forget * h_ref[span(n, tall), :].astype(F32) + (1.0 - forget) * cand)

    loop(width // tall, gate)


def attend(q_ref, key_ref, vt_ref, places, limit, mask, old_o, old_ml, new_o, new_ml):
    head = q_ref.shape[1] // HEADS
    pitch = head + ONES
    tile = new_o[places[0]].shape[1]

    def scores(h):
        return [
            dot_t(key_ref[: limit(t), span(h, head)], q_ref[t * tile : (t + 1) * tile, span(h, head)]) for t in places
        ]

    def finish(h, all_s):
        for t, s in zip(places, all_s):
            s = mask(s, t)
            top = jnp.max(s, axis=0, keepdims=True)
            if old_o is not None:
                old = old_ml[t][h][:1]
                top = jnp.maximum(top, old)
            p = jnp.exp2(s - top).astype(BF16)
            ol = dot(vt_ref[span(h, pitch), : limit(t)], p)
            o, l = ol[:head], ol[head : head + 1]
            if old_o is not None:
                keep = jnp.exp2(old - top)
                o = o + keep * old_o[t][span(h, head), :]
                l = l + keep * old_ml[t][HEADS + h][:1]
            new_o[t][span(h, head), :] = o
            new_ml[t][h] = jnp.broadcast_to(top, (8, tile))
            new_ml[t][HEADS + h] = jnp.broadcast_to(l, (8, tile))

    in_turn(HEADS, scores, finish, 2 if len(places) == 1 else 1)


def mixed_guess(pick, init_ref, got_ref, cur_ref, prev_ref, prev_pick, mixing, sweep, guess_ref):
    a, b, c = mixing[sweep, 0], mixing[sweep, 1], mixing[sweep, 2]
    rows = guess_ref.shape[0]
    step = min(128, rows)

    def body(numbers):
        part = span(numbers[0], step)
        init = init_ref[part, :].astype(F32)
        shift = jnp.where(pick, init, got_ref[part, :].astype(F32))
        prev = prev_ref[part, :].astype(F32)
        if prev_pick:
            prev = jnp.where(pick, init, prev)
        guess = a * shift + b * cur_ref[part, :].astype(F32)
        guess_ref[part, :] = (guess + c * prev).astype(BF16)

    loop(rows // step, body)


def either(pick, yes_ref, no_ref, out_ref):
    @pl.when(pick)
    def _():
        out_ref[...] = yes_ref[...]

    @pl.when(jnp.logical_not(pick))
    def _():
        out_ref[...] = no_ref[...]


def bf(*shape):
    return jax.ShapeDtypeStruct(shape, BF16)


def f32(*shape):
    return jax.ShapeDtypeStruct(shape, F32)


def vm(*shape, dtype=BF16):
    return pltpu.VMEM(shape, dtype)


def per_device(
    tokens, init_state, w_query, w_key, w_value, w_out, w_query_state, w_cand_gate, w_state_kv,
    gate_bias, mixing, retrieval,
):
    rows, width = tokens.shape
    states = init_state.shape[0]
    head = width // HEADS
    some = states // PARTS
    tile = min(256, rows)
    tiles = list(range(rows // tile))
    mem = retrieval.shape[1] * BLK
    count = lax.axis_size("seq")
    place = lax.axis_index("seq").astype(jnp.int32).reshape(1)
    work = 2 * rows * width * width

    def step(value, by):
        return lax.ppermute(value, "seq", [(i, i + by) for i in range(count - by)])

    def swap(value, bit):
        return lax.ppermute(value, "seq", [(i, i ^ bit) for i in range(count)])

    def columns_of(ref, p):
        return ref.at[:, p * some : (p + 1) * some]

    def state_rows(env):
        def store(number, value):
            env.state[span(number, value.shape[0]), :] = value.astype(BF16)

        return store

    back4 = step(tokens, WIN)

    arguments = dict(
        tok=tokens, wk=w_key, wv=w_value, wqs=w_query_state, init=init_state, wcg=w_cand_gate,
        bias=gate_bias.reshape(1, width),
    )
    lanes = 128

    def first_body(env):
        copies = {}

        def start(*names):
            for name in names:
                copies[name] = env.copy(env.refs[name], env.tok_v if name == "tok" else env.refs[name + "_s"])

        def wait(*names):
            for name in names:
                copies.pop(name).wait()

        start("tok", "wk")
        start("wv", "wqs", "init")
        wait("tok", "wk")
        start("wcg", "bias")
        project(env.tok_v, env.wk_s, store_scaled(env.key, None))
        wait("wv", "wqs", "init")
        store = store_values(env.vt, head)

        def store_and_turn(number, value):
            store(number, value)
            part = span(number, value.shape[1])
            env.wqs_t[part, :] = stand(env.wqs_s[:, part])
            env.init_t[part, :] = stand(env.init_s[:, part])

        project(env.tok_v, env.wv_s, store_and_turn)
        wait("wcg", "bias")
        for col in range(0, width, lanes):
            part = slice(col, col + lanes)
            env.bias_t[part, :] = jnp.broadcast_to(env.bias_s[:, part], (lanes, lanes)).T

        def turn_gates(h):
            part = span(h, 2 * width // HEADS)
            env.wcg_t[part, :] = stand(env.wcg_s[:, part])

        update_columns(
            columns_of(env.init_t, 0), env.wqs_t, env.key, env.vt, env.wcg_t, env.bias_t, env.qs, env.o,
            state_rows(env), turn_gates,
        )

    k = Kernel("keys_values_update", 2 * work + 4 * work // PARTS)
    k.far.update(arguments)
    k.near_out.update(
        tok_v=bf(rows, width), wcg_t=bf(2 * width, width), wqs_t=bf(width, width), init_t=bf(width, states), bias_t=f32(width, lanes), key=bf(rows, width), vt=bf(value_rows(width), rows),
        state=bf(width, some),
    )
    k.scratch.update(
        {n + "_s": vm(*arguments[n].shape, dtype=arguments[n].dtype) for n in arguments if n != "tok"},
        qs=vm(width, some), o=vm(width, some),
    )
    k.copies = len(arguments)
    k.grant = 16 * 1024 * 1024
    tok_v, gates_v, wqs_t, init_t, bias_t, key, vt, state = k.call(first_body)
    got1 = [step(state, 1)]

    def update_operands(k):
        k.near.update(init=init_t, wqs=wqs_t, bias=bias_t, key=key, vt=vt)
        k.near_out.update(state=bf(width, some))
        k.scratch.update(qs=vm(width, some), o=vm(width, some))
        k.copies = 2
        k.grant = 8 * 1024 * 1024

    def fetched_gates(k):
        k.far.update(wcg=wcg_t)
        k.scratch.update(gates=vm(2 * width, width))

    def update(env, h_ref, finish_rows, gates):
        update_columns(
            h_ref, env.wqs, env.key, env.vt, env.gates, env.bias, env.qs, env.o, finish_rows, None, gates.wait if gates else None
        )

    def more_states(env, p):
        out = [env.copy(env.gates, env.wcg_t), env.copy(env.wq, env.wq_v)]
        update(env, columns_of(env.init, p), state_rows(env), None)
        for copy in out:
            copy.wait()

    p = 1
    k = Kernel("update_more", work // 32)
    update_operands(k)
    k.near.update(gates=gates_v)
    k.far.update(wq=w_query)
    k.near_out.update(wq_v=bf(width, width))
    k.far_out.update(wcg_t=bf(2 * width, width))
    state, wq_v, wcg_t = k.call(lambda env: more_states(env, p), after=[state])
    got1.append(step(state, 1))
    after = state

    def causal(s, t):
        down = lax.broadcasted_iota(jnp.int32, (tile, tile), 0)
        across = lax.broadcasted_iota(jnp.int32, (tile, tile), 1)
        last = jnp.where(down <= across, s[t * tile :], NEG)
        return last if t == 0 else jnp.concatenate([s[: t * tile], last], axis=0)

    def local(env, t):
        attend(env.q, env.key, env.vt, [t], lambda t: (t + 1) * tile, causal, None, None, {t: env.o}, {t: env.ml})

    def local_outs(k):
        k.near_out.update(o=f32(width, tile), ml=f32(2 * HEADS, 8, tile))

    def query_body(env):
        project(env.tok, env.wq, store_scaled(env.q, score_scale(head)))
        local(env, 0)

    k = Kernel("query_local", work // 32)
    k.near.update(tok=tok_v, wq=wq_v, key=key, vt=vt)
    k.near_out.update(q=bf(rows, width))
    local_outs(k)
    q, o, ml = k.call(query_body, after=[after])
    after, run_o, run_ml = ml, [o], [ml]

    guesses, got2 = [], []

    def second_body(env, p):
        gates = env.copy(env.wcg, env.gates)
        init = columns_of(env.init, p)
        mixed_guess(env.place[0] == 0, init, env.got, init, init, False, env.mixing, 0, env.guess)
        update(env, env.guess, state_rows(env), gates)

    for p in range(PARTS):
        k = Kernel("update_second", work // 32)
        k.smem.update(place=place, mixing=mixing)
        update_operands(k)
        fetched_gates(k)
        k.near.update(got=got1[p])
        k.near_out.update(guess=bf(width, some))
        state, guess = k.call(lambda env: second_body(env, p), after=[after, back4])
        after = state
        guesses.append(guess)
        got2.append(step(state, 1))

    def more_body(env, t):
        late = t == tiles[-1]
        tok = env.copy(env.tok_h, env.tok) if late else None
        local(env, t)
        if late:
            tok.wait()
            either(env.place[0] % WIN < WIN // 2, env.tok, env.back4, env.pair)
            either(env.place[0] % 2 == 0, env.tok, env.back4, env.core)

    for t in tiles[1:]:
        k = Kernel("local_more", work // 32)
        k.smem.update(place=place)
        k.near.update(q=q, key=key, vt=vt)
        local_outs(k)
        if t == tiles[-1]:
            k.near.update(back4=back4)
            k.far.update(tok_h=tokens)
            k.scratch.update(tok=vm(rows, width))
            k.near_out.update(pair=bf(rows, width), core=bf(rows, width))
        o, ml, *more = k.call(lambda env: more_body(env, t), after=[after])
        after = ml
        run_o.append(o)
        run_ml.append(ml)
    pair, core = more
    back2 = swap(pair, WIN // 2)
    beside = swap(core, 1)

    finals, state_parts = [], []

    def third_body(env, p):
        gates = env.copy(env.wcg, env.gates)
        wskv = env.copy(env.wskv, env.wskv_v) if p == PARTS - 1 else None
        mixed_guess(
            env.place[0] == 0, columns_of(env.init, p), env.got, env.cur, env.before, True, env.mixing, 1, env.guess
        )

        def store(number, value):
            env.state[:, span(number, value.shape[0])] = value.T.astype(BF16)

        update(env, env.guess, store, gates)
        if wskv is not None:
            wskv.wait()

    for p in range(PARTS):
        k = Kernel("update_third", 32 * work // PARTS)
        k.smem.update(place=place, mixing=mixing)
        update_operands(k)
        fetched_gates(k)
        k.near.update(got=got2[p], before=got1[p], cur=guesses[p])
        k.near_out.update(state=bf(some, width), guess=bf(width, some))
        if p == PARTS - 1:
            k.far.update(wskv=w_state_kv)
            k.near_out.update(wskv_v=bf(width, 2 * width))
        state, guess, *wskv_v = k.call(lambda env: third_body(env, p), after=[after])
        after = guess
        finals.append(guess)
        state_parts.append(state)

    def running(k):
        for t in tiles:
            k.near.update({"o%d" % t: run_o[t], "ml%d" % t: run_ml[t]})

    def refs_of(env, name):
        return {t: env.refs["%s%d" % (name, t)] for t in tiles}

    def state_body(env):
        copies = [
            env.copy(env.refs["state%d" % p], env.new_state.at[p * some : (p + 1) * some]) for p in range(PARTS)
        ]
        copies += [env.copy(env.refs[n], env.refs[n + "_v"]) for n in ("wk", "wv")]
        for p in range(PARTS):
            for col in range(0, width, tile):
                part = slice(col, col + tile)
                env.guess[p * some : (p + 1) * some, part] = stand(env.refs["guess%d" % p][part, :])
        project(env.guess, env.wskv.at[:, :width], store_scaled(env.skey, None))
        project(env.guess, env.wskv.at[:, width:], store_values(env.svt, head))
        attend(
            env.q, env.skey, env.svt, tiles, lambda t: states, lambda s, t: s,
            refs_of(env, "o"), refs_of(env, "ml"), refs_of(env, "new_o"), refs_of(env, "new_ml"),
        )
        for copy in copies:
            copy.wait()

    k = Kernel("state_keys", 32 * work)
    k.near.update(wskv=wskv_v[0], q=q)
    k.near.update({"guess%d" % p: finals[p] for p in range(PARTS)})
    k.near.update({"state%d" % p: state_parts[p] for p in range(PARTS)})
    k.far.update(wk=w_key, wv=w_value)
    running(k)
    for t in tiles:
        k.near_out.update({"new_o%d" % t: f32(width, tile), "new_ml%d" % t: f32(2 * HEADS, 8, tile)})
    k.near_out.update({n: bf(width, width) for n in ("wk_v", "wv_v")})
    k.far_out.update(new_state=bf(states, width))
    k.scratch.update(skey=vm(states, width), svt=vm(value_rows(width), states), guess=vm(states, width))
    k.copies = PARTS + 2
    k.grant = 8 * 1024 * 1024
    *pairs, wk_v, wv_v, new_state = k.call(state_body)
    run_o, run_ml = pairs[0::2], pairs[1::2]

    k = Kernel("pass_on", 1)
    k.near.update(back2=back2)
    k.near_out.update(out=bf(rows, width))
    k.aliases.update(back2="out")
    (back2,) = k.call(lambda env: None, after=[run_ml[0]])
    last = swap(back2, 1)

    def last_body(env):
        late = [env.copy(env.tok_h, env.tok), env.copy(env.wout_h, env.wout)]
        even = env.place[0] % 2 == 0
        lift = []
        for e in range(mem // BLK):
            entry = env.retrieval[0, e]
            distance = entry // MBLK + 1
            start = pl.multiple_of((entry % MBLK) * BLK, BLK)
            from_last = ((distance == 1) & even) | ((distance == 3) & jnp.logical_not(even))
            from_beside = ((distance == 3) & even) | ((distance == 1) & jnp.logical_not(even))
            for pick, source in (
                (from_last, env.last), (from_beside, env.beside), (distance == 2, env.back2), (distance == 4, env.back4)
            ):

                @pl.when(pick)
                def _(source=source, start=start, e=e):
                    env.mem[e * BLK : (e + 1) * BLK, :] = source[pl.ds(start, BLK), :]

            lift.append(jnp.where(distance > env.place[0], NEG, 0.0))
        project(env.mem, env.wk, store_scaled(env.key, None))
        project(env.mem, env.wv, store_values(env.vt, head))

        def mask(s, t):
            return jnp.concatenate([s[e * BLK : (e + 1) * BLK] + lift[e] for e in range(mem // BLK)], axis=0)

        new_o, new_ml = refs_of(env, "new_o"), refs_of(env, "new_ml")
        attend(env.q, env.key, env.vt, tiles, lambda t: mem, mask, refs_of(env, "o"), refs_of(env, "ml"), new_o, new_ml)
        for t in tiles:
            for h in range(HEADS):
                part = slice(h * head, (h + 1) * head)
                o = new_o[t][part, :] * (1.0 / new_ml[t][HEADS + h][:1])
                env.on[t * tile : (t + 1) * tile, part] = o.T.astype(BF16)
        for copy in late:
            copy.wait()

        def store(number, value):
            part = span(number, value.shape[1])
            env.sum[:, part] = (env.tok[:, part].astype(F32) + value).astype(BF16)

        project(env.on, env.wout, store)
        env.copy(env.sum, env.mixed).wait()

    k = Kernel("memory_out", 5 * work)
    k.smem.update(place=place, retrieval=retrieval)
    k.far.update(tok_h=tokens, wout_h=w_out)
    k.scratch.update(tok=vm(rows, width), wout=vm(width, width))
    k.near.update(wk=wk_v, wv=wv_v, q=q, last=last, beside=beside, back2=back2, back4=back4)
    running(k)
    k.scratch.update(
        mem=vm(mem, width), key=vm(mem, width), vt=vm(value_rows(width), mem), on=vm(rows, width), sum=vm(rows, width)
    )
    for t in tiles:
        k.scratch.update({"new_o%d" % t: vm(width, tile, dtype=F32), "new_ml%d" % t: vm(2 * HEADS, 8, tile, dtype=F32)})
    k.far_out.update(mixed=bf(rows, width))
    k.copies = 3
    k.grant = 14 * 1024 * 1024
    (mixed,) = k.call(last_body)
    return mixed, new_state


def solution(mesh):
    return jax.shard_map(
        per_device,
        mesh=mesh,
        in_specs=(P("seq", None), P(), P(), P(), P(), P(), P(), P(), P(), P(), P(), P("seq", None)),
        out_specs=(P("seq", None), P("seq", None)),
        check_vma=False,
    )
```

```python
import math

import jax
import jax.numpy as jnp
from jax import lax
from jax.experimental import pallas as pl
from jax.experimental.pallas import tpu as pltpu
from jax.sharding import PartitionSpec as P

HEADS = 8
BLK = 64
MBLK = 8
WIN = 4
PARTS = 2
ONES = 16
NEG = -1e30
VMEM_LIMIT = 6 * 1024 * 1024

BF16 = jnp.bfloat16
F32 = jnp.float32


def dot(a, b):
    return jnp.dot(a, b, preferred_element_type=F32)


def dot_t(a, b):
    return lax.dot_general(a, b, (((1,), (1,)), ((), ())), preferred_element_type=F32)


class Kernel:
    def __init__(self, name, flops):
        self.name, self.flops = name, flops
        self.smem, self.near, self.far = {}, {}, {}
        self.near_out, self.far_out, self.scratch = {}, {}, {}
        self.aliases = {}
        self.copies = 1
        self.grant = VMEM_LIMIT

    def call(self, body, after=()):
        smem, near, far = list(self.smem), list(self.near), list(self.far)
        near_out, far_out, scratch = list(self.near_out), list(self.far_out), list(self.scratch)
        arrays = [self.smem[n] for n in smem]
        arrays += [pltpu.with_memory_space_constraint(self.near[n], pltpu.VMEM) for n in near]
        arrays += [pltpu.with_memory_space_constraint(self.far[n], pltpu.HBM) for n in far]
        arrays += [pltpu.with_memory_space_constraint(a, pltpu.VMEM) for a in after]
        memory = [pltpu.SMEM] * len(smem) + [pltpu.VMEM] * len(near) + [pltpu.HBM] * len(far) + [pltpu.VMEM] * len(after)
        outs = [pltpu.VMEM(self.near_out[n].shape, self.near_out[n].dtype) for n in near_out]
        outs += [pltpu.HBM(self.far_out[n].shape, self.far_out[n].dtype) for n in far_out]
        out_memory = [pltpu.VMEM] * len(near_out) + [pltpu.HBM] * len(far_out)
        names = smem + near + far
        out_names = near_out + far_out

        def kernel(*refs):
            env = Env()
            env.refs = dict(zip(names, refs))
            env.refs.update(zip(out_names, refs[len(arrays) :]))
            env.refs.update(zip(scratch, refs[len(arrays) + len(outs) :]))
            env.sems, env.started = refs[-1], 0
            body(env)

        return pl.pallas_call(
            kernel,
            out_shape=outs,
            in_specs=[pl.BlockSpec(memory_space=m) for m in memory],
            out_specs=[pl.BlockSpec(memory_space=m) for m in out_memory],
            scratch_shapes=[self.scratch[n] for n in scratch] + [pltpu.SemaphoreType.DMA((self.copies,))],
            input_output_aliases={names.index(a): out_names.index(b) for a, b in self.aliases.items()},
            compiler_params=pltpu.CompilerParams(vmem_limit_bytes=self.grant),
            cost_estimate=pl.CostEstimate(flops=self.flops, bytes_accessed=1 << 10, transcendentals=0),
            name=self.name,
        )(*arrays)


class Env:
    def __getattr__(self, name):
        return self.refs[name]

    def copy(self, src, dst):
        copy = pltpu.make_async_copy(src, dst, self.sems.at[self.started])
        self.started += 1
        copy.start()
        return copy


def project(x_ref, w_ref, store, tile=256):
    for col in range(0, w_ref.shape[1], tile):
        store(col, dot(x_ref[...], w_ref[:, col : col + tile]))


def store_scaled(out_ref, scale):
    def store(col, value):
        if scale is not None:
            value = value * scale
        out_ref[:, col : col + value.shape[1]] = value.astype(BF16)

    return store


def score_scale(head):
    return math.log2(math.e) / math.sqrt(head)


def value_rows(width):
    return width + HEADS * ONES


def store_values(vt_ref, head):
    keys = vt_ref.shape[1]
    pitch = head + ONES

    def store(col, value):
        for part in range(0, value.shape[1], head):
            at = (col + part) // head * pitch
            vt_ref[at : at + head, :] = value[:, part : part + head].T.astype(BF16)
            vt_ref[at + head : at + pitch, :] = jnp.ones((ONES, keys), BF16)

    return store


def in_turn(units, scores, finish):
    ahead = scores(*units[0])
    for number, unit in enumerate(units):
        now = ahead
        if number + 1 < len(units):
            ahead = scores(*units[number + 1])
        finish(*unit, now)


def stand(value):
    return value.T


def update_columns(h_ref, wqs_ref, key_ref, vt_ref, wcg_ref, bias_ref, qs_ref, o_ref, finish_rows, beside=None, ready=None):
    width, some = h_ref.shape
    head = width // HEADS
    pitch = head + ONES
    scale = score_scale(head)
    tall = min(512, width)
    for row in range(0, width, tall):
        part = slice(row, row + tall)
        qs_ref[part, :] = (dot(wqs_ref[part, :], h_ref[...]) * scale).astype(BF16)

    def scores(h):
        part = slice(h * head, (h + 1) * head)
        return dot(key_ref[:, part], qs_ref[part, :])

    def finish(h, s):
        if beside is not None:
            beside(h)
        p = jnp.exp2(s - jnp.max(s, axis=0, keepdims=True)).astype(BF16)
        ol = dot(vt_ref[h * pitch : (h + 1) * pitch, :], p)
        o_ref[h * head : (h + 1) * head, :] = (ol[:head] * (1.0 / ol[head : head + 1])).astype(BF16)

    in_turn([(h,) for h in range(HEADS)], scores, finish)
    if ready is not None:
        ready()
    tall = min(256, width)
    for row in range(0, width, tall):
        part = slice(row, row + tall)
        zc = dot(wcg_ref[part, :], o_ref[...])
        zg = dot(wcg_ref[width + row : width + row + tall, :], o_ref[...])
        lanes = bias_ref.shape[1]
        bias = jnp.concatenate([bias_ref[part, :]] * (some // lanes), axis=1)
        cand = jnp.tanh(zc)
        forget = 0.5 * jnp.tanh(0.5 * (zg + bias)) + 0.5
        finish_rows(row, forget * h_ref[part, :].astype(F32) + (1.0 - forget) * cand)


def attend(q_ref, key_ref, vt_ref, places, limit, mask, old_o, old_ml, new_o, new_ml):
    head = q_ref.shape[1] // HEADS
    pitch = head + ONES
    tile = new_o[places[0]].shape[1]

    def scores(h, t):
        part = slice(h * head, (h + 1) * head)
        return dot_t(key_ref[: limit(t), part], q_ref[t * tile : (t + 1) * tile, part])

    def finish(h, t, s):
        part = slice(h * head, (h + 1) * head)
        top_row, sum_row = slice(h, h + 1), slice(HEADS + h, HEADS + h + 1)
        s = mask(s, t)
        top = jnp.max(s, axis=0, keepdims=True)
        if old_o is not None:
            old = old_ml[t][top_row, :]
            top = jnp.maximum(top, old)
        p = jnp.exp2(s - top).astype(BF16)
        ol = dot(vt_ref[h * pitch : (h + 1) * pitch, : limit(t)], p)
        o, l = ol[:head], ol[head : head + 1]
        if old_o is not None:
            keep = jnp.exp2(old - top)
            o = o + keep * old_o[t][part, :]
            l = l + keep * old_ml[t][sum_row, :]
        new_o[t][part, :] = o
        new_ml[t][top_row, :] = top
        new_ml[t][sum_row, :] = l

    in_turn([(h, t) for h in range(HEADS) for t in places], scores, finish)


def mixed_guess(pick, init_ref, got_ref, cur_ref, prev_ref, prev_pick, mixing, sweep, guess_ref):
    a, b, c = mixing[sweep, 0], mixing[sweep, 1], mixing[sweep, 2]
    rows = guess_ref.shape[0]
    step = min(64, rows)
    for r in range(0, rows, step):
        part = slice(r, r + step)
        init = init_ref[part, :].astype(F32)
        shift = jnp.where(pick, init, got_ref[part, :].astype(F32))
        prev = prev_ref[part, :].astype(F32)
        if prev_pick:
            prev = jnp.where(pick, init, prev)
        guess = a * shift + b * cur_ref[part, :].astype(F32)
        guess_ref[part, :] = (guess + c * prev).astype(BF16)


def either(pick, yes_ref, no_ref, out_ref):
    @pl.when(pick)
    def _():
        out_ref[...] = yes_ref[...]

    @pl.when(jnp.logical_not(pick))
    def _():
        out_ref[...] = no_ref[...]


def bf(*shape):
    return jax.ShapeDtypeStruct(shape, BF16)


def f32(*shape):
    return jax.ShapeDtypeStruct(shape, F32)


def vm(*shape, dtype=BF16):
    return pltpu.VMEM(shape, dtype)


def per_device(
    tokens, init_state, w_query, w_key, w_value, w_out, w_query_state, w_cand_gate, w_state_kv,
    gate_bias, mixing, retrieval,
):
    rows, width = tokens.shape
    states = init_state.shape[0]
    head = width // HEADS
    some = states // PARTS
    tile = min(256, rows)
    tiles = list(range(rows // tile))
    mem = retrieval.shape[1] * BLK
    count = lax.axis_size("seq")
    place = lax.axis_index("seq").astype(jnp.int32).reshape(1)
    work = 2 * rows * width * width

    def step(value, by):
        return lax.ppermute(value, "seq", [(i, i + by) for i in range(count - by)])

    def swap(value, bit):
        return lax.ppermute(value, "seq", [(i, i ^ bit) for i in range(count)])

    def columns_of(ref, p):
        return ref.at[:, p * some : (p + 1) * some]

    def state_rows(env):
        def store(row, value):
            env.state[row : row + value.shape[0], :] = value.astype(BF16)

        return store

    back4 = step(tokens, WIN)

    arguments = dict(
        tok=tokens, wk=w_key, wv=w_value, wqs=w_query_state, init=init_state, wcg=w_cand_gate,
        bias=gate_bias.reshape(1, width),
    )
    lanes = 128

    def first_body(env):
        copies = {}

        def start(*names):
            for name in names:
                copies[name] = env.copy(env.refs[name], env.refs[name + "_s"])

        def wait(*names):
            for name in names:
                copies.pop(name).wait()

        start("tok", "wk")
        start("wv", "wqs", "init")
        wait("tok", "wk")
        start("wcg", "bias")
        project(env.tok_s, env.wk_s, store_scaled(env.key, None))
        wait("wv", "wqs", "init")
        store = store_values(env.vt, head)

        def store_and_turn(col, value):
            store(col, value)
            part = slice(col, col + value.shape[1])
            env.wqs_t[part, :] = stand(env.wqs_s[:, part])
            env.init_t[part, :] = stand(env.init_s[:, part])

        project(env.tok_s, env.wv_s, store_and_turn)
        wait("wcg", "bias")
        for col in range(0, width, lanes):
            part = slice(col, col + lanes)
            env.bias_t[part, :] = jnp.broadcast_to(env.bias_s[:, part], (lanes, lanes)).T

        def turn_gates(h):
            size = 2 * width // HEADS
            part = slice(h * size, (h + 1) * size)
            env.wcg_t[part, :] = stand(env.wcg_s[:, part])

        update_columns(
            columns_of(env.init_t, 0), env.wqs_t, env.key, env.vt, env.wcg_t, env.bias_t, env.qs, env.o,
            state_rows(env), turn_gates,
        )

    k = Kernel("keys_values_update", 2 * work + 4 * work // PARTS)
    k.far.update(arguments)
    k.near_out.update(
        wcg_t=bf(2 * width, width), wqs_t=bf(width, width), init_t=bf(width, states), bias_t=f32(width, lanes), key=bf(rows, width), vt=bf(value_rows(width), rows),
        state=bf(width, some),
    )
    k.scratch.update(
        {n + "_s": vm(*arguments[n].shape, dtype=arguments[n].dtype) for n in arguments},
        qs=vm(width, some), o=vm(width, some),
    )
    k.copies = len(arguments)
    k.grant = 16 * 1024 * 1024
    gates_v, wqs_t, init_t, bias_t, key, vt, state = k.call(first_body)
    got1 = [step(state, 1)]

    def update_operands(k):
        k.near.update(init=init_t, wqs=wqs_t, bias=bias_t, key=key, vt=vt)
        k.near_out.update(state=bf(width, some))
        k.scratch.update(qs=vm(width, some), o=vm(width, some))
        k.copies = 3
        k.grant = 8 * 1024 * 1024

    def fetched_gates(k):
        k.far.update(wcg=wcg_t)
        k.scratch.update(gates=vm(2 * width, width))

    def update(env, h_ref, finish_rows, gates):
        update_columns(
            h_ref, env.wqs, env.key, env.vt, env.gates, env.bias, env.qs, env.o, finish_rows, None, gates.wait if gates else None
        )

    def more_states(env, p):
        out = env.copy(env.gates, env.wcg_t)
        update(env, columns_of(env.init, p), state_rows(env), None)
        out.wait()

    p = 1
    k = Kernel("update_more", work // 32)
    update_operands(k)
    k.near.update(gates=gates_v)
    k.far_out.update(wcg_t=bf(2 * width, width))
    state, wcg_t = k.call(lambda env: more_states(env, p), after=[state])
    got1.append(step(state, 1))
    after = state

    def causal(s, t):
        down = lax.broadcasted_iota(jnp.int32, (tile, tile), 0)
        across = lax.broadcasted_iota(jnp.int32, (tile, tile), 1)
        last = jnp.where(down <= across, s[t * tile :], NEG)
        return last if t == 0 else jnp.concatenate([s[: t * tile], last], axis=0)

    def local(env, t):
        attend(env.q, env.key, env.vt, [t], lambda t: (t + 1) * tile, causal, None, None, {t: env.o}, {t: env.ml})

    def local_outs(k):
        k.near_out.update(o=f32(width, tile), ml=f32(2 * HEADS, tile))

    def query_body(env):
        tok = env.copy(env.tok_h, env.tok)
        pieces = [slice(col, col + tile) for col in range(0, width, tile)]
        copies = [env.copy(env.wq_h.at[:, part], env.wq.at[:, part]) for part in pieces]
        tok.wait()
        for part, copy in zip(pieces, copies):
            copy.wait()
            env.q[:, part] = (dot(env.tok[...], env.wq[:, part]) * score_scale(head)).astype(BF16)
        local(env, 0)

    k = Kernel("query_local", work // 32)
    k.near.update(key=key, vt=vt)
    k.far.update(tok_h=tokens, wq_h=w_query)
    k.scratch.update(tok=vm(rows, width), wq=vm(width, width))
    k.copies = 1 + width // tile
    k.near_out.update(q=bf(rows, width))
    local_outs(k)
    q, o, ml = k.call(query_body, after=[after])
    after, run_o, run_ml = ml, [o], [ml]

    guesses, got2 = [], []

    def chosen(env, pick, yes, no, dst):
        number = env.started
        env.started += 1

        @pl.when(pick)
        def _():
            pltpu.make_async_copy(yes, dst, env.sems.at[number]).start()

        @pl.when(jnp.logical_not(pick))
        def _():
            pltpu.make_async_copy(no, dst, env.sems.at[number]).start()

        return pltpu.make_async_copy(no, dst, env.sems.at[number])

    def second_body(env, p):
        waits = []
        if p == 0:
            low = env.place[0] % WIN < WIN // 2
            even = env.place[0] % 2 == 0
            waits = [
                chosen(env, low, env.tok_h, env.back4, env.pair),
                chosen(env, low, env.tok_h, env.back4, env.pair_odd),
                chosen(env, even, env.tok_h, env.back4, env.core),
            ]
        gates = env.copy(env.wcg, env.gates)
        init = columns_of(env.init, p)
        mixed_guess(env.place[0] == 0, init, env.got, init, init, False, env.mixing, 0, env.guess)
        update(env, env.guess, state_rows(env), gates)
        for copy in waits:
            copy.wait()

    for p in range(PARTS):
        k = Kernel("update_second", work // 32)
        k.smem.update(place=place, mixing=mixing)
        update_operands(k)
        fetched_gates(k)
        k.near.update(got=got1[p])
        k.near_out.update(guess=bf(width, some))
        if p == 0:
            k.near.update(back4=back4)
            k.far.update(tok_h=tokens)
            k.near_out.update(pair=bf(rows, width), pair_odd=bf(rows, width), core=bf(rows, width))
            k.copies = 4
        state, guess, *more = k.call(lambda env: second_body(env, p), after=[after])
        if p == 0:
            pair, pair_odd, core = more
        after = state
        guesses.append(guess)
        got2.append(step(state, 1))

    back2_even = lax.ppermute(pair, "seq", [(i, i ^ (WIN // 2)) for i in range(0, count, 2)])

    for t in tiles[1:]:
        k = Kernel("local_more", work // 32)
        k.near.update(q=q, key=key, vt=vt)
        local_outs(k)
        if t == tiles[-1]:
            k.near.update(core=core, pair_odd=pair_odd)
            k.near_out.update(core_out=bf(rows, width), pair_out=bf(rows, width))
            k.aliases.update(core="core_out", pair_odd="pair_out")
        o, ml, *more = k.call(lambda env: local(env, t), after=[after])
        after = ml
        run_o.append(o)
        run_ml.append(ml)
    core, pair_odd = more
    back2_odd = lax.ppermute(pair_odd, "seq", [(i, i ^ (WIN // 2)) for i in range(1, count, 2)])
    beside = swap(core, 1)

    finals, state_parts = [], []

    def third_body(env, p):
        gates = env.copy(env.wcg, env.gates)
        wskv = env.copy(env.wskv, env.wskv_v) if p == PARTS - 1 else None
        mixed_guess(
            env.place[0] == 0, columns_of(env.init, p), env.got, env.cur, env.before, True, env.mixing, 1, env.guess
        )

        def store(row, value):
            env.state[:, row : row + value.shape[0]] = value.T.astype(BF16)

        update(env, env.guess, store, gates)
        if wskv is not None:
            wskv.wait()

    for p in range(PARTS):
        k = Kernel("update_third", 32 * work // PARTS)
        k.smem.update(place=place, mixing=mixing)
        update_operands(k)
        fetched_gates(k)
        k.near.update(got=got2[p], before=got1[p], cur=guesses[p])
        k.near_out.update(state=bf(some, width), guess=bf(width, some))
        if p == PARTS - 1:
            k.far.update(wskv=w_state_kv)
            k.near_out.update(wskv_v=bf(width, 2 * width))
        state, guess, *more = k.call(lambda env: third_body(env, p), after=[after])
        after = guess
        finals.append(guess)
        state_parts.append(state)

    (wskv_v,) = more

    def running(k):
        for t in tiles:
            k.near.update({"o%d" % t: run_o[t], "ml%d" % t: run_ml[t]})

    def refs_of(env, name):
        return {t: env.refs["%s%d" % (name, t)] for t in tiles}

    def state_body(env):
        copies = [
            env.copy(env.refs["state%d" % p], env.new_state.at[p * some : (p + 1) * some]) for p in range(PARTS)
        ]
        copies += [env.copy(env.refs[n], env.refs[n + "_v"]) for n in ("wk", "wv")]
        for p in range(PARTS):
            for col in range(0, width, tile):
                part = slice(col, col + tile)
                env.guess[p * some : (p + 1) * some, part] = stand(env.refs["guess%d" % p][part, :])
        project(env.guess, env.wskv.at[:, :width], store_scaled(env.skey, None))
        project(env.guess, env.wskv.at[:, width:], store_values(env.svt, head))
        attend(
            env.q, env.skey, env.svt, tiles, lambda t: states, lambda s, t: s,
            refs_of(env, "o"), refs_of(env, "ml"), refs_of(env, "new_o"), refs_of(env, "new_ml"),
        )
        for copy in copies:
            copy.wait()

    k = Kernel("state_keys", 32 * work)
    k.near.update(wskv=wskv_v, q=q)
    k.near.update({"guess%d" % p: finals[p] for p in range(PARTS)})
    k.near.update({"state%d" % p: state_parts[p] for p in range(PARTS)})
    k.far.update(wk=w_key, wv=w_value)
    running(k)
    for t in tiles:
        k.near_out.update({"new_o%d" % t: f32(width, tile), "new_ml%d" % t: f32(2 * HEADS, tile)})
    k.near_out.update({n: bf(width, width) for n in ("wk_v", "wv_v")})
    k.far_out.update(new_state=bf(states, width))
    k.scratch.update(skey=vm(states, width), svt=vm(value_rows(width), states), guess=vm(states, width))
    k.copies = PARTS + 2
    k.grant = 8 * 1024 * 1024
    k.near.update(back2=back2_even)
    k.near_out.update(back2_out=bf(rows, width))
    k.aliases.update(back2="back2_out")
    *pairs, wk_v, wv_v, back2_even, new_state = k.call(state_body)
    last_even = lax.ppermute(back2_even, "seq", [(i, i + 1) for i in range(0, count, 2)])
    run_o, run_ml = pairs[0::2], pairs[1::2]

    k = Kernel("pass_on", 1)
    k.near.update(back2=back2_odd)
    k.near_out.update(out=bf(rows, width))
    k.aliases.update(back2="out")
    (back2_odd,) = k.call(lambda env: None, after=[run_ml[0]])
    last_odd = lax.ppermute(back2_odd, "seq", [(i, i - 1) for i in range(1, count, 2)])

    def last_body(env):
        late = [env.copy(env.tok_h, env.tok), env.copy(env.wout_h, env.wout)]
        even = env.place[0] % 2 == 0
        lift = []
        for e in range(mem // BLK):
            entry = env.retrieval[0, e]
            distance = entry // MBLK + 1
            start = pl.multiple_of((entry % MBLK) * BLK, BLK)
            odd = jnp.logical_not(even)
            for pick, source in (
                ((distance == 1) & even, env.last_odd), ((distance == 1) & odd, env.beside),
                ((distance == 2) & even, env.back2_even), ((distance == 2) & odd, env.back2_odd),
                ((distance == 3) & even, env.beside), ((distance == 3) & odd, env.last_even),
                (distance == 4, env.back4),
            ):

                @pl.when(pick)
                def _(source=source, start=start, e=e):
                    env.mem[e * BLK : (e + 1) * BLK, :] = source[pl.ds(start, BLK), :]

            lift.append(jnp.where(distance > env.place[0], NEG, 0.0))
        project(env.mem, env.wk, store_scaled(env.key, None))
        project(env.mem, env.wv, store_values(env.vt, head))

        def mask(s, t):
            return jnp.concatenate([s[e * BLK : (e + 1) * BLK] + lift[e] for e in range(mem // BLK)], axis=0)

        new_o, new_ml = refs_of(env, "new_o"), refs_of(env, "new_ml")
        attend(env.q, env.key, env.vt, tiles, lambda t: mem, mask, refs_of(env, "o"), refs_of(env, "ml"), new_o, new_ml)
        for t in tiles:
            for h in range(HEADS):
                part = slice(h * head, (h + 1) * head)
                o = new_o[t][part, :] * (1.0 / new_ml[t][HEADS + h : HEADS + h + 1, :])
                env.on[t * tile : (t + 1) * tile, part] = o.T.astype(BF16)
        copies = []
        for copy in late:
            copy.wait()

        def store(col, value):
            part = slice(col, col + value.shape[1])
            env.sum[:, part] = (env.tok[:, part].astype(F32) + value).astype(BF16)
            copies.append(env.copy(env.sum.at[:, part], env.mixed.at[:, part]))

        project(env.on, env.wout, store)
        for copy in copies:
            copy.wait()

    k = Kernel("memory_out", 5 * work)
    k.smem.update(place=place, retrieval=retrieval)
    k.near.update(last_even=last_even, last_odd=last_odd, back2_even=back2_even, back2_odd=back2_odd)
    k.far.update(tok_h=tokens, wout_h=w_out)
    k.scratch.update(tok=vm(rows, width), wout=vm(width, width))
    k.near.update(wk=wk_v, wv=wv_v, q=q, beside=beside, back4=back4)
    running(k)
    k.scratch.update(
        mem=vm(mem, width), key=vm(mem, width), vt=vm(value_rows(width), mem), on=vm(rows, width), sum=vm(rows, width)
    )
    for t in tiles:
        k.scratch.update({"new_o%d" % t: vm(width, tile, dtype=F32), "new_ml%d" % t: vm(2 * HEADS, tile, dtype=F32)})
    k.far_out.update(mixed=bf(rows, width))
    k.copies = width // 256 + 2
    k.grant = 14 * 1024 * 1024
    (mixed,) = k.call(last_body)
    return mixed, new_state


def solution(mesh):
    return jax.shard_map(
        per_device,
        mesh=mesh,
        in_specs=(P("seq", None), P(), P(), P(), P(), P(), P(), P(), P(), P(), P(), P("seq", None)),
        out_specs=(P("seq", None), P("seq", None)),
        check_vma=False,
    )
```

```python
import math

import jax
import jax.numpy as jnp
from jax import lax
from jax.experimental import pallas as pl
from jax.experimental.pallas import tpu as pltpu
from jax.sharding import PartitionSpec as P

HEADS = 8
BLK = 64
MBLK = 8
WIN = 4
PARTS = 2
ONES = 16
NEG = -1e30
VMEM_LIMIT = 6 * 1024 * 1024

BF16 = jnp.bfloat16
F32 = jnp.float32


def dot(a, b):
    return jnp.dot(a, b, preferred_element_type=F32)


def dot_t(a, b):
    return lax.dot_general(a, b, (((1,), (1,)), ((), ())), preferred_element_type=F32)


class Kernel:
    def __init__(self, name, flops):
        self.name, self.flops = name, flops
        self.smem, self.near, self.far = {}, {}, {}
        self.near_out, self.far_out, self.scratch = {}, {}, {}
        self.aliases = {}
        self.copies = 1
        self.grant = VMEM_LIMIT

    def call(self, body, after=()):
        smem, near, far = list(self.smem), list(self.near), list(self.far)
        near_out, far_out, scratch = list(self.near_out), list(self.far_out), list(self.scratch)
        arrays = [self.smem[n] for n in smem]
        arrays += [pltpu.with_memory_space_constraint(self.near[n], pltpu.VMEM) for n in near]
        arrays += [pltpu.with_memory_space_constraint(self.far[n], pltpu.HBM) for n in far]
        arrays += [pltpu.with_memory_space_constraint(a, pltpu.VMEM) for a in after]
        memory = [pltpu.SMEM] * len(smem) + [pltpu.VMEM] * len(near) + [pltpu.HBM] * len(far) + [pltpu.VMEM] * len(after)
        outs = [pltpu.VMEM(self.near_out[n].shape, self.near_out[n].dtype) for n in near_out]
        outs += [pltpu.HBM(self.far_out[n].shape, self.far_out[n].dtype) for n in far_out]
        out_memory = [pltpu.VMEM] * len(near_out) + [pltpu.HBM] * len(far_out)
        names = smem + near + far
        out_names = near_out + far_out

        def kernel(*refs):
            env = Env()
            env.refs = dict(zip(names, refs))
            env.refs.update(zip(out_names, refs[len(arrays) :]))
            env.refs.update(zip(scratch, refs[len(arrays) + len(outs) :]))
            env.sems, env.started = refs[-1], 0
            body(env)

        return pl.pallas_call(
            kernel,
            out_shape=outs,
            in_specs=[pl.BlockSpec(memory_space=m) for m in memory],
            out_specs=[pl.BlockSpec(memory_space=m) for m in out_memory],
            scratch_shapes=[self.scratch[n] for n in scratch] + [pltpu.SemaphoreType.DMA((self.copies,))],
            input_output_aliases={names.index(a): out_names.index(b) for a, b in self.aliases.items()},
            compiler_params=pltpu.CompilerParams(vmem_limit_bytes=self.grant),
            cost_estimate=pl.CostEstimate(flops=self.flops, bytes_accessed=1 << 10, transcendentals=0),
            name=self.name,
        )(*arrays)


class Env:
    def __getattr__(self, name):
        return self.refs[name]

    def copy(self, src, dst):
        copy = pltpu.make_async_copy(src, dst, self.sems.at[self.started])
        self.started += 1
        copy.start()
        return copy


def project(x_ref, w_ref, store, tile=256):
    for col in range(0, w_ref.shape[1], tile):
        store(col, dot(x_ref[...], w_ref[:, col : col + tile]))


def store_scaled(out_ref, scale):
    def store(col, value):
        if scale is not None:
            value = value * scale
        out_ref[:, col : col + value.shape[1]] = value.astype(BF16)

    return store


def score_scale(head):
    return math.log2(math.e) / math.sqrt(head)


def value_rows(width):
    return width + HEADS * ONES


def store_values(vt_ref, head):
    keys = vt_ref.shape[1]
    pitch = head + ONES

    def store(col, value):
        for part in range(0, value.shape[1], head):
            at = (col + part) // head * pitch
            vt_ref[at : at + head, :] = value[:, part : part + head].T.astype(BF16)
            vt_ref[at + head : at + pitch, :] = jnp.ones((ONES, keys), BF16)

    return store


def in_turn(units, scores, finish):
    ahead = scores(*units[0])
    for number, unit in enumerate(units):
        now = ahead
        if number + 1 < len(units):
            ahead = scores(*units[number + 1])
        finish(*unit, now)


def stand(value):
    return value.T


def update_columns(h_ref, wqs_ref, key_ref, vt_ref, wcg_ref, bias_ref, qs_ref, o_ref, finish_rows, beside=None, ready=None):
    width, some = h_ref.shape
    head = width // HEADS
    pitch = head + ONES
    scale = score_scale(head)
    tall = min(512, width)
    for row in range(0, width, tall):
        part = slice(row, row + tall)
        qs_ref[part, :] = (dot(wqs_ref[part, :], h_ref[...]) * scale).astype(BF16)

    def scores(h):
        part = slice(h * head, (h + 1) * head)
        return dot(key_ref[:, part], qs_ref[part, :])

    def finish(h, s):
        if beside is not None:
            beside(h)
        p = jnp.exp2(s - jnp.max(s, axis=0, keepdims=True)).astype(BF16)
        ol = dot(vt_ref[h * pitch : (h + 1) * pitch, :], p)
        o_ref[h * head : (h + 1) * head, :] = (ol[:head] * (1.0 / ol[head : head + 1])).astype(BF16)

    in_turn([(h,) for h in range(HEADS)], scores, finish)
    if ready is not None:
        ready()
    tall = min(256, width)
    for row in range(0, width, tall):
        part = slice(row, row + tall)
        zc = dot(wcg_ref[part, :], o_ref[...])
        zg = dot(wcg_ref[width + row : width + row + tall, :], o_ref[...])
        lanes = bias_ref.shape[1]
        bias = jnp.concatenate([bias_ref[part, :]] * (some // lanes), axis=1)
        cand = jnp.tanh(zc)
        forget = 0.5 * jnp.tanh(0.5 * (zg + bias)) + 0.5
        finish_rows(row, forget * h_ref[part, :].astype(F32) + (1.0 - forget) * cand)


def attend(q_ref, key_ref, vt_ref, places, limit, mask, old_o, old_ml, new_o, new_ml):
    head = q_ref.shape[1] // HEADS
    pitch = head + ONES
    tile = new_o[places[0]].shape[1]

    def scores(h, t):
        part = slice(h * head, (h + 1) * head)
        return dot_t(key_ref[: limit(t), part], q_ref[t * tile : (t + 1) * tile, part])

    def finish(h, t, s):
        part = slice(h * head, (h + 1) * head)
        top_row, sum_row = slice(h, h + 1), slice(HEADS + h, HEADS + h + 1)
        s = mask(s, t)
        top = jnp.max(s, axis=0, keepdims=True)
        if old_o is not None:
            old = old_ml[t][top_row, :]
            top = jnp.maximum(top, old)
        p = jnp.exp2(s - top).astype(BF16)
        ol = dot(vt_ref[h * pitch : (h + 1) * pitch, : limit(t)], p)
        o, l = ol[:head], ol[head : head + 1]
        if old_o is not None:
            keep = jnp.exp2(old - top)
            o = o + keep * old_o[t][part, :]
            l = l + keep * old_ml[t][sum_row, :]
        new_o[t][part, :] = o
        new_ml[t][top_row, :] = top
        new_ml[t][sum_row, :] = l

    in_turn([(h, t) for h in range(HEADS) for t in places], scores, finish)


def mixed_guess(pick, init_ref, got_ref, cur_ref, prev_ref, prev_pick, mixing, sweep, guess_ref):
    a, b, c = mixing[sweep, 0], mixing[sweep, 1], mixing[sweep, 2]
    rows = guess_ref.shape[0]
    step = min(64, rows)
    for r in range(0, rows, step):
        part = slice(r, r + step)
        init = init_ref[part, :].astype(F32)
        shift = jnp.where(pick, init, got_ref[part, :].astype(F32))
        prev = prev_ref[part, :].astype(F32)
        if prev_pick:
            prev = jnp.where(pick, init, prev)
        guess = a * shift + b * cur_ref[part, :].astype(F32)
        guess_ref[part, :] = (guess + c * prev).astype(BF16)


def bf(*shape):
    return jax.ShapeDtypeStruct(shape, BF16)


def f32(*shape):
    return jax.ShapeDtypeStruct(shape, F32)


def vm(*shape, dtype=BF16):
    return pltpu.VMEM(shape, dtype)


def per_device(
    tokens, init_state, w_query, w_key, w_value, w_out, w_query_state, w_cand_gate, w_state_kv,
    gate_bias, mixing, retrieval,
):
    rows, width = tokens.shape
    states = init_state.shape[0]
    head = width // HEADS
    some = states // PARTS
    tile = min(256, rows)
    tiles = list(range(rows // tile))
    mem = retrieval.shape[1] * BLK
    count = lax.axis_size("seq")
    place = lax.axis_index("seq").astype(jnp.int32).reshape(1)
    work = 2 * rows * width * width

    def step(value, by):
        return lax.ppermute(value, "seq", [(i, i + by) for i in range(count - by)])

    def swap(value, bit):
        return lax.ppermute(value, "seq", [(i, i ^ bit) for i in range(count)])

    def columns_of(ref, p):
        return ref.at[:, p * some : (p + 1) * some]

    def state_rows(env):
        def store(row, value):
            env.state[row : row + value.shape[0], :] = value.astype(BF16)

        return store

    back4 = step(tokens, WIN)

    arguments = dict(
        tok=tokens, wk=w_key, wv=w_value, wqs=w_query_state, init=init_state, wcg=w_cand_gate,
        bias=gate_bias.reshape(1, width),
    )
    lanes = 128

    def first_body(env):
        copies = {}

        def start(*names):
            for name in names:
                copies[name] = env.copy(env.refs[name], env.refs[name + "_s"])

        def wait(*names):
            for name in names:
                copies.pop(name).wait()

        start("tok", "wk")
        start("wv", "wqs", "init")
        wait("tok", "wk")
        start("wcg", "bias")
        project(env.tok_s, env.wk_s, store_scaled(env.key, None))
        wait("wv", "wqs", "init")
        store = store_values(env.vt, head)

        def store_and_turn(col, value):
            store(col, value)
            part = slice(col, col + value.shape[1])
            env.wqs_t[part, :] = stand(env.wqs_s[:, part])
            env.init_t[part, :] = stand(env.init_s[:, part])

        project(env.tok_s, env.wv_s, store_and_turn)
        wait("wcg", "bias")
        for col in range(0, width, lanes):
            part = slice(col, col + lanes)
            env.bias_t[part, :] = jnp.broadcast_to(env.bias_s[:, part], (lanes, lanes)).T

        def turn_gates(h):
            size = 2 * width // HEADS
            part = slice(h * size, (h + 1) * size)
            env.wcg_t[part, :] = stand(env.wcg_s[:, part])

        update_columns(
            columns_of(env.init_t, 0), env.wqs_t, env.key, env.vt, env.wcg_t, env.bias_t, env.qs, env.o,
            state_rows(env), turn_gates,
        )

    k = Kernel("keys_values_update", 2 * work + 4 * work // PARTS)
    k.far.update(arguments)
    k.near_out.update(
        wcg_t=bf(2 * width, width), wqs_t=bf(width, width), init_t=bf(width, states), bias_t=f32(width, lanes), key=bf(rows, width), vt=bf(value_rows(width), rows),
        state=bf(width, some),
    )
    k.scratch.update(
        {n + "_s": vm(*arguments[n].shape, dtype=arguments[n].dtype) for n in arguments},
        qs=vm(width, some), o=vm(width, some),
    )
    k.copies = len(arguments)
    k.grant = 16 * 1024 * 1024
    gates_v, wqs_t, init_t, bias_t, key, vt, state = k.call(first_body)
    got1 = [step(state, 1)]

    def update_operands(k):
        k.near.update(init=init_t, wqs=wqs_t, bias=bias_t, key=key, vt=vt)
        k.near_out.update(state=bf(width, some))
        k.scratch.update(qs=vm(width, some), o=vm(width, some))
        k.copies = 3
        k.grant = 8 * 1024 * 1024

    def fetched_gates(k):
        k.far.update(wcg=wcg_t)
        k.scratch.update(gates=vm(2 * width, width))

    def update(env, h_ref, finish_rows, gates):
        update_columns(
            h_ref, env.wqs, env.key, env.vt, env.gates, env.bias, env.qs, env.o, finish_rows, None, gates.wait if gates else None
        )

    def more_states(env, p):
        out = env.copy(env.gates, env.wcg_t)
        update(env, columns_of(env.init, p), state_rows(env), None)
        out.wait()

    p = 1
    k = Kernel("update_more", work // 32)
    update_operands(k)
    k.near.update(gates=gates_v)
    k.far_out.update(wcg_t=bf(2 * width, width))
    state, wcg_t = k.call(lambda env: more_states(env, p), after=[state])
    got1.append(step(state, 1))
    after = state

    def causal(s, t):
        down = lax.broadcasted_iota(jnp.int32, (tile, tile), 0)
        across = lax.broadcasted_iota(jnp.int32, (tile, tile), 1)
        last = jnp.where(down <= across, s[t * tile :], NEG)
        return last if t == 0 else jnp.concatenate([s[: t * tile], last], axis=0)

    def local(env, t):
        attend(env.q, env.key, env.vt, [t], lambda t: (t + 1) * tile, causal, None, None, {t: env.o}, {t: env.ml})

    def local_outs(k):
        k.near_out.update(o=f32(width, tile), ml=f32(2 * HEADS, tile))

    def query_body(env):
        for copy in [env.copy(env.tok_h, env.tok), env.copy(env.wq_h, env.wq)]:
            copy.wait()
        project(env.tok, env.wq, store_scaled(env.q, score_scale(head)))
        local(env, 0)

    k = Kernel("query_local", work // 32)
    k.near.update(key=key, vt=vt)
    k.far.update(tok_h=tokens, wq_h=w_query)
    k.scratch.update(tok=vm(rows, width), wq=vm(width, width))
    k.copies = 2
    k.near_out.update(q=bf(rows, width))
    local_outs(k)
    q, o, ml = k.call(query_body, after=[after])
    after, run_o, run_ml = ml, [o], [ml]

    guesses, got2 = [], []

    def second_body(env, p):
        gates = env.copy(env.wcg, env.gates)
        init = columns_of(env.init, p)
        mixed_guess(env.place[0] == 0, init, env.got, init, init, False, env.mixing, 0, env.guess)
        update(env, env.guess, state_rows(env), gates)

    for p in range(PARTS):
        k = Kernel("update_second", work // 32)
        k.smem.update(place=place, mixing=mixing)
        update_operands(k)
        fetched_gates(k)
        k.near.update(got=got1[p])
        k.near_out.update(guess=bf(width, some))
        state, guess = k.call(lambda env: second_body(env, p), after=[after])
        after = state
        guesses.append(guess)
        got2.append(step(state, 1))

    def chosen(env, pick, yes, no, dst):
        number = env.started
        env.started += 1

        @pl.when(pick)
        def _():
            pltpu.make_async_copy(yes, dst, env.sems.at[number]).start()

        @pl.when(jnp.logical_not(pick))
        def _():
            pltpu.make_async_copy(no, dst, env.sems.at[number]).start()

        return pltpu.make_async_copy(no, dst, env.sems.at[number])

    def more_body(env, t):
        copies = []
        if t == tiles[-1]:
            copies = [
                chosen(env, env.place[0] % WIN < WIN // 2, env.tok_h, env.back4, env.pair),
                chosen(env, env.place[0] % 2 == 0, env.tok_h, env.back4, env.core),
            ]
        local(env, t)
        for copy in copies:
            copy.wait()

    for t in tiles[1:]:
        k = Kernel("local_more", 4 * work)
        k.smem.update(place=place)
        k.near.update(q=q, key=key, vt=vt)
        local_outs(k)
        if t == tiles[-1]:
            k.near.update(back4=back4)
            k.far.update(tok_h=tokens)
            k.copies = 2
            k.near_out.update(pair=bf(rows, width), core=bf(rows, width))
        o, ml, *more = k.call(lambda env: more_body(env, t), after=[after])
        after = ml
        run_o.append(o)
        run_ml.append(ml)
    pair, core = more
    back2 = swap(pair, WIN // 2)
    beside = swap(core, 1)

    finals, state_parts = [], []

    def third_body(env, p):
        gates = env.copy(env.wcg, env.gates)
        wskv = env.copy(env.wskv, env.wskv_v) if p == PARTS - 1 else None
        mixed_guess(
            env.place[0] == 0, columns_of(env.init, p), env.got, env.cur, env.before, True, env.mixing, 1, env.guess
        )

        def store(row, value):
            env.state[:, row : row + value.shape[0]] = value.T.astype(BF16)

        update(env, env.guess, store, gates)
        if wskv is not None:
            wskv.wait()

    for p in range(PARTS):
        k = Kernel("update_third", 32 * work // PARTS)
        k.smem.update(place=place, mixing=mixing)
        update_operands(k)
        fetched_gates(k)
        k.near.update(got=got2[p], before=got1[p], cur=guesses[p])
        k.near_out.update(state=bf(some, width), guess=bf(width, some))
        if p == PARTS - 1:
            k.far.update(wskv=w_state_kv)
            k.near_out.update(wskv_v=bf(width, 2 * width))
        state, guess, *wskv_v = k.call(lambda env: third_body(env, p), after=[after])
        after = guess
        finals.append(guess)
        state_parts.append(state)

    def running(k):
        for t in tiles:
            k.near.update({"o%d" % t: run_o[t], "ml%d" % t: run_ml[t]})

    def refs_of(env, name):
        return {t: env.refs["%s%d" % (name, t)] for t in tiles}

    def state_body(env):
        copies = [
            env.copy(env.refs["state%d" % p], env.new_state.at[p * some : (p + 1) * some]) for p in range(PARTS)
        ]
        copies += [env.copy(env.refs[n], env.refs[n + "_v"]) for n in ("wk", "wv")]
        for p in range(PARTS):
            for col in range(0, width, tile):
                part = slice(col, col + tile)
                env.guess[p * some : (p + 1) * some, part] = stand(env.refs["guess%d" % p][part, :])
        project(env.guess, env.wskv.at[:, :width], store_scaled(env.skey, None))
        project(env.guess, env.wskv.at[:, width:], store_values(env.svt, head))
        attend(
            env.q, env.skey, env.svt, tiles, lambda t: states, lambda s, t: s,
            refs_of(env, "o"), refs_of(env, "ml"), refs_of(env, "new_o"), refs_of(env, "new_ml"),
        )
        for copy in copies:
            copy.wait()

    k = Kernel("state_keys", 32 * work)
    k.near.update(wskv=wskv_v[0], q=q)
    k.near.update({"guess%d" % p: finals[p] for p in range(PARTS)})
    k.near.update({"state%d" % p: state_parts[p] for p in range(PARTS)})
    k.far.update(wk=w_key, wv=w_value)
    running(k)
    for t in tiles:
        k.near_out.update({"new_o%d" % t: f32(width, tile), "new_ml%d" % t: f32(2 * HEADS, tile)})
    k.near_out.update({n: bf(width, width) for n in ("wk_v", "wv_v")})
    k.far_out.update(new_state=bf(states, width))
    k.scratch.update(skey=vm(states, width), svt=vm(value_rows(width), states), guess=vm(states, width))
    k.copies = PARTS + 2
    k.grant = 8 * 1024 * 1024
    *pairs, wk_v, wv_v, new_state = k.call(state_body)
    run_o, run_ml = pairs[0::2], pairs[1::2]

    k = Kernel("pass_on", 1)
    k.near.update(back2=back2)
    k.near_out.update(out=bf(rows, width))
    k.aliases.update(back2="out")
    (back2,) = k.call(lambda env: None, after=[run_ml[0]])
    last = swap(back2, 1)

    def last_body(env):
        late = [env.copy(env.tok_h, env.tok), env.copy(env.wout_h, env.wout)]
        even = env.place[0] % 2 == 0
        lift = []
        for e in range(mem // BLK):
            entry = env.retrieval[0, e]
            distance = entry // MBLK + 1
            start = pl.multiple_of((entry % MBLK) * BLK, BLK)
            from_last = ((distance == 1) & even) | ((distance == 3) & jnp.logical_not(even))
            from_beside = ((distance == 3) & even) | ((distance == 1) & jnp.logical_not(even))
            for pick, source in (
                (from_last, env.last), (from_beside, env.beside), (distance == 2, env.back2), (distance == 4, env.back4)
            ):

                @pl.when(pick)
                def _(source=source, start=start, e=e):
                    env.mem[e * BLK : (e + 1) * BLK, :] = source[pl.ds(start, BLK), :]

            lift.append(jnp.where(distance > env.place[0], NEG, 0.0))
        project(env.mem, env.wk, store_scaled(env.key, None))
        project(env.mem, env.wv, store_values(env.vt, head))

        def mask(s, t):
            return jnp.concatenate([s[e * BLK : (e + 1) * BLK] + lift[e] for e in range(mem // BLK)], axis=0)

        new_o, new_ml = refs_of(env, "new_o"), refs_of(env, "new_ml")
        attend(env.q, env.key, env.vt, tiles, lambda t: mem, mask, refs_of(env, "o"), refs_of(env, "ml"), new_o, new_ml)
        for t in tiles:
            for h in range(HEADS):
                part = slice(h * head, (h + 1) * head)
                o = new_o[t][part, :] * (1.0 / new_ml[t][HEADS + h : HEADS + h + 1, :])
                env.on[t * tile : (t + 1) * tile, part] = o.T.astype(BF16)
        copies = []
        for copy in late:
            copy.wait()

        def store(col, value):
            part = slice(col, col + value.shape[1])
            env.sum[:, part] = (env.tok[:, part].astype(F32) + value).astype(BF16)
            copies.append(env.copy(env.sum.at[:, part], env.mixed.at[:, part]))

        project(env.on, env.wout, store)
        for copy in copies:
            copy.wait()

    k = Kernel("memory_out", 5 * work)
    k.smem.update(place=place, retrieval=retrieval)
    k.far.update(tok_h=tokens, wout_h=w_out)
    k.scratch.update(tok=vm(rows, width), wout=vm(width, width))
    k.near.update(wk=wk_v, wv=wv_v, q=q, last=last, beside=beside, back2=back2, back4=back4)
    running(k)
    k.scratch.update(
        mem=vm(mem, width), key=vm(mem, width), vt=vm(value_rows(width), mem), on=vm(rows, width), sum=vm(rows, width)
    )
    for t in tiles:
        k.scratch.update({"new_o%d" % t: vm(width, tile, dtype=F32), "new_ml%d" % t: vm(2 * HEADS, tile, dtype=F32)})
    k.far_out.update(mixed=bf(rows, width))
    k.copies = width // 256 + 2
    k.grant = 14 * 1024 * 1024
    (mixed,) = k.call(last_body)
    return mixed, new_state


def solution(mesh):
    return jax.shard_map(
        per_device,
        mesh=mesh,
        in_specs=(P("seq", None), P(), P(), P(), P(), P(), P(), P(), P(), P(), P(), P("seq", None)),
        out_specs=(P("seq", None), P("seq", None)),
        check_vma=False,
    )
```

```python
import math

import jax
import jax.numpy as jnp
from jax import lax
from jax.experimental import pallas as pl
from jax.experimental.pallas import tpu as pltpu
from jax.sharding import PartitionSpec as P

HEADS = 8
BLK = 64
MBLK = 8
WIN = 4
PARTS = 2
ONES = 16
NEG = -1e30
VMEM_LIMIT = 6 * 1024 * 1024

BF16 = jnp.bfloat16
F32 = jnp.float32


def dot(a, b):
    return jnp.dot(a, b, preferred_element_type=F32)


def dot_t(a, b):
    return lax.dot_general(a, b, (((1,), (1,)), ((), ())), preferred_element_type=F32)


class Kernel:
    def __init__(self, name, flops):
        self.name, self.flops = name, flops
        self.smem, self.near, self.far = {}, {}, {}
        self.near_out, self.far_out, self.scratch = {}, {}, {}
        self.aliases = {}
        self.copies = 1
        self.grant = VMEM_LIMIT

    def call(self, body, after=()):
        smem, near, far = list(self.smem), list(self.near), list(self.far)
        near_out, far_out, scratch = list(self.near_out), list(self.far_out), list(self.scratch)
        arrays = [self.smem[n] for n in smem]
        arrays += [pltpu.with_memory_space_constraint(self.near[n], pltpu.VMEM) for n in near]
        arrays += [pltpu.with_memory_space_constraint(self.far[n], pltpu.HBM) for n in far]
        arrays += [pltpu.with_memory_space_constraint(a, pltpu.VMEM) for a in after]
        memory = [pltpu.SMEM] * len(smem) + [pltpu.VMEM] * len(near) + [pltpu.HBM] * len(far) + [pltpu.VMEM] * len(after)
        outs = [pltpu.VMEM(self.near_out[n].shape, self.near_out[n].dtype) for n in near_out]
        outs += [pltpu.HBM(self.far_out[n].shape, self.far_out[n].dtype) for n in far_out]
        out_memory = [pltpu.VMEM] * len(near_out) + [pltpu.HBM] * len(far_out)
        names = smem + near + far
        out_names = near_out + far_out

        def kernel(*refs):
            env = Env()
            env.refs = dict(zip(names, refs))
            env.refs.update(zip(out_names, refs[len(arrays) :]))
            env.refs.update(zip(scratch, refs[len(arrays) + len(outs) :]))
            env.sems, env.started = refs[-1], 0
            body(env)

        return pl.pallas_call(
            kernel,
            out_shape=outs,
            in_specs=[pl.BlockSpec(memory_space=m) for m in memory],
            out_specs=[pl.BlockSpec(memory_space=m) for m in out_memory],
            scratch_shapes=[self.scratch[n] for n in scratch] + [pltpu.SemaphoreType.DMA((self.copies,))],
            input_output_aliases={names.index(a): out_names.index(b) for a, b in self.aliases.items()},
            compiler_params=pltpu.CompilerParams(vmem_limit_bytes=self.grant),
            cost_estimate=pl.CostEstimate(flops=self.flops, bytes_accessed=1 << 10, transcendentals=0),
            name=self.name,
        )(*arrays)


class Env:
    def __getattr__(self, name):
        return self.refs[name]

    def copy(self, src, dst):
        copy = pltpu.make_async_copy(src, dst, self.sems.at[self.started])
        self.started += 1
        copy.start()
        return copy


def project(x_ref, w_ref, store, tile=256):
    for col in range(0, w_ref.shape[1], tile):
        store(col, dot(x_ref[...], w_ref[:, col : col + tile]))


def store_scaled(out_ref, scale):
    def store(col, value):
        if scale is not None:
            value = value * scale
        out_ref[:, col : col + value.shape[1]] = value.astype(BF16)

    return store


def score_scale(head):
    return math.log2(math.e) / math.sqrt(head)


def value_rows(width):
    return width + HEADS * ONES


def store_values(vt_ref, head):
    keys = vt_ref.shape[1]
    pitch = head + ONES

    def store(col, value):
        for part in range(0, value.shape[1], head):
            at = (col + part) // head * pitch
            vt_ref[at : at + head, :] = value[:, part : part + head].T.astype(BF16)
            vt_ref[at + head : at + pitch, :] = jnp.ones((ONES, keys), BF16)

    return store


def in_turn(units, scores, finish):
    ahead = scores(*units[0])
    for number, unit in enumerate(units):
        now = ahead
        if number + 1 < len(units):
            ahead = scores(*units[number + 1])
        finish(*unit, now)


def stand(value):
    return value.T


def update_columns(h_ref, wqs_ref, key_ref, vt_ref, wcg_ref, bias_ref, qs_ref, o_ref, finish_rows, beside=None, ready=None):
    width, some = h_ref.shape
    head = width // HEADS
    pitch = head + ONES
    scale = score_scale(head)
    tall = min(512, width)
    for row in range(0, width, tall):
        part = slice(row, row + tall)
        qs_ref[part, :] = (dot(wqs_ref[part, :], h_ref[...]) * scale).astype(BF16)

    def scores(h):
        part = slice(h * head, (h + 1) * head)
        return dot(key_ref[:, part], qs_ref[part, :])

    def finish(h, s):
        if beside is not None:
            beside(h)
        p = jnp.exp2(s - jnp.max(s, axis=0, keepdims=True)).astype(BF16)
        ol = dot(vt_ref[h * pitch : (h + 1) * pitch, :], p)
        o_ref[h * head : (h + 1) * head, :] = (ol[:head] * (1.0 / ol[head : head + 1])).astype(BF16)

    in_turn([(h,) for h in range(HEADS)], scores, finish)
    if ready is not None:
        ready()
    tall = min(256, width)
    for row in range(0, width, tall):
        part = slice(row, row + tall)
        zc = dot(wcg_ref[part, :], o_ref[...])
        zg = dot(wcg_ref[width + row : width + row + tall, :], o_ref[...])
        lanes = bias_ref.shape[1]
        bias = jnp.concatenate([bias_ref[part, :]] * (some // lanes), axis=1)
        cand = jnp.tanh(zc)
        forget = 0.5 * jnp.tanh(0.5 * (zg + bias)) + 0.5
        finish_rows(row, forget * h_ref[part, :].astype(F32) + (1.0 - forget) * cand)


def attend(q_ref, key_ref, vt_ref, places, limit, mask, old_o, old_ml, new_o, new_ml):
    head = q_ref.shape[1] // HEADS
    pitch = head + ONES
    tile = new_o[places[0]].shape[1]

    def scores(h, t):
        part = slice(h * head, (h + 1) * head)
        return dot_t(key_ref[: limit(t), part], q_ref[t * tile : (t + 1) * tile, part])

    def finish(h, t, s):
        part = slice(h * head, (h + 1) * head)
        top_row, sum_row = slice(h, h + 1), slice(HEADS + h, HEADS + h + 1)
        s = mask(s, t)
        top = jnp.max(s, axis=0, keepdims=True)
        if old_o is not None:
            old = old_ml[t][top_row, :]
            top = jnp.maximum(top, old)
        p = jnp.exp2(s - top).astype(BF16)
        ol = dot(vt_ref[h * pitch : (h + 1) * pitch, : limit(t)], p)
        o, l = ol[:head], ol[head : head + 1]
        if old_o is not None:
            keep = jnp.exp2(old - top)
            o = o + keep * old_o[t][part, :]
            l = l + keep * old_ml[t][sum_row, :]
        new_o[t][part, :] = o
        new_ml[t][top_row, :] = top
        new_ml[t][sum_row, :] = l

    in_turn([(h, t) for h in range(HEADS) for t in places], scores, finish)


def mixed_guess(pick, init_ref, got_ref, cur_ref, prev_ref, prev_pick, mixing, sweep, guess_ref):
    a, b, c = mixing[sweep, 0], mixing[sweep, 1], mixing[sweep, 2]
    rows = guess_ref.shape[0]
    step = min(64, rows)
    for r in range(0, rows, step):
        part = slice(r, r + step)
        init = init_ref[part, :].astype(F32)
        shift = jnp.where(pick, init, got_ref[part, :].astype(F32))
        prev = prev_ref[part, :].astype(F32)
        if prev_pick:
            prev = jnp.where(pick, init, prev)
        guess = a * shift + b * cur_ref[part, :].astype(F32)
        guess_ref[part, :] = (guess + c * prev).astype(BF16)


def bf(*shape):
    return jax.ShapeDtypeStruct(shape, BF16)


def f32(*shape):
    return jax.ShapeDtypeStruct(shape, F32)


def vm(*shape, dtype=BF16):
    return pltpu.VMEM(shape, dtype)


def per_device(
    tokens, init_state, w_query, w_key, w_value, w_out, w_query_state, w_cand_gate, w_state_kv,
    gate_bias, mixing, retrieval,
):
    rows, width = tokens.shape
    states = init_state.shape[0]
    head = width // HEADS
    some = states // PARTS
    tile = min(256, rows)
    tiles = list(range(rows // tile))
    mem = retrieval.shape[1] * BLK
    count = lax.axis_size("seq")
    place = lax.axis_index("seq").astype(jnp.int32).reshape(1)
    work = 2 * rows * width * width

    def step(value, by):
        return lax.ppermute(value, "seq", [(i, i + by) for i in range(count - by)])

    def swap(value, bit):
        return lax.ppermute(value, "seq", [(i, i ^ bit) for i in range(count)])

    def columns_of(ref, p):
        return ref.at[:, p * some : (p + 1) * some]

    def state_rows(env):
        def store(row, value):
            env.state[row : row + value.shape[0], :] = value.astype(BF16)

        return store

    back4 = step(tokens, WIN)

    arguments = dict(
        tok=tokens, wk=w_key, wv=w_value, wqs=w_query_state, init=init_state, wcg=w_cand_gate,
        bias=gate_bias.reshape(1, width),
    )
    lanes = 128

    def first_body(env):
        copies = {}

        def start(*names):
            for name in names:
                copies[name] = env.copy(env.refs[name], env.refs[name + "_s"])

        def wait(*names):
            for name in names:
                copies.pop(name).wait()

        start("tok", "wk")
        start("wv", "wqs", "init")
        wait("tok", "wk")
        start("wcg", "bias")
        project(env.tok_s, env.wk_s, store_scaled(env.key, None))
        wait("wv", "wqs", "init")
        store = store_values(env.vt, head)

        def store_and_turn(col, value):
            store(col, value)
            part = slice(col, col + value.shape[1])
            env.wqs_t[part, :] = stand(env.wqs_s[:, part])
            env.init_t[part, :] = stand(env.init_s[:, part])

        project(env.tok_s, env.wv_s, store_and_turn)
        wait("wcg", "bias")
        for col in range(0, width, lanes):
            part = slice(col, col + lanes)
            env.bias_t[part, :] = jnp.broadcast_to(env.bias_s[:, part], (lanes, lanes)).T

        def turn_gates(h):
            size = 2 * width // HEADS
            part = slice(h * size, (h + 1) * size)
            env.wcg_t[part, :] = stand(env.wcg_s[:, part])

        update_columns(
            columns_of(env.init_t, 0), env.wqs_t, env.key, env.vt, env.wcg_t, env.bias_t, env.qs, env.o,
            state_rows(env), turn_gates,
        )

    k = Kernel("keys_values_update", 2 * work + 4 * work // PARTS)
    k.far.update(arguments)
    k.near_out.update(
        wcg_t=bf(2 * width, width), wqs_t=bf(width, width), init_t=bf(width, states), bias_t=f32(width, lanes), key=bf(rows, width), vt=bf(value_rows(width), rows),
        state=bf(width, some),
    )
    k.scratch.update(
        {n + "_s": vm(*arguments[n].shape, dtype=arguments[n].dtype) for n in arguments},
        qs=vm(width, some), o=vm(width, some),
    )
    k.copies = len(arguments)
    k.grant = 16 * 1024 * 1024
    gates_v, wqs_t, init_t, bias_t, key, vt, state = k.call(first_body)
    got1 = [step(state, 1)]

    def update_operands(k):
        k.near.update(init=init_t, wqs=wqs_t, bias=bias_t, key=key, vt=vt)
        k.near_out.update(state=bf(width, some))
        k.scratch.update(qs=vm(width, some), o=vm(width, some))
        k.copies = 4
        k.grant = 8 * 1024 * 1024

    def fetched_gates(k):
        k.far.update(wcg=wcg_t)
        k.scratch.update(gates=vm(2 * width, width))

    def update(env, h_ref, finish_rows, gates):
        update_columns(
            h_ref, env.wqs, env.key, env.vt, env.gates, env.bias, env.qs, env.o, finish_rows, None, gates.wait if gates else None
        )

    def more_states(env, p):
        out = env.copy(env.gates, env.wcg_t)
        update(env, columns_of(env.init, p), state_rows(env), None)
        out.wait()

    p = 1
    k = Kernel("update_more", work // 32)
    update_operands(k)
    k.near.update(gates=gates_v)
    k.far_out.update(wcg_t=bf(2 * width, width))
    state, wcg_t = k.call(lambda env: more_states(env, p), after=[state])
    got1.append(step(state, 1))
    after = state

    def causal(s, t):
        down = lax.broadcasted_iota(jnp.int32, (tile, tile), 0)
        across = lax.broadcasted_iota(jnp.int32, (tile, tile), 1)
        last = jnp.where(down <= across, s[t * tile :], NEG)
        return last if t == 0 else jnp.concatenate([s[: t * tile], last], axis=0)

    def local(env, t):
        attend(env.q, env.key, env.vt, [t], lambda t: (t + 1) * tile, causal, None, None, {t: env.o}, {t: env.ml})

    def local_outs(k):
        k.near_out.update(o=f32(width, tile), ml=f32(2 * HEADS, tile))

    def query_body(env):
        for copy in [env.copy(env.tok_h, env.tok), env.copy(env.wq_h, env.wq)]:
            copy.wait()
        project(env.tok, env.wq, store_scaled(env.q, score_scale(head)))
        local(env, 0)

    k = Kernel("query_local", work // 32)
    k.near.update(key=key, vt=vt)
    k.far.update(tok_h=tokens, wq_h=w_query)
    k.scratch.update(tok=vm(rows, width), wq=vm(width, width))
    k.copies = 2
    k.near_out.update(q=bf(rows, width))
    local_outs(k)
    q, o, ml = k.call(query_body, after=[after])
    after, run_o, run_ml = ml, [o], [ml]

    guesses, got2 = [], []

    def chosen(env, pick, yes, no, dst):
        number = env.started
        env.started += 1

        @pl.when(pick)
        def _():
            pltpu.make_async_copy(yes, dst, env.sems.at[number]).start()

        @pl.when(jnp.logical_not(pick))
        def _():
            pltpu.make_async_copy(no, dst, env.sems.at[number]).start()

        return pltpu.make_async_copy(no, dst, env.sems.at[number])

    def second_body(env, p):
        copies = []
        if p == PARTS - 1:
            copies = [
                chosen(env, env.place[0] % WIN < WIN // 2, env.tok_h, env.back4, env.pair),
                chosen(env, env.place[0] % 2 == 0, env.tok_h, env.back4, env.core),
            ]
        gates = env.copy(env.wcg, env.gates)
        init = columns_of(env.init, p)
        mixed_guess(env.place[0] == 0, init, env.got, init, init, False, env.mixing, 0, env.guess)
        update(env, env.guess, state_rows(env), gates)
        for copy in copies:
            copy.wait()

    for p in range(PARTS):
        k = Kernel("update_second", work // 32)
        k.smem.update(place=place, mixing=mixing)
        update_operands(k)
        fetched_gates(k)
        k.near.update(got=got1[p])
        k.near_out.update(guess=bf(width, some))
        if p == PARTS - 1:
            k.near.update(back4=back4)
            k.far.update(tok_h=tokens)
            k.near_out.update(pair=bf(rows, width), core=bf(rows, width))
        state, guess, *more = k.call(lambda env: second_body(env, p), after=[after])
        after = state
        guesses.append(guess)
        got2.append(step(state, 1))

    pair, core = more
    k = Kernel("hand_over", 4 * work)
    k.near.update(pair=pair, core=core)
    k.near_out.update(pair_out=bf(rows, width), core_out=bf(rows, width))
    k.aliases.update(pair="pair_out", core="core_out")
    pair, core = k.call(lambda env: None, after=[after])
    after = core
    back2 = swap(pair, WIN // 2)
    beside = swap(core, 1)

    finals, state_parts = [], []

    def third_body(env, p):
        gates = env.copy(env.wcg, env.gates)
        wskv = env.copy(env.wskv, env.wskv_v) if p == PARTS - 1 else None
        mixed_guess(
            env.place[0] == 0, columns_of(env.init, p), env.got, env.cur, env.before, True, env.mixing, 1, env.guess
        )

        def store(row, value):
            env.state[:, row : row + value.shape[0]] = value.T.astype(BF16)

        update(env, env.guess, store, gates)
        if wskv is not None:
            wskv.wait()

    for p in range(PARTS):
        k = Kernel("update_third", 32 * work // PARTS)
        k.smem.update(place=place, mixing=mixing)
        update_operands(k)
        fetched_gates(k)
        k.near.update(got=got2[p], before=got1[p], cur=guesses[p])
        k.near_out.update(state=bf(some, width), guess=bf(width, some))
        if p == PARTS - 1:
            k.far.update(wskv=w_state_kv)
            k.near_out.update(wskv_v=bf(width, 2 * width))
        state, guess, *wskv_v = k.call(lambda env: third_body(env, p), after=[after])
        after = guess
        finals.append(guess)
        state_parts.append(state)

    for t in tiles[1:]:
        k = Kernel("local_more", work)
        k.near.update(q=q, key=key, vt=vt)
        local_outs(k)
        o, ml = k.call(lambda env: local(env, t), after=[after])
        after = ml
        run_o.append(o)
        run_ml.append(ml)

    def running(k):
        for t in tiles:
            k.near.update({"o%d" % t: run_o[t], "ml%d" % t: run_ml[t]})

    def refs_of(env, name):
        return {t: env.refs["%s%d" % (name, t)] for t in tiles}

    def state_body(env):
        copies = [
            env.copy(env.refs["state%d" % p], env.new_state.at[p * some : (p + 1) * some]) for p in range(PARTS)
        ]
        copies += [env.copy(env.refs[n], env.refs[n + "_v"]) for n in ("wk", "wv")]
        for p in range(PARTS):
            for col in range(0, width, tile):
                part = slice(col, col + tile)
                env.guess[p * some : (p + 1) * some, part] = stand(env.refs["guess%d" % p][part, :])
        project(env.guess, env.wskv.at[:, :width], store_scaled(env.skey, None))
        project(env.guess, env.wskv.at[:, width:], store_values(env.svt, head))
        attend(
            env.q, env.skey, env.svt, tiles, lambda t: states, lambda s, t: s,
            refs_of(env, "o"), refs_of(env, "ml"), refs_of(env, "new_o"), refs_of(env, "new_ml"),
        )
        for copy in copies:
            copy.wait()

    k = Kernel("state_keys", 32 * work)
    k.near.update(wskv=wskv_v[0], q=q)
    k.near.update({"guess%d" % p: finals[p] for p in range(PARTS)})
    k.near.update({"state%d" % p: state_parts[p] for p in range(PARTS)})
    k.far.update(wk=w_key, wv=w_value)
    running(k)
    for t in tiles:
        k.near_out.update({"new_o%d" % t: f32(width, tile), "new_ml%d" % t: f32(2 * HEADS, tile)})
    k.near_out.update({n: bf(width, width) for n in ("wk_v", "wv_v")})
    k.far_out.update(new_state=bf(states, width))
    k.scratch.update(skey=vm(states, width), svt=vm(value_rows(width), states), guess=vm(states, width))
    k.copies = PARTS + 2
    k.grant = 8 * 1024 * 1024
    *pairs, wk_v, wv_v, new_state = k.call(state_body)
    run_o, run_ml = pairs[0::2], pairs[1::2]

    k = Kernel("pass_on", 1)
    k.near.update(back2=back2)
    k.near_out.update(out=bf(rows, width))
    k.aliases.update(back2="out")
    (back2,) = k.call(lambda env: None, after=[run_ml[0]])
    last = swap(back2, 1)

    def last_body(env):
        late = [env.copy(env.tok_h, env.tok), env.copy(env.wout_h, env.wout)]
        even = env.place[0] % 2 == 0
        lift = []
        for e in range(mem // BLK):
            entry = env.retrieval[0, e]
            distance = entry // MBLK + 1
            start = pl.multiple_of((entry % MBLK) * BLK, BLK)
            from_last = ((distance == 1) & even) | ((distance == 3) & jnp.logical_not(even))
            from_beside = ((distance == 3) & even) | ((distance == 1) & jnp.logical_not(even))
            for pick, source in (
                (from_last, env.last), (from_beside, env.beside), (distance == 2, env.back2), (distance == 4, env.back4)
            ):

                @pl.when(pick)
                def _(source=source, start=start, e=e):
                    env.mem[e * BLK : (e + 1) * BLK, :] = source[pl.ds(start, BLK), :]

            lift.append(jnp.where(distance > env.place[0], NEG, 0.0))
        project(env.mem, env.wk, store_scaled(env.key, None))
        project(env.mem, env.wv, store_values(env.vt, head))

        def mask(s, t):
            return jnp.concatenate([s[e * BLK : (e + 1) * BLK] + lift[e] for e in range(mem // BLK)], axis=0)

        new_o, new_ml = refs_of(env, "new_o"), refs_of(env, "new_ml")
        attend(env.q, env.key, env.vt, tiles, lambda t: mem, mask, refs_of(env, "o"), refs_of(env, "ml"), new_o, new_ml)
        for t in tiles:
            for h in range(HEADS):
                part = slice(h * head, (h + 1) * head)
                o = new_o[t][part, :] * (1.0 / new_ml[t][HEADS + h : HEADS + h + 1, :])
                env.on[t * tile : (t + 1) * tile, part] = o.T.astype(BF16)
        copies = []
        for copy in late:
            copy.wait()

        def store(col, value):
            part = slice(col, col + value.shape[1])
            env.sum[:, part] = (env.tok[:, part].astype(F32) + value).astype(BF16)
            copies.append(env.copy(env.sum.at[:, part], env.mixed.at[:, part]))

        project(env.on, env.wout, store)
        for copy in copies:
            copy.wait()

    k = Kernel("memory_out", 5 * work)
    k.smem.update(place=place, retrieval=retrieval)
    k.far.update(tok_h=tokens, wout_h=w_out)
    k.scratch.update(tok=vm(rows, width), wout=vm(width, width))
    k.near.update(wk=wk_v, wv=wv_v, q=q, last=last, beside=beside, back2=back2, back4=back4)
    running(k)
    k.scratch.update(
        mem=vm(mem, width), key=vm(mem, width), vt=vm(value_rows(width), mem), on=vm(rows, width), sum=vm(rows, width)
    )
    for t in tiles:
        k.scratch.update({"new_o%d" % t: vm(width, tile, dtype=F32), "new_ml%d" % t: vm(2 * HEADS, tile, dtype=F32)})
    k.far_out.update(mixed=bf(rows, width))
    k.copies = width // 256 + 2
    k.grant = 14 * 1024 * 1024
    (mixed,) = k.call(last_body)
    return mixed, new_state


def solution(mesh):
    return jax.shard_map(
        per_device,
        mesh=mesh,
        in_specs=(P("seq", None), P(), P(), P(), P(), P(), P(), P(), P(), P(), P(), P("seq", None)),
        out_specs=(P("seq", None), P("seq", None)),
        check_vma=False,
    )
```

```python
import math

import jax
import jax.numpy as jnp
from jax import lax
from jax.experimental import pallas as pl
from jax.experimental.pallas import tpu as pltpu
from jax.sharding import PartitionSpec as P

HEADS = 8
BLK = 64
MBLK = 8
WIN = 4
PARTS = 2
ONES = 16
NEG = -1e30
VMEM_LIMIT = 6 * 1024 * 1024

BF16 = jnp.bfloat16
F32 = jnp.float32


def dot(a, b):
    return jnp.dot(a, b, preferred_element_type=F32)


def dot_t(a, b):
    return lax.dot_general(a, b, (((1,), (1,)), ((), ())), preferred_element_type=F32)


class Kernel:
    def __init__(self, name, flops):
        self.name, self.flops = name, flops
        self.smem, self.near, self.far = {}, {}, {}
        self.near_out, self.far_out, self.scratch = {}, {}, {}
        self.aliases = {}
        self.copies = 1
        self.grant = VMEM_LIMIT

    def call(self, body, after=()):
        smem, near, far = list(self.smem), list(self.near), list(self.far)
        near_out, far_out, scratch = list(self.near_out), list(self.far_out), list(self.scratch)
        arrays = [self.smem[n] for n in smem]
        arrays += [pltpu.with_memory_space_constraint(self.near[n], pltpu.VMEM) for n in near]
        arrays += [pltpu.with_memory_space_constraint(self.far[n], pltpu.HBM) for n in far]
        arrays += [pltpu.with_memory_space_constraint(a, pltpu.VMEM) for a in after]
        memory = [pltpu.SMEM] * len(smem) + [pltpu.VMEM] * len(near) + [pltpu.HBM] * len(far) + [pltpu.VMEM] * len(after)
        outs = [pltpu.VMEM(self.near_out[n].shape, self.near_out[n].dtype) for n in near_out]
        outs += [pltpu.HBM(self.far_out[n].shape, self.far_out[n].dtype) for n in far_out]
        out_memory = [pltpu.VMEM] * len(near_out) + [pltpu.HBM] * len(far_out)
        names = smem + near + far
        out_names = near_out + far_out

        def kernel(*refs):
            env = Env()
            env.refs = dict(zip(names, refs))
            env.refs.update(zip(out_names, refs[len(arrays) :]))
            env.refs.update(zip(scratch, refs[len(arrays) + len(outs) :]))
            env.sems, env.started = refs[-1], 0
            body(env)

        return pl.pallas_call(
            kernel,
            out_shape=outs,
            in_specs=[pl.BlockSpec(memory_space=m) for m in memory],
            out_specs=[pl.BlockSpec(memory_space=m) for m in out_memory],
            scratch_shapes=[self.scratch[n] for n in scratch] + [pltpu.SemaphoreType.DMA((self.copies,))],
            input_output_aliases={names.index(a): out_names.index(b) for a, b in self.aliases.items()},
            compiler_params=pltpu.CompilerParams(vmem_limit_bytes=self.grant),
            cost_estimate=pl.CostEstimate(flops=self.flops, bytes_accessed=1 << 10, transcendentals=0),
            name=self.name,
        )(*arrays)


class Env:
    def __getattr__(self, name):
        return self.refs[name]

    def copy(self, src, dst):
        copy = pltpu.make_async_copy(src, dst, self.sems.at[self.started])
        self.started += 1
        copy.start()
        return copy


def project(x_ref, w_ref, store, tile=256):
    for col in range(0, w_ref.shape[1], tile):
        store(col, dot(x_ref[...], w_ref[:, col : col + tile]))


def store_scaled(out_ref, scale):
    def store(col, value):
        if scale is not None:
            value = value * scale
        out_ref[:, col : col + value.shape[1]] = value.astype(BF16)

    return store


def score_scale(head):
    return math.log2(math.e) / math.sqrt(head)


def value_rows(width):
    return width + HEADS * ONES


def store_values(vt_ref, head):
    keys = vt_ref.shape[1]
    pitch = head + ONES

    def store(col, value):
        for part in range(0, value.shape[1], head):
            at = (col + part) // head * pitch
            vt_ref[at : at + head, :] = value[:, part : part + head].T.astype(BF16)
            vt_ref[at + head : at + pitch, :] = jnp.ones((ONES, keys), BF16)

    return store


def in_turn(units, scores, finish):
    ahead = scores(*units[0])
    for number, unit in enumerate(units):
        now = ahead
        if number + 1 < len(units):
            ahead = scores(*units[number + 1])
        finish(*unit, now)


def stand(value):
    return value.T


def update_columns(h_ref, wqs_ref, key_ref, vt_ref, wcg_ref, bias_ref, qs_ref, o_ref, finish_rows, beside=None, ready=None):
    width, some = h_ref.shape
    head = width // HEADS
    pitch = head + ONES
    scale = score_scale(head)
    tall = min(512, width)
    for row in range(0, width, tall):
        part = slice(row, row + tall)
        qs_ref[part, :] = (dot(wqs_ref[part, :], h_ref[...]) * scale).astype(BF16)

    def scores(h):
        part = slice(h * head, (h + 1) * head)
        return dot(key_ref[:, part], qs_ref[part, :])

    def finish(h, s):
        if beside is not None:
            beside(h)
        p = jnp.exp2(s - jnp.max(s, axis=0, keepdims=True)).astype(BF16)
        ol = dot(vt_ref[h * pitch : (h + 1) * pitch, :], p)
        o_ref[h * head : (h + 1) * head, :] = (ol[:head] * (1.0 / ol[head : head + 1])).astype(BF16)

    in_turn([(h,) for h in range(HEADS)], scores, finish)
    if ready is not None:
        ready()
    tall = min(256, width)
    for row in range(0, width, tall):
        part = slice(row, row + tall)
        zc = dot(wcg_ref[part, :], o_ref[...])
        zg = dot(wcg_ref[width + row : width + row + tall, :], o_ref[...])
        lanes = bias_ref.shape[1]
        bias = jnp.concatenate([bias_ref[part, :]] * (some // lanes), axis=1)
        cand = jnp.tanh(zc)
        forget = 0.5 * jnp.tanh(0.5 * (zg + bias)) + 0.5
        finish_rows(row, forget * h_ref[part, :].astype(F32) + (1.0 - forget) * cand)


def attend(q_ref, key_ref, vt_ref, places, limit, mask, old_o, old_ml, new_o, new_ml):
    head = q_ref.shape[1] // HEADS
    pitch = head + ONES
    tile = new_o[places[0]].shape[1]

    def scores(h, t):
        part = slice(h * head, (h + 1) * head)
        return dot_t(key_ref[: limit(t), part], q_ref[t * tile : (t + 1) * tile, part])

    def finish(h, t, s):
        part = slice(h * head, (h + 1) * head)
        top_row, sum_row = slice(h, h + 1), slice(HEADS + h, HEADS + h + 1)
        s = mask(s, t)
        top = jnp.max(s, axis=0, keepdims=True)
        if old_o is not None:
            old = old_ml[t][top_row, :]
            top = jnp.maximum(top, old)
        p = jnp.exp2(s - top).astype(BF16)
        ol = dot(vt_ref[h * pitch : (h + 1) * pitch, : limit(t)], p)
        o, l = ol[:head], ol[head : head + 1]
        if old_o is not None:
            keep = jnp.exp2(old - top)
            o = o + keep * old_o[t][part, :]
            l = l + keep * old_ml[t][sum_row, :]
        new_o[t][part, :] = o
        new_ml[t][top_row, :] = top
        new_ml[t][sum_row, :] = l

    in_turn([(h, t) for h in range(HEADS) for t in places], scores, finish)


def mixed_guess(pick, init_ref, got_ref, cur_ref, prev_ref, prev_pick, mixing, sweep, guess_ref):
    a, b, c = mixing[sweep, 0], mixing[sweep, 1], mixing[sweep, 2]
    rows = guess_ref.shape[0]
    step = min(64, rows)
    for r in range(0, rows, step):
        part = slice(r, r + step)
        init = init_ref[part, :].astype(F32)
        shift = jnp.where(pick, init, got_ref[part, :].astype(F32))
        prev = prev_ref[part, :].astype(F32)
        if prev_pick:
            prev = jnp.where(pick, init, prev)
        guess = a * shift + b * cur_ref[part, :].astype(F32)
        guess_ref[part, :] = (guess + c * prev).astype(BF16)


def bf(*shape):
    return jax.ShapeDtypeStruct(shape, BF16)


def f32(*shape):
    return jax.ShapeDtypeStruct(shape, F32)


def vm(*shape, dtype=BF16):
    return pltpu.VMEM(shape, dtype)


def per_device(
    tokens, init_state, w_query, w_key, w_value, w_out, w_query_state, w_cand_gate, w_state_kv,
    gate_bias, mixing, retrieval,
):
    rows, width = tokens.shape
    states = init_state.shape[0]
    head = width // HEADS
    some = states // PARTS
    tile = min(256, rows)
    tiles = list(range(rows // tile))
    mem = retrieval.shape[1] * BLK
    count = lax.axis_size("seq")
    place = lax.axis_index("seq").astype(jnp.int32).reshape(1)
    work = 2 * rows * width * width

    def step(value, by):
        return lax.ppermute(value, "seq", [(i, i + by) for i in range(count - by)])

    def swap(value, bit):
        return lax.ppermute(value, "seq", [(i, i ^ bit) for i in range(count)])

    def columns_of(ref, p):
        return ref.at[:, p * some : (p + 1) * some]

    def state_rows(env):
        def store(row, value):
            env.state[row : row + value.shape[0], :] = value.astype(BF16)

        return store

    back4 = step(tokens, WIN)

    arguments = dict(
        tok=tokens, wk=w_key, wv=w_value, wqs=w_query_state, init=init_state, wcg=w_cand_gate,
        bias=gate_bias.reshape(1, width),
    )
    lanes = 128

    def first_body(env):
        copies = {}

        def start(*names):
            for name in names:
                copies[name] = env.copy(env.refs[name], env.refs[name + "_s"])

        def wait(*names):
            for name in names:
                copies.pop(name).wait()

        start("tok", "wk")
        start("wv", "wqs", "init")
        wait("tok", "wk")
        start("wcg", "bias")
        project(env.tok_s, env.wk_s, store_scaled(env.key, None))
        wait("wv", "wqs", "init")
        store = store_values(env.vt, head)

        def store_and_turn(col, value):
            store(col, value)
            part = slice(col, col + value.shape[1])
            env.wqs_t[part, :] = stand(env.wqs_s[:, part])
            env.init_t[part, :] = stand(env.init_s[:, part])

        project(env.tok_s, env.wv_s, store_and_turn)
        wait("wcg", "bias")
        for col in range(0, width, lanes):
            part = slice(col, col + lanes)
            env.bias_t[part, :] = jnp.broadcast_to(env.bias_s[:, part], (lanes, lanes)).T

        def turn_gates(h):
            size = 2 * width // HEADS
            part = slice(h * size, (h + 1) * size)
            env.wcg_t[part, :] = stand(env.wcg_s[:, part])

        update_columns(
            columns_of(env.init_t, 0), env.wqs_t, env.key, env.vt, env.wcg_t, env.bias_t, env.qs, env.o,
            state_rows(env), turn_gates,
        )

    k = Kernel("keys_values_update", 2 * work + 4 * work // PARTS)
    k.far.update(arguments)
    k.near_out.update(
        wcg_t=bf(2 * width, width), wqs_t=bf(width, width), init_t=bf(width, states), bias_t=f32(width, lanes), key=bf(rows, width), vt=bf(value_rows(width), rows),
        state=bf(width, some),
    )
    k.scratch.update(
        {n + "_s": vm(*arguments[n].shape, dtype=arguments[n].dtype) for n in arguments},
        qs=vm(width, some), o=vm(width, some),
    )
    k.copies = len(arguments)
    k.grant = 16 * 1024 * 1024
    gates_v, wqs_t, init_t, bias_t, key, vt, state = k.call(first_body)
    got1 = [step(state, 1)]

    def update_operands(k):
        k.near.update(init=init_t, wqs=wqs_t, bias=bias_t, key=key, vt=vt)
        k.near_out.update(state=bf(width, some))
        k.scratch.update(qs=vm(width, some), o=vm(width, some))
        k.copies = 4
        k.grant = 8 * 1024 * 1024

    def fetched_gates(k):
        k.far.update(wcg=wcg_t)
        k.scratch.update(gates=vm(2 * width, width))

    def update(env, h_ref, finish_rows, gates):
        update_columns(
            h_ref, env.wqs, env.key, env.vt, env.gates, env.bias, env.qs, env.o, finish_rows, None, gates.wait if gates else None
        )

    def more_states(env, p):
        out = env.copy(env.gates, env.wcg_t)
        update(env, columns_of(env.init, p), state_rows(env), None)
        out.wait()

    p = 1
    k = Kernel("update_more", work // 32)
    update_operands(k)
    k.near.update(gates=gates_v)
    k.far_out.update(wcg_t=bf(2 * width, width))
    state, wcg_t = k.call(lambda env: more_states(env, p), after=[state])
    got1.append(step(state, 1))
    after = state

    def causal(s, t):
        down = lax.broadcasted_iota(jnp.int32, (tile, tile), 0)
        across = lax.broadcasted_iota(jnp.int32, (tile, tile), 1)
        last = jnp.where(down <= across, s[t * tile :], NEG)
        return last if t == 0 else jnp.concatenate([s[: t * tile], last], axis=0)

    def local(env, t):
        attend(env.q, env.key, env.vt, [t], lambda t: (t + 1) * tile, causal, None, None, {t: env.o}, {t: env.ml})

    def local_outs(k):
        k.near_out.update(o=f32(width, tile), ml=f32(2 * HEADS, tile))

    guesses, got2 = [], []

    def chosen(env, pick, yes, no, dst):
        number = env.started
        env.started += 1

        @pl.when(pick)
        def _():
            pltpu.make_async_copy(yes, dst, env.sems.at[number]).start()

        @pl.when(jnp.logical_not(pick))
        def _():
            pltpu.make_async_copy(no, dst, env.sems.at[number]).start()

        return pltpu.make_async_copy(no, dst, env.sems.at[number])

    def second_body(env, p):
        gates = env.copy(env.wcg, env.gates)
        init = columns_of(env.init, p)
        mixed_guess(env.place[0] == 0, init, env.got, init, init, False, env.mixing, 0, env.guess)
        update(env, env.guess, state_rows(env), gates)
    for p in range(PARTS):
        k = Kernel("update_second", work // 32)
        k.smem.update(place=place, mixing=mixing)
        update_operands(k)
        fetched_gates(k)
        k.near.update(got=got1[p])
        k.near_out.update(guess=bf(width, some))
        state, guess, *more = k.call(lambda env: second_body(env, p), after=[after])
        after = state
        guesses.append(guess)
        got2.append(step(state, 1))


    def payloads(env):
        copies = [
            chosen(env, env.place[0] % WIN < WIN // 2, env.tok_h, env.back4, env.pair),
            chosen(env, env.place[0] % 2 == 0, env.tok_h, env.back4, env.core),
        ]
        for copy in copies:
            copy.wait()

    k = Kernel("hand_over", 4 * work)
    k.smem.update(place=place)
    k.near.update(back4=back4)
    k.far.update(tok_h=tokens)
    k.near_out.update(pair=bf(rows, width), core=bf(rows, width))
    k.copies = 2
    pair, core = k.call(payloads, after=[after])
    after = core
    back2 = swap(pair, WIN // 2)
    beside = swap(core, 1)

    finals, state_parts = [], []

    def third_body(env, p):
        gates = env.copy(env.wcg, env.gates)
        wskv = env.copy(env.wskv, env.wskv_v) if p == PARTS - 1 else None
        mixed_guess(
            env.place[0] == 0, columns_of(env.init, p), env.got, env.cur, env.before, True, env.mixing, 1, env.guess
        )

        def store(row, value):
            env.state[:, row : row + value.shape[0]] = value.T.astype(BF16)

        update(env, env.guess, store, gates)
        if wskv is not None:
            wskv.wait()

    for p in range(PARTS):
        k = Kernel("update_third", 32 * work // PARTS)
        k.smem.update(place=place, mixing=mixing)
        update_operands(k)
        fetched_gates(k)
        k.near.update(got=got2[p], before=got1[p], cur=guesses[p])
        k.near_out.update(state=bf(some, width), guess=bf(width, some))
        if p == PARTS - 1:
            k.far.update(wskv=w_state_kv)
            k.near_out.update(wskv_v=bf(width, 2 * width))
        state, guess, *wskv_v = k.call(lambda env: third_body(env, p), after=[after])
        after = guess
        finals.append(guess)
        state_parts.append(state)

    def query_body(env):
        for copy in [env.copy(env.tok_h, env.tok), env.copy(env.wq_h, env.wq)]:
            copy.wait()
        project(env.tok, env.wq, store_scaled(env.q, score_scale(head)))
        local(env, 0)

    k = Kernel("query_local", work // 32)
    k.near.update(key=key, vt=vt)
    k.far.update(tok_h=tokens, wq_h=w_query)
    k.scratch.update(tok=vm(rows, width), wq=vm(width, width))
    k.copies = 2
    k.near_out.update(q=bf(rows, width))
    local_outs(k)
    q, o, ml = k.call(query_body, after=[after])
    after, run_o, run_ml = ml, [o], [ml]

    for t in tiles[1:]:
        k = Kernel("local_more", work)
        k.near.update(q=q, key=key, vt=vt)
        local_outs(k)
        o, ml = k.call(lambda env: local(env, t), after=[after])
        after = ml
        run_o.append(o)
        run_ml.append(ml)

    def running(k):
        for t in tiles:
            k.near.update({"o%d" % t: run_o[t], "ml%d" % t: run_ml[t]})

    def refs_of(env, name):
        return {t: env.refs["%s%d" % (name, t)] for t in tiles}

    def state_body(env):
        copies = [
            env.copy(env.refs["state%d" % p], env.new_state.at[p * some : (p + 1) * some]) for p in range(PARTS)
        ]
        copies += [env.copy(env.refs[n], env.refs[n + "_v"]) for n in ("wk", "wv")]
        for p in range(PARTS):
            for col in range(0, width, tile):
                part = slice(col, col + tile)
                env.guess[p * some : (p + 1) * some, part] = stand(env.refs["guess%d" % p][part, :])
        project(env.guess, env.wskv.at[:, :width], store_scaled(env.skey, None))
        project(env.guess, env.wskv.at[:, width:], store_values(env.svt, head))
        attend(
            env.q, env.skey, env.svt, tiles, lambda t: states, lambda s, t: s,
            refs_of(env, "o"), refs_of(env, "ml"), refs_of(env, "new_o"), refs_of(env, "new_ml"),
        )
        for copy in copies:
            copy.wait()

    k = Kernel("state_keys", 32 * work)
    k.near.update(wskv=wskv_v[0], q=q)
    k.near.update({"guess%d" % p: finals[p] for p in range(PARTS)})
    k.near.update({"state%d" % p: state_parts[p] for p in range(PARTS)})
    k.far.update(wk=w_key, wv=w_value)
    running(k)
    for t in tiles:
        k.near_out.update({"new_o%d" % t: f32(width, tile), "new_ml%d" % t: f32(2 * HEADS, tile)})
    k.near_out.update({n: bf(width, width) for n in ("wk_v", "wv_v")})
    k.far_out.update(new_state=bf(states, width))
    k.scratch.update(skey=vm(states, width), svt=vm(value_rows(width), states), guess=vm(states, width))
    k.copies = PARTS + 2
    k.grant = 8 * 1024 * 1024
    *pairs, wk_v, wv_v, new_state = k.call(state_body)
    run_o, run_ml = pairs[0::2], pairs[1::2]

    k = Kernel("pass_on", 1)
    k.near.update(back2=back2)
    k.near_out.update(out=bf(rows, width))
    k.aliases.update(back2="out")
    (back2,) = k.call(lambda env: None, after=[run_ml[0]])
    last = swap(back2, 1)

    def last_body(env):
        late = [env.copy(env.tok_h, env.tok), env.copy(env.wout_h, env.wout)]
        even = env.place[0] % 2 == 0
        lift = []
        for e in range(mem // BLK):
            entry = env.retrieval[0, e]
            distance = entry // MBLK + 1
            start = pl.multiple_of((entry % MBLK) * BLK, BLK)
            from_last = ((distance == 1) & even) | ((distance == 3) & jnp.logical_not(even))
            from_beside = ((distance == 3) & even) | ((distance == 1) & jnp.logical_not(even))
            for pick, source in (
                (from_last, env.last), (from_beside, env.beside), (distance == 2, env.back2), (distance == 4, env.back4)
            ):

                @pl.when(pick)
                def _(source=source, start=start, e=e):
                    env.mem[e * BLK : (e + 1) * BLK, :] = source[pl.ds(start, BLK), :]

            lift.append(jnp.where(distance > env.place[0], NEG, 0.0))
        project(env.mem, env.wk, store_scaled(env.key, None))
        project(env.mem, env.wv, store_values(env.vt, head))

        def mask(s, t):
            return jnp.concatenate([s[e * BLK : (e + 1) * BLK] + lift[e] for e in range(mem // BLK)], axis=0)

        new_o, new_ml = refs_of(env, "new_o"), refs_of(env, "new_ml")
        attend(env.q, env.key, env.vt, tiles, lambda t: mem, mask, refs_of(env, "o"), refs_of(env, "ml"), new_o, new_ml)
        for t in tiles:
            for h in range(HEADS):
                part = slice(h * head, (h + 1) * head)
                o = new_o[t][part, :] * (1.0 / new_ml[t][HEADS + h : HEADS + h + 1, :])
                env.on[t * tile : (t + 1) * tile, part] = o.T.astype(BF16)
        copies = []
        for copy in late:
            copy.wait()

        def store(col, value):
            part = slice(col, col + value.shape[1])
            env.sum[:, part] = (env.tok[:, part].astype(F32) + value).astype(BF16)
            copies.append(env.copy(env.sum.at[:, part], env.mixed.at[:, part]))

        project(env.on, env.wout, store)
        for copy in copies:
            copy.wait()

    k = Kernel("memory_out", 5 * work)
    k.smem.update(place=place, retrieval=retrieval)
    k.far.update(tok_h=tokens, wout_h=w_out)
    k.scratch.update(tok=vm(rows, width), wout=vm(width, width))
    k.near.update(wk=wk_v, wv=wv_v, q=q, last=last, beside=beside, back2=back2, back4=back4)
    running(k)
    k.scratch.update(
        mem=vm(mem, width), key=vm(mem, width), vt=vm(value_rows(width), mem), on=vm(rows, width), sum=vm(rows, width)
    )
    for t in tiles:
        k.scratch.update({"new_o%d" % t: vm(width, tile, dtype=F32), "new_ml%d" % t: vm(2 * HEADS, tile, dtype=F32)})
    k.far_out.update(mixed=bf(rows, width))
    k.copies = width // 256 + 2
    k.grant = 14 * 1024 * 1024
    (mixed,) = k.call(last_body)
    return mixed, new_state


def solution(mesh):
    return jax.shard_map(
        per_device,
        mesh=mesh,
        in_specs=(P("seq", None), P(), P(), P(), P(), P(), P(), P(), P(), P(), P(), P("seq", None)),
        out_specs=(P("seq", None), P("seq", None)),
        check_vma=False,
    )
```

```python
import math

import jax
import jax.numpy as jnp
from jax import lax
from jax.experimental import pallas as pl
from jax.experimental.pallas import tpu as pltpu
from jax.sharding import PartitionSpec as P

HEADS = 8
BLK = 64
MBLK = 8
WIN = 4
PARTS = 2
ONES = 16
NEG = -1e30
VMEM_LIMIT = 6 * 1024 * 1024

BF16 = jnp.bfloat16
F32 = jnp.float32


def dot(a, b):
    return jnp.dot(a, b, preferred_element_type=F32)


def dot_t(a, b):
    return lax.dot_general(a, b, (((1,), (1,)), ((), ())), preferred_element_type=F32)


class Kernel:
    def __init__(self, name, flops):
        self.name, self.flops = name, flops
        self.smem, self.near, self.far = {}, {}, {}
        self.near_out, self.far_out, self.scratch = {}, {}, {}
        self.aliases = {}
        self.copies = 1
        self.grant = VMEM_LIMIT

    def call(self, body, after=()):
        smem, near, far = list(self.smem), list(self.near), list(self.far)
        near_out, far_out, scratch = list(self.near_out), list(self.far_out), list(self.scratch)
        arrays = [self.smem[n] for n in smem]
        arrays += [pltpu.with_memory_space_constraint(self.near[n], pltpu.VMEM) for n in near]
        arrays += [pltpu.with_memory_space_constraint(self.far[n], pltpu.HBM) for n in far]
        arrays += [pltpu.with_memory_space_constraint(a, pltpu.VMEM) for a in after]
        memory = [pltpu.SMEM] * len(smem) + [pltpu.VMEM] * len(near) + [pltpu.HBM] * len(far) + [pltpu.VMEM] * len(after)
        outs = [pltpu.VMEM(self.near_out[n].shape, self.near_out[n].dtype) for n in near_out]
        outs += [pltpu.HBM(self.far_out[n].shape, self.far_out[n].dtype) for n in far_out]
        out_memory = [pltpu.VMEM] * len(near_out) + [pltpu.HBM] * len(far_out)
        names = smem + near + far
        out_names = near_out + far_out

        def kernel(*refs):
            env = Env()
            env.refs = dict(zip(names, refs))
            env.refs.update(zip(out_names, refs[len(arrays) :]))
            env.refs.update(zip(scratch, refs[len(arrays) + len(outs) :]))
            env.sems, env.started = refs[-1], 0
            body(env)

        return pl.pallas_call(
            kernel,
            out_shape=outs,
            in_specs=[pl.BlockSpec(memory_space=m) for m in memory],
            out_specs=[pl.BlockSpec(memory_space=m) for m in out_memory],
            scratch_shapes=[self.scratch[n] for n in scratch] + [pltpu.SemaphoreType.DMA((self.copies,))],
            input_output_aliases={names.index(a): out_names.index(b) for a, b in self.aliases.items()},
            compiler_params=pltpu.CompilerParams(vmem_limit_bytes=self.grant),
            cost_estimate=pl.CostEstimate(flops=self.flops, bytes_accessed=1 << 10, transcendentals=0),
            name=self.name,
        )(*arrays)


class Env:
    def __getattr__(self, name):
        return self.refs[name]

    def copy(self, src, dst):
        copy = pltpu.make_async_copy(src, dst, self.sems.at[self.started])
        self.started += 1
        copy.start()
        return copy


def project(x_ref, w_ref, store, tile=256):
    for col in range(0, w_ref.shape[1], tile):
        store(col, dot(x_ref[...], w_ref[:, col : col + tile]))


def store_scaled(out_ref, scale):
    def store(col, value):
        if scale is not None:
            value = value * scale
        out_ref[:, col : col + value.shape[1]] = value.astype(BF16)

    return store


def score_scale(head):
    return math.log2(math.e) / math.sqrt(head)


def value_rows(width):
    return width + HEADS * ONES


def store_values(vt_ref, head):
    keys = vt_ref.shape[1]
    pitch = head + ONES

    def store(col, value):
        for part in range(0, value.shape[1], head):
            at = (col + part) // head * pitch
            vt_ref[at : at + head, :] = value[:, part : part + head].T.astype(BF16)
            vt_ref[at + head : at + pitch, :] = jnp.ones((ONES, keys), BF16)

    return store


def in_turn(units, scores, finish):
    ahead = scores(*units[0])
    before = None
    for number, unit in enumerate(units):
        now = ahead
        if number + 1 < len(units):
            ahead = scores(*units[number + 1])
        later = finish(*unit, now)
        if before is not None:
            before()
        before = later
    before()


def stand(value):
    return value.T


def update_columns(h_ref, wqs_ref, key_ref, vt_ref, wcg_ref, bias_ref, qs_ref, o_ref, finish_rows, beside=None, ready=None):
    width, some = h_ref.shape
    head = width // HEADS
    pitch = head + ONES
    scale = score_scale(head)
    tall = min(512, width)
    for row in range(0, width, tall):
        part = slice(row, row + tall)
        qs_ref[part, :] = (dot(wqs_ref[part, :], h_ref[...]) * scale).astype(BF16)

    def scores(h):
        part = slice(h * head, (h + 1) * head)
        return dot(key_ref[:, part], qs_ref[part, :])

    def finish(h, s):
        if beside is not None:
            beside(h)
        p = jnp.exp2(s - jnp.max(s, axis=0, keepdims=True)).astype(BF16)

        def combine():
            ol = dot(vt_ref[h * pitch : (h + 1) * pitch, :], p)
            o_ref[h * head : (h + 1) * head, :] = (ol[:head] * (1.0 / ol[head : head + 1])).astype(BF16)

        return combine

    in_turn([(h,) for h in range(HEADS)], scores, finish)
    if ready is not None:
        ready()
    tall = min(256, width)
    for row in range(0, width, tall):
        part = slice(row, row + tall)
        zc = dot(wcg_ref[part, :], o_ref[...])
        zg = dot(wcg_ref[width + row : width + row + tall, :], o_ref[...])
        lanes = bias_ref.shape[1]
        bias = jnp.concatenate([bias_ref[part, :]] * (some // lanes), axis=1)
        cand = jnp.tanh(zc)
        forget = 0.5 * jnp.tanh(0.5 * (zg + bias)) + 0.5
        finish_rows(row, forget * h_ref[part, :].astype(F32) + (1.0 - forget) * cand)


def attend(q_ref, key_ref, vt_ref, places, limit, mask, old_o, old_ml, new_o, new_ml):
    head = q_ref.shape[1] // HEADS
    pitch = head + ONES
    tile = new_o[places[0]].shape[1]

    def scores(h, t):
        part = slice(h * head, (h + 1) * head)
        return dot_t(key_ref[: limit(t), part], q_ref[t * tile : (t + 1) * tile, part])

    def finish(h, t, s):
        part = slice(h * head, (h + 1) * head)
        top_row, sum_row = slice(h, h + 1), slice(HEADS + h, HEADS + h + 1)
        s = mask(s, t)
        top = jnp.max(s, axis=0, keepdims=True)
        if old_o is not None:
            old = old_ml[t][top_row, :]
            top = jnp.maximum(top, old)
        p = jnp.exp2(s - top).astype(BF16)

        def combine():
            ol = dot(vt_ref[h * pitch : (h + 1) * pitch, : limit(t)], p)
            o, l = ol[:head], ol[head : head + 1]
            if old_o is not None:
                keep = jnp.exp2(old - top)
                o = o + keep * old_o[t][part, :]
                l = l + keep * old_ml[t][sum_row, :]
            new_o[t][part, :] = o
            new_ml[t][top_row, :] = top
            new_ml[t][sum_row, :] = l

        return combine

    in_turn([(h, t) for h in range(HEADS) for t in places], scores, finish)


def mixed_guess(pick, init_ref, got_ref, cur_ref, prev_ref, prev_pick, mixing, sweep, guess_ref):
    a, b, c = mixing[sweep, 0], mixing[sweep, 1], mixing[sweep, 2]
    rows = guess_ref.shape[0]
    step = min(64, rows)
    for r in range(0, rows, step):
        part = slice(r, r + step)
        init = init_ref[part, :].astype(F32)
        shift = jnp.where(pick, init, got_ref[part, :].astype(F32))
        prev = prev_ref[part, :].astype(F32)
        if prev_pick:
            prev = jnp.where(pick, init, prev)
        guess = a * shift + b * cur_ref[part, :].astype(F32)
        guess_ref[part, :] = (guess + c * prev).astype(BF16)


def bf(*shape):
    return jax.ShapeDtypeStruct(shape, BF16)


def f32(*shape):
    return jax.ShapeDtypeStruct(shape, F32)


def vm(*shape, dtype=BF16):
    return pltpu.VMEM(shape, dtype)


def per_device(
    tokens, init_state, w_query, w_key, w_value, w_out, w_query_state, w_cand_gate, w_state_kv,
    gate_bias, mixing, retrieval,
):
    rows, width = tokens.shape
    states = init_state.shape[0]
    head = width // HEADS
    some = states // PARTS
    tile = min(256, rows)
    tiles = list(range(rows // tile))
    mem = retrieval.shape[1] * BLK
    count = lax.axis_size("seq")
    place = lax.axis_index("seq").astype(jnp.int32).reshape(1)
    work = 2 * rows * width * width

    def step(value, by):
        return lax.ppermute(value, "seq", [(i, i + by) for i in range(count - by)])

    def swap(value, bit):
        return lax.ppermute(value, "seq", [(i, i ^ bit) for i in range(count)])

    def columns_of(ref, p):
        return ref.at[:, p * some : (p + 1) * some]

    def state_rows(env):
        def store(row, value):
            env.state[row : row + value.shape[0], :] = value.astype(BF16)

        return store

    back4 = step(tokens, WIN)

    arguments = dict(
        tok=tokens, wk=w_key, wv=w_value, wqs=w_query_state, init=init_state, wcg=w_cand_gate,
        bias=gate_bias.reshape(1, width),
    )
    lanes = 128

    def first_body(env):
        copies = {}

        def start(*names):
            for name in names:
                copies[name] = env.copy(env.refs[name], env.refs[name + "_s"])

        def wait(*names):
            for name in names:
                copies.pop(name).wait()

        start("tok", "wk")
        start("wv", "wqs", "init")
        wait("tok", "wk")
        start("wcg", "bias")
        project(env.tok_s, env.wk_s, store_scaled(env.key, None))
        wait("wv", "wqs", "init")
        store = store_values(env.vt, head)

        def store_and_turn(col, value):
            store(col, value)
            part = slice(col, col + value.shape[1])
            env.wqs_t[part, :] = stand(env.wqs_s[:, part])
            env.init_t[part, :] = stand(env.init_s[:, part])

        project(env.tok_s, env.wv_s, store_and_turn)
        wait("wcg", "bias")
        for col in range(0, width, lanes):
            part = slice(col, col + lanes)
            env.bias_t[part, :] = jnp.broadcast_to(env.bias_s[:, part], (lanes, lanes)).T

        def turn_gates(h):
            size = 2 * width // HEADS
            part = slice(h * size, (h + 1) * size)
            env.wcg_t[part, :] = stand(env.wcg_s[:, part])

        update_columns(
            columns_of(env.init_t, 0), env.wqs_t, env.key, env.vt, env.wcg_t, env.bias_t, env.qs, env.o,
            state_rows(env), turn_gates,
        )

    k = Kernel("keys_values_update", 2 * work + 4 * work // PARTS)
    k.far.update(arguments)
    k.near_out.update(
        wcg_t=bf(2 * width, width), wqs_t=bf(width, width), init_t=bf(width, states), bias_t=f32(width, lanes), key=bf(rows, width), vt=bf(value_rows(width), rows),
        state=bf(width, some),
    )
    k.scratch.update(
        {n + "_s": vm(*arguments[n].shape, dtype=arguments[n].dtype) for n in arguments},
        qs=vm(width, some), o=vm(width, some),
    )
    k.copies = len(arguments)
    k.grant = 16 * 1024 * 1024
    gates_v, wqs_t, init_t, bias_t, key, vt, state = k.call(first_body)
    got1 = [step(state, 1)]

    def update_operands(k):
        k.near.update(init=init_t, wqs=wqs_t, bias=bias_t, key=key, vt=vt)
        k.near_out.update(state=bf(width, some))
        k.scratch.update(qs=vm(width, some), o=vm(width, some))
        k.copies = 3
        k.grant = 8 * 1024 * 1024

    def fetched_gates(k):
        k.far.update(wcg=wcg_t)
        k.scratch.update(gates=vm(2 * width, width))

    def update(env, h_ref, finish_rows, gates):
        update_columns(
            h_ref, env.wqs, env.key, env.vt, env.gates, env.bias, env.qs, env.o, finish_rows, None, gates.wait if gates else None
        )

    def more_states(env, p):
        out = env.copy(env.gates, env.wcg_t)
        update(env, columns_of(env.init, p), state_rows(env), None)
        out.wait()

    p = 1
    k = Kernel("update_more", work // 32)
    update_operands(k)
    k.near.update(gates=gates_v)
    k.far_out.update(wcg_t=bf(2 * width, width))
    state, wcg_t = k.call(lambda env: more_states(env, p), after=[state])
    got1.append(step(state, 1))
    after = state

    def causal(s, t):
        down = lax.broadcasted_iota(jnp.int32, (tile, tile), 0)
        across = lax.broadcasted_iota(jnp.int32, (tile, tile), 1)
        last = jnp.where(down <= across, s[t * tile :], NEG)
        return last if t == 0 else jnp.concatenate([s[: t * tile], last], axis=0)

    def local(env, t):
        attend(env.q, env.key, env.vt, [t], lambda t: (t + 1) * tile, causal, None, None, {t: env.o}, {t: env.ml})

    def local_outs(k):
        k.near_out.update(o=f32(width, tile), ml=f32(2 * HEADS, tile))

    def query_body(env):
        for copy in [env.copy(env.tok_h, env.tok), env.copy(env.wq_h, env.wq)]:
            copy.wait()
        project(env.tok, env.wq, store_scaled(env.q, score_scale(head)))
        local(env, 0)

    k = Kernel("query_local", work // 32)
    k.near.update(key=key, vt=vt)
    k.far.update(tok_h=tokens, wq_h=w_query)
    k.scratch.update(tok=vm(rows, width), wq=vm(width, width))
    k.copies = 2
    k.near_out.update(q=bf(rows, width))
    local_outs(k)
    q, o, ml = k.call(query_body, after=[after])
    after, run_o, run_ml = ml, [o], [ml]

    guesses, got2 = [], []

    def second_body(env, p):
        gates = env.copy(env.wcg, env.gates)
        init = columns_of(env.init, p)
        mixed_guess(env.place[0] == 0, init, env.got, init, init, False, env.mixing, 0, env.guess)
        update(env, env.guess, state_rows(env), gates)

    for p in range(PARTS):
        k = Kernel("update_second", work // 32)
        k.smem.update(place=place, mixing=mixing)
        update_operands(k)
        fetched_gates(k)
        k.near.update(got=got1[p])
        k.near_out.update(guess=bf(width, some))
        state, guess = k.call(lambda env: second_body(env, p), after=[after])
        after = state
        guesses.append(guess)
        got2.append(step(state, 1))

    def chosen(env, pick, yes, no, dst):
        number = env.started
        env.started += 1

        @pl.when(pick)
        def _():
            pltpu.make_async_copy(yes, dst, env.sems.at[number]).start()

        @pl.when(jnp.logical_not(pick))
        def _():
            pltpu.make_async_copy(no, dst, env.sems.at[number]).start()

        return pltpu.make_async_copy(no, dst, env.sems.at[number])

    def more_body(env, t):
        copies = []
        if t == tiles[-1]:
            copies = [
                chosen(env, env.place[0] % WIN < WIN // 2, env.tok_h, env.back4, env.pair),
                chosen(env, env.place[0] % 2 == 0, env.tok_h, env.back4, env.core),
            ]
        local(env, t)
        for copy in copies:
            copy.wait()

    for t in tiles[1:]:
        k = Kernel("local_more", 4 * work)
        k.smem.update(place=place)
        k.near.update(q=q, key=key, vt=vt)
        local_outs(k)
        if t == tiles[-1]:
            k.near.update(back4=back4)
            k.far.update(tok_h=tokens)
            k.copies = 2
            k.near_out.update(pair=bf(rows, width), core=bf(rows, width))
        o, ml, *more = k.call(lambda env: more_body(env, t), after=[after])
        after = ml
        run_o.append(o)
        run_ml.append(ml)
    pair, core = more
    back2 = swap(pair, WIN // 2)
    beside = swap(core, 1)

    finals, state_parts = [], []

    def third_body(env, p):
        gates = env.copy(env.wcg, env.gates)
        wskv = env.copy(env.wskv, env.wskv_v) if p == PARTS - 1 else None
        mixed_guess(
            env.place[0] == 0, columns_of(env.init, p), env.got, env.cur, env.before, True, env.mixing, 1, env.guess
        )

        def store(row, value):
            env.state[:, row : row + value.shape[0]] = value.T.astype(BF16)

        update(env, env.guess, store, gates)
        if wskv is not None:
            wskv.wait()

    for p in range(PARTS):
        k = Kernel("update_third", 32 * work // PARTS)
        k.smem.update(place=place, mixing=mixing)
        update_operands(k)
        fetched_gates(k)
        k.near.update(got=got2[p], before=got1[p], cur=guesses[p])
        k.near_out.update(state=bf(some, width), guess=bf(width, some))
        if p == PARTS - 1:
            k.far.update(wskv=w_state_kv)
            k.near_out.update(wskv_v=bf(width, 2 * width))
        state, guess, *wskv_v = k.call(lambda env: third_body(env, p), after=[after])
        after = guess
        finals.append(guess)
        state_parts.append(state)

    def running(k):
        for t in tiles:
            k.near.update({"o%d" % t: run_o[t], "ml%d" % t: run_ml[t]})

    def refs_of(env, name):
        return {t: env.refs["%s%d" % (name, t)] for t in tiles}

    def state_body(env):
        copies = [
            env.copy(env.refs["state%d" % p], env.new_state.at[p * some : (p + 1) * some]) for p in range(PARTS)
        ]
        copies += [env.copy(env.refs[n], env.refs[n + "_v"]) for n in ("wk", "wv")]
        for p in range(PARTS):
            for col in range(0, width, tile):
                part = slice(col, col + tile)
                env.guess[p * some : (p + 1) * some, part] = stand(env.refs["guess%d" % p][part, :])
        project(env.guess, env.wskv.at[:, :width], store_scaled(env.skey, None))
        project(env.guess, env.wskv.at[:, width:], store_values(env.svt, head))
        attend(
            env.q, env.skey, env.svt, tiles, lambda t: states, lambda s, t: s,
            refs_of(env, "o"), refs_of(env, "ml"), refs_of(env, "new_o"), refs_of(env, "new_ml"),
        )
        for copy in copies:
            copy.wait()

    k = Kernel("state_keys", 32 * work)
    k.near.update(wskv=wskv_v[0], q=q)
    k.near.update({"guess%d" % p: finals[p] for p in range(PARTS)})
    k.near.update({"state%d" % p: state_parts[p] for p in range(PARTS)})
    k.far.update(wk=w_key, wv=w_value)
    running(k)
    for t in tiles:
        k.near_out.update({"new_o%d" % t: f32(width, tile), "new_ml%d" % t: f32(2 * HEADS, tile)})
    k.near_out.update({n: bf(width, width) for n in ("wk_v", "wv_v")})
    k.far_out.update(new_state=bf(states, width))
    k.scratch.update(skey=vm(states, width), svt=vm(value_rows(width), states), guess=vm(states, width))
    k.copies = PARTS + 2
    k.grant = 8 * 1024 * 1024
    *pairs, wk_v, wv_v, new_state = k.call(state_body)
    run_o, run_ml = pairs[0::2], pairs[1::2]

    k = Kernel("pass_on", 1)
    k.near.update(back2=back2)
    k.near_out.update(out=bf(rows, width))
    k.aliases.update(back2="out")
    (back2,) = k.call(lambda env: None, after=[run_ml[0]])
    last = swap(back2, 1)

    def last_body(env):
        late = [env.copy(env.tok_h, env.tok), env.copy(env.wout_h, env.wout)]
        even = env.place[0] % 2 == 0
        lift = []
        for e in range(mem // BLK):
            entry = env.retrieval[0, e]
            distance = entry // MBLK + 1
            start = pl.multiple_of((entry % MBLK) * BLK, BLK)
            from_last = ((distance == 1) & even) | ((distance == 3) & jnp.logical_not(even))
            from_beside = ((distance == 3) & even) | ((distance == 1) & jnp.logical_not(even))
            for pick, source in (
                (from_last, env.last), (from_beside, env.beside), (distance == 2, env.back2), (distance == 4, env.back4)
            ):

                @pl.when(pick)
                def _(source=source, start=start, e=e):
                    env.mem[e * BLK : (e + 1) * BLK, :] = source[pl.ds(start, BLK), :]

            lift.append(jnp.where(distance > env.place[0], NEG, 0.0))
        project(env.mem, env.wk, store_scaled(env.key, None))
        project(env.mem, env.wv, store_values(env.vt, head))

        def mask(s, t):
            return jnp.concatenate([s[e * BLK : (e + 1) * BLK] + lift[e] for e in range(mem // BLK)], axis=0)

        new_o, new_ml = refs_of(env, "new_o"), refs_of(env, "new_ml")
        attend(env.q, env.key, env.vt, tiles, lambda t: mem, mask, refs_of(env, "o"), refs_of(env, "ml"), new_o, new_ml)
        for t in tiles:
            for h in range(HEADS):
                part = slice(h * head, (h + 1) * head)
                o = new_o[t][part, :] * (1.0 / new_ml[t][HEADS + h : HEADS + h + 1, :])
                env.on[t * tile : (t + 1) * tile, part] = o.T.astype(BF16)
        copies = []
        for copy in late:
            copy.wait()

        def store(col, value):
            part = slice(col, col + value.shape[1])
            env.sum[:, part] = (env.tok[:, part].astype(F32) + value).astype(BF16)
            copies.append(env.copy(env.sum.at[:, part], env.mixed.at[:, part]))

        project(env.on, env.wout, store)
        for copy in copies:
            copy.wait()

    k = Kernel("memory_out", 5 * work)
    k.smem.update(place=place, retrieval=retrieval)
    k.far.update(tok_h=tokens, wout_h=w_out)
    k.scratch.update(tok=vm(rows, width), wout=vm(width, width))
    k.near.update(wk=wk_v, wv=wv_v, q=q, last=last, beside=beside, back2=back2, back4=back4)
    running(k)
    k.scratch.update(
        mem=vm(mem, width), key=vm(mem, width), vt=vm(value_rows(width), mem), on=vm(rows, width), sum=vm(rows, width)
    )
    for t in tiles:
        k.scratch.update({"new_o%d" % t: vm(width, tile, dtype=F32), "new_ml%d" % t: vm(2 * HEADS, tile, dtype=F32)})
    k.far_out.update(mixed=bf(rows, width))
    k.copies = width // 256 + 2
    k.grant = 14 * 1024 * 1024
    (mixed,) = k.call(last_body)
    return mixed, new_state


def solution(mesh):
    return jax.shard_map(
        per_device,
        mesh=mesh,
        in_specs=(P("seq", None), P(), P(), P(), P(), P(), P(), P(), P(), P(), P(), P("seq", None)),
        out_specs=(P("seq", None), P("seq", None)),
        check_vma=False,
    )
```
